32 devices in a mesh: dp: 8 (over z, y), mp: 4 (over x, core).
Axes of the slice: x: 2, y: 2, z: 4, core: 2. Of those that a mesh axis runs over, the one named last changes fastest.
Arguments:
- patches: bfloat16 [64, 196, 1024], P('dp'), may hold values from -6 to 6
- keep_mask: int32 [64, 196], P('dp'), may hold values from 0 to 1, as said below
- w_query: bfloat16 [1024, 1024], P(None, 'mp'), may hold values from -0.1875 to 0.1875
- w_key: bfloat16 [1024, 1024], P(None, 'mp'), may hold values from -0.1875 to 0.1875
- w_value: bfloat16 [1024, 1024], P(None, 'mp'), may hold values from -0.1875 to 0.1875
- w_out: bfloat16 [1024, 1024], P('mp'), may hold values from -0.5 to 0.5
- w_up: bfloat16 [1024, 4096], P(None, 'mp'), may hold values from -0.1875 to 0.1875
- w_down: bfloat16 [4096, 1024], P('mp'), may hold values from -0.09375 to 0.09375
- gain_attn: float32 [1024], replicated, may hold values from 0.5 to 1.5
- gain_mlp: float32 [1024], replicated, may hold values from 0.5 to 1.5
- gain_learn: float32 [1024], replicated, may hold values from 0.5 to 1.5
- w_learn: bfloat16 [1024, 64], P('dp'), may hold values from -0.1875 to 0.1875
- w_select: bfloat16 [64, 8], replicated, may hold values from -0.75 to 0.75
- cotangent: bfloat16 [64, 8, 1024], P('dp'), may hold values from -96 to 96
Outputs:
- learned: bfloat16 [64, 8, 1024], P('dp')
- block_out: bfloat16 [64, 196, 1024], P('dp')
- grad_patches: bfloat16 [64, 196, 1024], P('dp')
- grad_query: float32 [1024, 1024], P(None, 'mp')
- grad_key: float32 [1024, 1024], P(None, 'mp')
- grad_value: float32 [1024, 1024], P(None, 'mp')
- grad_out: float32 [1024, 1024], P('mp')
- grad_up: float32 [1024, 4096], P(None, 'mp')
- grad_down: float32 [4096, 1024], P('mp')
- grad_gain_attn: float32 [1024], replicated
- grad_gain_mlp: float32 [1024], replicated
- grad_gain_learn: float32 [1024], replicated
- grad_learn: float32 [1024, 64], P('dp')
- grad_select: float32 [64, 8], replicated
The draws below stay inside these ranges and needn't reach their ends.
Inputs may be any that keep to these rules, and one draw needn't show every extreme that they name: `keep_mask`: every image keeps at least one patch.
All inputs are finite; a program needn't handle non-finite values.
Results may differ from the reference program's by a relative error of at most 0.025.
Values may be sent and summed in bfloat16 or wider, within the bound.
A program may use at most 192 MiB of HBM per device.

```python
import jax
import jax.numpy as jnp
from jax import lax

D = 1024
HEADS = 16
FF = 4096
PATCHES = 196
NT = 8
LH = 64
IMAGES = 64


def draw_keep_mask(key, part):
    draw_bits = jax.random.randint(jax.random.fold_in(key, 11), (IMAGES, PATCHES), 0, 4)
    chosen = jax.random.randint(jax.random.fold_in(key, 12), (IMAGES, 1), 0, PATCHES)
    position = lax.broadcasted_iota(jnp.int32, (IMAGES, PATCHES), 1)
    return jnp.where((draw_bits > 0) | (position == chosen), 1, 0).astype(jnp.int32)


def shard_levels(key, extent, cuts, low, largest):
    factor_of = 1.0
    for dim, blocks in cuts:
        steps = jax.random.uniform(jax.random.fold_in(jax.random.fold_in(key, 6), dim), (blocks,), jnp.float32, low / len(cuts), largest / len(cuts))
        factor_of = factor_of * jnp.repeat(jnp.exp(steps), extent[dim] // blocks).reshape((-1,) + (1,) * (len(extent) - 1 - dim))
    return factor_of


def normal_values(stream_key, dims, scale, most, cuts=(), held_as=jnp.bfloat16):
    level = shard_levels(stream_key, dims, cuts, -0.22, 0.18) if cuts else 1.0
    entries = jax.random.normal(stream_key, dims, jnp.float32) * scale * level
    return jnp.minimum(jnp.maximum(entries, -most), most).astype(held_as)


def setup_inputs(seed: int = 0) -> dict:
    key_of = jax.random.split(jax.random.key(seed), 15)
    return {
        "patches": normal_values(key_of[0], (IMAGES, PATCHES, D), 1.0, 6.0, ((0, 8),)),
        "keep_mask": draw_keep_mask(jax.random.fold_in(key_of[14], 71), 0),
        "w_query": normal_values(key_of[2], (D, D), D ** -0.5, 0.1875, ((1, 4),)),
        "w_key": normal_values(key_of[3], (D, D), D ** -0.5, 0.1875, ((1, 4),)),
        "w_value": normal_values(key_of[4], (D, D), D ** -0.5, 0.1875, ((1, 4),)),
        "w_out": normal_values(key_of[5], (D, D), (D // 8) ** -0.5, 0.5, ((0, 4),)),
        "w_up": normal_values(key_of[6], (D, FF), D ** -0.5, 0.1875, ((1, 4),)),
        "w_down": normal_values(key_of[7], (FF, D), FF ** -0.5, 0.09375, ((0, 4),)),
        "gain_attn": jnp.clip(1.0 + 0.1 * jax.random.normal(key_of[8], (D,), jnp.float32), 0.5, 1.5),
        "gain_mlp": jnp.clip(1.0 + 0.1 * jax.random.normal(key_of[9], (D,), jnp.float32), 0.5, 1.5),
        "gain_learn": jnp.clip(1.0 + 0.1 * jax.random.normal(key_of[10], (D,), jnp.float32), 0.5, 1.5),
        "w_learn": normal_values(key_of[11], (D, LH), D ** -0.5, 0.1875, ((0, 8),)),
        "w_select": normal_values(key_of[12], (LH, NT), LH ** -0.5, 0.75),
        "cotangent": normal_values(key_of[13], (IMAGES, NT, D), 16.0, 96.0, ((0, 8),)),
    }


@jax.custom_vjp
def low(v):
    return lax.optimization_barrier(v.astype(jnp.bfloat16)).astype(jnp.float32)

@jax.custom_vjp
def low_back(v):
    return v

def low_keep(v):
    return (low(v), None)

def low_pass(kept, grad):
    return (grad,)

def back_keep(v):
    return (v, None)

def back_low(kept, grad):
    return (low(grad),)
low.defvjp(low_keep, low_pass)
low_back.defvjp(back_keep, back_low)

def matmul(left, right):
    return jnp.dot(left, right, precision=lax.Precision.HIGHEST)

def layer_norm(inputs, gain):
    row_mean = lax.optimization_barrier(jnp.mean(inputs, axis=-1, keepdims=True))
    centered = inputs - row_mean
    variance = lax.optimization_barrier(jnp.mean(centered * centered, axis=-1, keepdims=True))
    return centered * lax.rsqrt(variance + 1e-06) * gain

def gelu_exact(inputs):
    return jax.nn.gelu(inputs, approximate=False)

def forward(patches, visible, w_query, w_key, w_value, w_out, w_up, w_down, gain_attn, gain_mlp, gain_learn, w_learn, w_select):
    images = patches.shape[0]
    head_size = D // HEADS
    score_scale = 1.0 / head_size ** 0.5
    row_data = patches.reshape(images * PATCHES, D)
    attn_input = low(layer_norm(row_data, gain_attn))
    head_shape = (images, PATCHES, HEADS, head_size)
    query_heads = low(low_back(matmul(attn_input, w_query))).reshape(head_shape)
    key_heads = low(low_back(matmul(attn_input, w_key))).reshape(head_shape)
    value_heads = low(low_back(matmul(attn_input, w_value))).reshape(head_shape)
    raw_scores = jnp.einsum('bqhe,bkhe->bhqk', query_heads, key_heads, precision=lax.Precision.HIGHEST) * score_scale
    raw_scores = low_back(raw_scores)
    raw_scores = jnp.where(visible[:, None, None, :], raw_scores, -1e+30)
    top_score = lax.optimization_barrier(jnp.max(raw_scores, axis=-1, keepdims=True))
    exponent = jnp.exp(raw_scores - top_score)
    probs = low(exponent / lax.optimization_barrier(jnp.sum(exponent, axis=-1, keepdims=True)))
    mixed_heads = jnp.einsum('bhqk,bkhe->bqhe', probs, value_heads, precision=lax.Precision.HIGHEST)
    mixed_heads = low(low_back(mixed_heads)).reshape(images * PATCHES, D)
    attention = low_back(matmul(mixed_heads, w_out))
    hidden_one = row_data + attention
    mlp_input = low(layer_norm(hidden_one, gain_mlp))
    hidden_pre = low_back(matmul(mlp_input, w_up))
    activated = low(gelu_exact(hidden_pre))
    mlp_out = low_back(matmul(activated, w_down))
    block_rows = low(hidden_one + mlp_out)
    learn_input = low(layer_norm(block_rows, gain_learn))
    learn_pre = low_back(matmul(learn_input, w_learn))
    learn_act = low(gelu_exact(learn_pre))
    logits = low_back(matmul(learn_act, w_select)).reshape(images, PATCHES, NT)
    logits = jnp.where(visible[:, :, None], logits, -1e+30)
    top_logit = lax.optimization_barrier(jnp.max(logits, axis=1, keepdims=True))
    exp_logit = jnp.exp(logits - top_logit)
    token_maps = low(exp_logit / lax.optimization_barrier(jnp.sum(exp_logit, axis=1, keepdims=True)))
    block_three = block_rows.reshape(images, PATCHES, D)
    learned = jnp.einsum('bpn,bpd->bnd', token_maps, block_three, precision=lax.Precision.HIGHEST)
    return (learned, block_three)

def reference(patches, keep_mask, w_query, w_key, w_value, w_out, w_up, w_down, gain_attn, gain_mlp, gain_learn, w_learn, w_select, cotangent):
    visible = keep_mask > 0
    operands = [item.astype(jnp.float32) for item in (patches, w_query, w_key, w_value, w_out, w_up, w_down, gain_attn, gain_mlp, gain_learn, w_learn, w_select)]

    def apply_layer(*inputs):
        return forward(inputs[0], visible, *inputs[1:])
    outputs, pullback = jax.vjp(apply_layer, *operands)
    learned, block_three = outputs
    gradients = pullback((cotangent.astype(jnp.float32), jnp.zeros_like(block_three)))
    return (learned.astype(jnp.bfloat16), block_three.astype(jnp.bfloat16), gradients[0].astype(jnp.bfloat16), gradients[1].astype(jnp.float32), gradients[2].astype(jnp.float32), gradients[3].astype(jnp.float32), gradients[4].astype(jnp.float32), gradients[5].astype(jnp.float32), gradients[6].astype(jnp.float32), gradients[7].astype(jnp.float32), gradients[8].astype(jnp.float32), gradients[9].astype(jnp.float32), gradients[10].astype(jnp.float32), gradients[11].astype(jnp.float32))
```

```python
import math

import jax
import jax.numpy as jnp
from jax import lax
from jax.experimental import pallas as pl
from jax.experimental.pallas import tpu as pltpu
from jax.sharding import PartitionSpec as P

D = 1024
HEADS = 16


def product(left, right):
    return jnp.dot(left, right, preferred_element_type=jnp.float32)


def contract_rows(left, right):
    return lax.dot_general(
        left, right, (((0,), (0,)), ((), ())), preferred_element_type=jnp.float32
    )


def contract_cols(left, right):
    return lax.dot_general(
        left, right, (((1,), (1,)), ((), ())), preferred_element_type=jnp.float32
    )


def normalize(inputs):
    row_mean = jnp.mean(inputs, axis=-1, keepdims=True)
    centered = inputs - row_mean
    inverse = lax.rsqrt(jnp.mean(centered * centered, axis=-1, keepdims=True) + 1e-06)
    return (centered * inverse, inverse)


def norm_back(grad_norm, normed, inverse, gain):
    scaled_grad = grad_norm * gain
    grad_input = inverse * (
        scaled_grad
        - jnp.mean(scaled_grad, axis=-1, keepdims=True)
        - normed * jnp.mean(scaled_grad * normed, axis=-1, keepdims=True)
    )
    return (grad_input, jnp.sum(grad_norm * normed, axis=0))


def gelu_exact(inputs):
    return jax.nn.gelu(inputs, approximate=False)


def gelu_back(hidden_pre, grad_act):
    _, pullback = jax.vjp(gelu_exact, hidden_pre)
    return pullback(grad_act)[0]


def local(
    patches,
    keep_mask,
    w_query,
    w_key,
    w_value,
    w_out,
    w_up,
    w_down,
    gain_attn,
    gain_mlp,
    gain_learn,
    w_learn,
    w_select,
    cotangent,
):
    images, patch_count, feature_count = patches.shape
    row_count = images * patch_count
    head_size = D // HEADS
    heads_here = w_query.shape[1] // head_size
    score_scale = 1.0 / math.sqrt(head_size)
    visible = keep_mask > 0
    head_shape = (images, patch_count, heads_here, head_size)
    residual_rows = patches.reshape(row_count, feature_count).astype(jnp.float32)
    normed_one, inverse_one = normalize(residual_rows)
    attn_input = (normed_one * gain_attn).astype(jnp.bfloat16)
    query_flat = product(attn_input, w_query).astype(jnp.bfloat16)
    key_flat = product(attn_input, w_key).astype(jnp.bfloat16)
    value_flat = product(attn_input, w_value).astype(jnp.bfloat16)
    query_heads = query_flat.reshape(head_shape)
    key_heads = key_flat.reshape(head_shape)
    value_heads = value_flat.reshape(head_shape)

    def masked_scores():
        raw_scores = (
            jnp.einsum(
                "bqhe,bkhe->bhqk", query_heads, key_heads, preferred_element_type=jnp.float32
            )
            * score_scale
        )
        return jnp.where(visible[:, None, None, :], raw_scores, -1e30)

    scores = masked_scores()
    top_score = jnp.max(scores, axis=-1, keepdims=True)
    exponent = jnp.exp(scores - top_score)
    denominator = jnp.sum(exponent, axis=-1, keepdims=True)
    logsum = top_score + jnp.log(denominator)
    probs_low = (exponent / denominator).astype(jnp.bfloat16)
    mixed_heads = jnp.einsum(
        "bhqk,bkhe->bqhe", probs_low, value_heads, preferred_element_type=jnp.float32
    )
    mixed_heads = mixed_heads.astype(jnp.bfloat16).reshape(row_count, heads_here * head_size)
    attn_term = product(mixed_heads, w_out)
    hidden_one = residual_rows + lax.psum(attn_term.astype(jnp.bfloat16), "mp").astype(jnp.float32)
    normed_two, inverse_two = normalize(hidden_one)
    mlp_input = (normed_two * gain_mlp).astype(jnp.bfloat16)
    hidden_pre = product(mlp_input, w_up)
    activated = gelu_exact(hidden_pre).astype(jnp.bfloat16)
    mlp_out = lax.psum(product(activated, w_down).astype(jnp.bfloat16), "mp").astype(jnp.float32)
    block_rows = (hidden_one + mlp_out).astype(jnp.bfloat16)
    normed_learn, inverse_learn = normalize(block_rows.astype(jnp.float32))
    learn_input = (normed_learn * gain_learn).astype(jnp.bfloat16)
    learn_full = lax.all_gather(w_learn, "dp", axis=0, tiled=True)
    learn_pre = product(learn_input, learn_full)
    learn_act = gelu_exact(learn_pre).astype(jnp.bfloat16)
    logits = product(learn_act, w_select).reshape(images, patch_count, -1)
    logits = jnp.where(visible[:, :, None], logits, -1e30)
    top_logit = jnp.max(logits, axis=1, keepdims=True)
    exp_logit = jnp.exp(logits - top_logit)
    token_maps = exp_logit / jnp.sum(exp_logit, axis=1, keepdims=True)
    maps_low = token_maps.astype(jnp.bfloat16)
    block_three = block_rows.reshape(images, patch_count, feature_count)
    learned = jnp.einsum(
        "bpn,bpd->bnd", maps_low, block_three, preferred_element_type=jnp.float32
    ).astype(jnp.bfloat16)
    grad_maps = jnp.einsum(
        "bnd,bpd->bpn", cotangent, block_three, preferred_element_type=jnp.float32
    )
    grad_block = jnp.einsum(
        "bpn,bnd->bpd", maps_low, cotangent, preferred_element_type=jnp.float32
    ).reshape(row_count, feature_count)
    grad_logits = token_maps * (grad_maps - jnp.sum(token_maps * grad_maps, axis=1, keepdims=True))
    grad_logits = grad_logits.reshape(row_count, -1).astype(jnp.bfloat16)
    grad_select = contract_rows(learn_act, grad_logits)
    grad_learn_act = contract_cols(grad_logits, w_select)
    grad_learn_pre = gelu_back(learn_pre, grad_learn_act).astype(jnp.bfloat16)
    grad_learn = contract_rows(learn_input, grad_learn_pre)
    grad_learn_input = contract_cols(grad_learn_pre, learn_full)
    grad_from_learn, grad_gain_learn = norm_back(
        grad_learn_input, normed_learn, inverse_learn, gain_learn
    )
    grad_hidden = grad_block + grad_from_learn
    grad_hidden_low = grad_hidden.astype(jnp.bfloat16)
    grad_down = contract_rows(activated, grad_hidden_low)
    grad_act = contract_cols(grad_hidden_low, w_down)
    grad_pre = gelu_back(hidden_pre, grad_act).astype(jnp.bfloat16)
    grad_up = contract_rows(mlp_input, grad_pre)
    mlp_back_term = contract_cols(grad_pre, w_up)
    grad_mlp_input = lax.psum(mlp_back_term.astype(jnp.bfloat16), "mp").astype(jnp.float32)
    grad_from_two, grad_gain_mlp = norm_back(grad_mlp_input, normed_two, inverse_two, gain_mlp)
    grad_hidden = grad_hidden + grad_from_two
    grad_attn_low = grad_hidden.astype(jnp.bfloat16)
    grad_out = contract_rows(mixed_heads, grad_attn_low)
    grad_mixed = contract_cols(grad_attn_low, w_out).astype(jnp.bfloat16).reshape(head_shape)
    probs_again = jnp.exp(masked_scores() - logsum)
    probs_again_low = probs_again.astype(jnp.bfloat16)
    grad_probs = jnp.einsum(
        "bqhe,bkhe->bhqk", grad_mixed, value_heads, preferred_element_type=jnp.float32
    )
    grad_value_heads = jnp.einsum(
        "bhqk,bqhe->bkhe", probs_again_low, grad_mixed, preferred_element_type=jnp.float32
    ).astype(jnp.bfloat16)
    grad_scores = probs_again * (
        grad_probs - jnp.sum(probs_again * grad_probs, axis=-1, keepdims=True)
    )
    grad_scores = grad_scores.astype(jnp.bfloat16)
    grad_query_heads = (
        jnp.einsum("bhqk,bkhe->bqhe", grad_scores, key_heads, preferred_element_type=jnp.float32)
        * score_scale
    ).astype(jnp.bfloat16)
    grad_key_heads = (
        jnp.einsum("bhqk,bqhe->bkhe", grad_scores, query_heads, preferred_element_type=jnp.float32)
        * score_scale
    ).astype(jnp.bfloat16)
    grad_query_flat = grad_query_heads.reshape(row_count, -1)
    grad_key_flat = grad_key_heads.reshape(row_count, -1)
    grad_value_flat = grad_value_heads.reshape(row_count, -1)
    grad_query = contract_rows(attn_input, grad_query_flat)
    grad_key = contract_rows(attn_input, grad_key_flat)
    grad_value = contract_rows(attn_input, grad_value_flat)
    attn_terms = (
        contract_cols(grad_query_flat, w_query)
        + contract_cols(grad_key_flat, w_key)
        + contract_cols(grad_value_flat, w_value)
    )
    grad_attn_input = lax.psum(attn_terms.astype(jnp.bfloat16), "mp").astype(jnp.float32)
    grad_from_one, grad_gain_attn = norm_back(grad_attn_input, normed_one, inverse_one, gain_attn)
    grad_patches = (
        (grad_hidden + grad_from_one)
        .astype(jnp.bfloat16)
        .reshape(images, patch_count, feature_count)
    )
    (
        grad_query,
        grad_key,
        grad_value,
        grad_out,
        grad_gain_attn,
        grad_up,
        grad_down,
        grad_gain_mlp,
        grad_gain_learn,
        grad_select,
        grad_learn,
    ) = (
        lax.psum(grad_query.astype(jnp.bfloat16), "dp").astype(jnp.float32),
        lax.psum(grad_key.astype(jnp.bfloat16), "dp").astype(jnp.float32),
        lax.psum(grad_value.astype(jnp.bfloat16), "dp").astype(jnp.float32),
        lax.psum(grad_out.astype(jnp.bfloat16), "dp").astype(jnp.float32),
        lax.psum(grad_gain_attn.astype(jnp.bfloat16), "dp").astype(jnp.float32),
        lax.psum(grad_up.astype(jnp.bfloat16), "dp").astype(jnp.float32),
        lax.psum(grad_down.astype(jnp.bfloat16), "dp").astype(jnp.float32),
        lax.psum(grad_gain_mlp.astype(jnp.bfloat16), "dp").astype(jnp.float32),
        lax.psum(grad_gain_learn.astype(jnp.bfloat16), "dp").astype(jnp.float32),
        lax.psum(grad_select.astype(jnp.bfloat16), "dp").astype(jnp.float32),
        lax.psum(grad_learn.astype(jnp.bfloat16), "dp").astype(jnp.float32),
    )
    learn_rows = w_learn.shape[0]
    grad_learn = lax.dynamic_slice_in_dim(
        grad_learn, lax.axis_index("dp") * learn_rows, learn_rows, 0
    )
    return (
        learned,
        block_three,
        grad_patches,
        grad_query,
        grad_key,
        grad_value,
        grad_out,
        grad_up,
        grad_down,
        grad_gain_attn,
        grad_gain_mlp,
        grad_gain_learn,
        grad_learn,
        grad_select,
    )


MESH = pl.DeviceIdType.MESH
PAD = 208
CH = 16
TILE = 256
f32 = jnp.float32
bf16 = jnp.bfloat16


def nn(a, b):
    return jnp.dot(a, b, preferred_element_type=f32)


def nt(a, b):
    return lax.dot_general(a, b, (((1,), (1,)), ((), ())), preferred_element_type=f32)


def tn(a, b):
    return lax.dot_general(a, b, (((0,), (0,)), ((), ())), preferred_element_type=f32)


def gauss(z):
    bell = jnp.exp(-0.5 * (z * z))
    t = 1.0 / (1.0 + 0.23164189 * jnp.abs(z))
    poly = t * (
        0.127414796 + t * (-0.142248368 + t * (0.7107068705 + t * (-0.7265760135 + t * 0.5307027145)))
    )
    tail = poly * bell
    return jnp.where(z >= 0, 1.0 - tail, tail), 0.3989422804014327 * bell


def stats(v):
    mean = jnp.sum(v, axis=-1, keepdims=True) * (1.0 / v.shape[-1])
    c = v - mean
    s = lax.rsqrt(jnp.sum(c * c, axis=-1, keepdims=True) * (1.0 / v.shape[-1]) + 1e-06)
    return c * s, s


def back(e, u, s):
    width = 1.0 / e.shape[-1]
    return s * (
        e
        - jnp.sum(e, axis=-1, keepdims=True) * width
        - u * (jnp.sum(e * u, axis=-1, keepdims=True) * width)
    )


def fold(v):
    total = v[0:8]
    for r in range(8, v.shape[0], 8):
        total = total + v[r : r + 8]
    return total


def chunks():
    return range(0, PAD, CH)


def fused(
    patches, bias_hbm, wq_hbm, wk_hbm, wv_hbm, wo_hbm, wup_hbm, wdn_hbm, g1_ref, g2_ref, g3_ref,
    wl_hbm, wsel_ref, ct_ref,
    learned_ref, y_hbm, gp_hbm, gup_hbm, gdn_hbm, gout_hbm, gqkv_hbm, dg_ref, gl_ref, gsel_ref,
    xraw, bias, wqkv, wo, wup, wdn, wl,
    xs, qkv, os, h1s, a2s, rs, gs, dhs, d1s,
    pbuf, rcore, tbuf, rx, sumb, gst,
    sx, sw, sy, sg, slearn_s, slearn_r, s_core, r_core, s_x, r_x, s_ag, r_ag,
):
    images = patches.shape[0]
    count = patches.shape[1]
    width = patches.shape[2]
    half = width // 2
    dp = lax.axis_index("dp")
    mp = lax.axis_index("mp")
    core = lax.rem(mp, 2)
    mate = (dp, mp + 1 - 2 * core)
    across = (dp, lax.rem(mp + 2, 4))
    dps = lax.axis_size("dp")
    lrows = wl_hbm.shape[0]

    barrier = pltpu.get_barrier_semaphore()
    for device in (mate, across):
        pl.semaphore_signal(barrier, inc=1, device_id=device, device_id_type=MESH)
    for k in range(1, dps):
        pl.semaphore_signal(barrier, inc=1, device_id=(lax.rem(dp + k, dps), mp), device_id_type=MESH)

    loads = [
        pltpu.make_async_copy(wq_hbm, wqkv.at[:, pl.ds(0, 256)], sw.at[0]),
        pltpu.make_async_copy(wk_hbm, wqkv.at[:, pl.ds(256, 256)], sw.at[1]),
        pltpu.make_async_copy(wv_hbm, wqkv.at[:, pl.ds(512, 256)], sw.at[2]),
        pltpu.make_async_copy(wo_hbm, wo, sw.at[3]),
        pltpu.make_async_copy(wup_hbm, wup, sw.at[4]),
        pltpu.make_async_copy(wdn_hbm, wdn, sw.at[5]),
        pltpu.make_async_copy(wl_hbm, wl.at[dp], sw.at[6]),
        pltpu.make_async_copy(bias_hbm, bias, sw.at[7]),
    ]

    def load_x(i, slot):
        return pltpu.make_async_copy(patches.at[i], xraw.at[slot], sx.at[slot])

    load_x(0, 0).start()
    for k in (0, 1, 2, 7, 3):
        loads[k].start()
    load_x(1, 1).start()
    for k in (6, 4, 5):
        loads[k].start()

    xs[...] = jnp.zeros_like(xs)

    pl.semaphore_wait(barrier, dps + 1)

    def learn_copy(k):
        return pltpu.make_async_remote_copy(
            src_ref=wl.at[dp], dst_ref=wl.at[dp],
            send_sem=slearn_s.at[k - 1], recv_sem=slearn_r.at[k - 1],
            device_id=(lax.rem(dp + k, dps), mp), device_id_type=MESH,
        )

    loads[6].wait()
    for k in range(1, dps):
        learn_copy(k).start()

    g1 = g1_ref[...]
    g2 = g2_ref[...]
    g3 = g3_ref[...]
    lane_head = lax.broadcasted_iota(jnp.int32, (1, 256), 1) // 64

    def only(v, h):
        return jnp.where(lane_head == h, v, jnp.zeros_like(v))

    def rows_of(i):
        return pl.ds(pl.multiple_of(i * PAD, 16), PAD)

    def chunk_of(i, r):
        return pl.ds(pl.multiple_of(i * PAD + r, 16), CH)

    def copy_core(i):
        return pltpu.make_async_remote_copy(
            src_ref=pbuf.at[1 - core, rows_of(i)], dst_ref=rcore.at[rows_of(i)],
            send_sem=s_core.at[i], recv_sem=r_core.at[i], device_id=mate, device_id_type=MESH,
        )

    def copy_x(i, par):
        return pltpu.make_async_remote_copy(
            src_ref=tbuf.at[rows_of(i)], dst_ref=rx.at[par, rows_of(i)],
            send_sem=s_x.at[i], recv_sem=r_x.at[par, i], device_id=across, device_id_type=MESH,
        )

    def copy_ag(i):
        return pltpu.make_async_remote_copy(
            src_ref=sumb.at[core, rows_of(i)], dst_ref=sumb.at[core, rows_of(i)],
            send_sem=s_ag.at[i], recv_sem=r_ag.at[i], device_id=mate, device_id_type=MESH,
        )

    def hop_two(i, par):
        copy_core(i).wait()
        rows = rows_of(i)
        tbuf[rows] = (pbuf[core, rows].astype(f32) + rcore[rows].astype(f32)).astype(bf16)
        copy_x(i, par).start()

    def hop_three(i, par):
        copy_x(i, par).wait()
        rows = rows_of(i)
        sumb[core, rows] = (tbuf[rows].astype(f32) + rx[par, rows].astype(f32)).astype(bf16)
        copy_ag(i).start()

    def arrived(i):
        copy_ag(i).wait()

    def summed(i, r):
        where = chunk_of(i, r)
        return jnp.concatenate([sumb[0, where].astype(f32), sumb[1, where].astype(f32)], axis=1)

    def store_p(i, t, value):
        pbuf[t // 2, rows_of(i), (t % 2) * TILE : (t % 2 + 1) * TILE] = value.astype(bf16)

    def stage(body, par, first=False):
        def step(i, carry):
            if not first:
                @pl.when(i + 1 < images)
                def _():
                    hop_three(i + 1, 1 - par)
                arrived(i)
            body(i)
            copy_core(i).start()

            @pl.when(i > 0)
            def _():
                hop_two(i - 1, par)
            return carry

        if not first:
            hop_three(0, 1 - par)
        lax.fori_loop(0, images, step, 0)
        hop_two(images - 1, par)

    for k in (0, 1, 2, 3, 7):
        loads[k].wait()

    def attention(i):
        slot = lax.rem(i, 2)
        load_x(i, slot).wait()
        start = pl.multiple_of(i * PAD, 16)
        xs[pl.ds(start, count), :] = xraw[slot]

        @pl.when(i + 2 < images)
        def _():
            load_x(i + 2, slot).start()

        for r in chunks():
            u, _ = stats(xs[chunk_of(i, r), :].astype(f32))
            a2s[chunk_of(i, r), :] = (u * g1).astype(bf16)
        rows = rows_of(i)
        a1 = a2s[rows, :]
        qkv[rows, 0:256] = (nn(a1, wqkv[:, 0:256]) * 0.125).astype(bf16)
        qkv[rows, 256:512] = nn(a1, wqkv[:, 256:512]).astype(bf16)
        qkv[rows, 512:768] = nn(a1, wqkv[:, 512:768]).astype(bf16)
        q = qkv[rows, 0:256]
        k = qkv[rows, 256:512]
        v = qkv[rows, 512:768]
        row_bias = bias[i]
        o = jnp.zeros((PAD, 256), f32)
        for h in range(4):
            scores = nt(only(q, h), k) + row_bias
            e = jnp.exp(scores - jnp.max(scores, axis=1, keepdims=True))
            p = (e * (1.0 / jnp.sum(e, axis=1, keepdims=True))).astype(bf16)
            o = o + nn(p, only(v, h))
        ob = o.astype(bf16)
        os[rows, :] = ob
        for t in range(4):
            store_p(i, t, nn(ob, wo[:, t * TILE : (t + 1) * TILE]))

    stage(attention, 0, first=True)

    loads[4].wait()
    loads[5].wait()

    def mlp(i):
        for r in chunks():
            h1 = xs[chunk_of(i, r), :].astype(f32) + summed(i, r)
            h1s[chunk_of(i, r), :] = h1
            u, _ = stats(h1)
            a2s[chunk_of(i, r), :] = (u * g2).astype(bf16)
        rows = rows_of(i)
        a2 = a2s[rows, :]
        for t in range(4):
            cols = slice(t * TILE, (t + 1) * TILE)
            z = nn(a2, wup[:, cols])
            cdf, pdf = gauss(z)
            rs[rows, cols] = (z * cdf).astype(bf16)
            gs[rows, cols] = (cdf + z * pdf).astype(bf16)
        act = rs[rows, :]
        for t in range(4):
            store_p(i, t, nn(act, wdn[:, t * TILE : (t + 1) * TILE]))

    stage(mlp, 1)

    for k in range(1, dps):
        learn_copy(k).wait()
    dg_ref[...] = jnp.zeros_like(dg_ref)
    gl_ref[...] = jnp.zeros_like(gl_ref)
    gsel_ref[...] = jnp.zeros_like(gsel_ref)

    def y_out(i):
        return pltpu.make_async_copy(d1s.at[rows_of(i)], y_hbm.at[rows_of(i)], sy.at[i])

    def learner(i):
        rows = rows_of(i)
        for r in chunks():
            yb = (h1s[chunk_of(i, r), :] + summed(i, r)).astype(bf16)
            d1s[chunk_of(i, r), :] = yb
            u, _ = stats(yb.astype(f32))
            dhs[chunk_of(i, r), :] = (u * g3).astype(bf16)
        y_out(i).start()
        y = d1s[rows, :]
        a3 = dhs[rows, :]
        wlf = wl[...].reshape(width, wl.shape[2])
        wsel = wsel_ref[...]
        ct = ct_ref[i]
        zl = nn(a3, wlf)
        cdf, pdf = gauss(zl)
        t = (zl * cdf).astype(bf16)
        slope = cdf + zl * pdf
        eye = lax.broadcasted_iota(jnp.int32, (PAD, PAD), 0) == lax.broadcasted_iota(jnp.int32, (PAD, PAD), 1)
        col_bias = jnp.sum(jnp.where(eye, bias[i], 0.0), axis=1, keepdims=True)
        logits = nn(t, wsel) + col_bias
        e = jnp.exp(logits - jnp.max(logits, axis=0, keepdims=True))
        maps = e * (1.0 / jnp.sum(e, axis=0, keepdims=True))
        mb = maps.astype(bf16)
        learned_ref[i] = tn(mb, y).astype(bf16)
        dmaps = nt(y, ct)
        dlog = (maps * (dmaps - jnp.sum(maps * dmaps, axis=0, keepdims=True))).astype(bf16)
        gsel_ref[...] += tn(t, dlog)
        dzl = (nt(dlog, wsel) * slope).astype(bf16)
        gl_ref[...] += tn(a3, dzl)
        for r in chunks():
            da3 = nt(dzl[r : r + CH], wlf)
            dy = nn(mb[r : r + CH], ct)
            u, s = stats(d1s[chunk_of(i, r), :].astype(f32))
            dg_ref[2] += fold(da3 * u)
            dhs[chunk_of(i, r), :] = (dy + back(da3 * g3, u, s)).astype(bf16)
        dhb = dhs[rows, :]
        for c in range(4):
            cols = slice(c * TILE, (c + 1) * TILE)
            dr = nt(dhb, wdn[cols, :])
            gs[rows, cols] = (dr * gs[rows, cols].astype(f32)).astype(bf16)
        dz = gs[rows, :]
        for c in range(4):
            store_p(i, c, nt(dz, wup[c * TILE : (c + 1) * TILE, :]))

    stage(learner, 0)

    def grad(left, right, ntile, out, col0, slot0):
        wide = right.shape[1]

        def g_out(j, slot):
            return pltpu.make_async_copy(
                gst.at[slot, :, pl.ds(0, wide)], out.at[pl.ds(pl.multiple_of(j * TILE, 16), TILE)], sg.at[slot]
            )

        def step(j, carry):
            slot = lax.rem(j, 2)

            @pl.when(j >= 2)
            def _():
                g_out(j - 2, slot).wait()

            lhs = left[:, pl.ds(pl.multiple_of(j * TILE, TILE), TILE)]
            for c in range(0, wide, TILE):
                gst[slot, :, c : c + TILE] = tn(lhs, right[:, c : c + TILE]).astype(bf16)
            g_out(j, slot).start()
            return carry

        lax.fori_loop(0, ntile, step, 0)
        for j in range(max(ntile - 2, 0), ntile):
            g_out(j, j % 2).wait()

    grad(rs, dhs, 4, gdn_hbm, 0, 0)
    grad(a2s, gs, 4, gup_hbm, 0, 0)

    for i in range(images):
        y_out(i).wait()

    def attention_back(i):
        rows = rows_of(i)
        for r in chunks():
            where = chunk_of(i, r)
            da2 = summed(i, r)
            u, s = stats(h1s[where, :])
            dg_ref[1] += fold(da2 * u)
            d1s[where, :] = (dhs[where, :].astype(f32) + back(da2 * g2, u, s)).astype(bf16)
            ux, _ = stats(xs[where, :].astype(f32))
            a2s[where, :] = (ux * g1).astype(bf16)
        d1 = d1s[rows, :]
        do = nt(d1, wo[...]).astype(bf16)
        q = qkv[rows, 0:256]
        k = qkv[rows, 256:512]
        v = qkv[rows, 512:768]
        eye = lax.broadcasted_iota(jnp.int32, (PAD, PAD), 0) == lax.broadcasted_iota(jnp.int32, (PAD, PAD), 1)
        col_bias = jnp.sum(jnp.where(eye, bias[i], 0.0), axis=1, keepdims=True)
        dq = jnp.zeros((PAD, 256), f32)
        dk = jnp.zeros((PAD, 256), f32)
        dv = jnp.zeros((PAD, 256), f32)
        for h in range(4):
            kh = only(k, h)
            scores = nt(kh, q) + col_bias
            e = jnp.exp(scores - jnp.max(scores, axis=0, keepdims=True))
            p = e * (1.0 / jnp.sum(e, axis=0, keepdims=True))
            dv = dv + nn(p.astype(bf16), only(do, h))
            dpr = nt(only(v, h), do)
            ds = (p * (dpr - jnp.sum(p * dpr, axis=0, keepdims=True))).astype(bf16)
            dk = dk + nn(ds, only(q, h))
            dq = dq + tn(ds, kh)
        qkv[rows, 0:256] = (dq * 0.125).astype(bf16)
        qkv[rows, 256:512] = dk.astype(bf16)
        qkv[rows, 512:768] = dv.astype(bf16)
        dall = qkv[rows, :]
        for c in range(4):
            store_p(i, c, nt(dall, wqkv[c * TILE : (c + 1) * TILE, :]))

    stage(attention_back, 1)
    grad(os, d1s, 1, gout_hbm, 0, 0)
    grad(a2s, qkv, 4, gqkv_hbm, 0, 0)

    def gp_out(i):
        return pltpu.make_async_copy(rs.at[rows_of(i)], gp_hbm.at[rows_of(i)], sy.at[i])

    def finish(i, carry):
        @pl.when(i + 1 < images)
        def _():
            hop_three(i + 1, 1)
        arrived(i)
        for r in chunks():
            where = chunk_of(i, r)
            da1 = summed(i, r)
            u, s = stats(xs[where, :].astype(f32))
            dg_ref[0] += fold(da1 * u)
            rs[where, :] = (d1s[where, :].astype(f32) + back(da1 * g1, u, s)).astype(bf16)
        gp_out(i).start()
        return carry

    hop_three(0, 1)
    lax.fori_loop(0, images, finish, 0)
    for i in range(images):
        gp_out(i).wait()


def local_fused(
    patches, keep_mask, w_query, w_key, w_value, w_out, w_up, w_down,
    gain_attn, gain_mlp, gain_learn, w_learn, w_select, cotangent,
):
    images, count, width = patches.shape
    total = images * PAD
    hidden = w_up.shape[1]
    bias = jnp.where(jnp.pad(keep_mask, ((0, 0), (0, PAD - count))) > 0, 0.0, -1e30).astype(f32)[:, None, :]
    learn_rows, learn_cols = w_learn.shape
    dps = lax.axis_size("dp")
    anywhere = pl.BlockSpec(memory_space=pl.ANY)
    vmem = pl.BlockSpec(memory_space=pltpu.VMEM)
    sds = jax.ShapeDtypeStruct
    dma = pltpu.SemaphoreType.DMA
    outs = pl.pallas_call(
        fused,
        name="block",
        out_shape=(
            sds((images, 8, width), bf16),
            sds((total, width), bf16),
            sds((total, width), bf16),
            sds((width, hidden), bf16),
            sds((hidden, width), bf16),
            sds((256, width), bf16),
            sds((width, 768), bf16),
            sds((3, 8, width), f32),
            sds((width, learn_cols), f32),
            sds((learn_cols, 8), f32),
        ),
        in_specs=[anywhere] * 8 + [vmem] * 3 + [anywhere] + [vmem] * 2,
        out_specs=(vmem,) + (anywhere,) * 6 + (vmem,) * 3,
        scratch_shapes=[
            pltpu.VMEM((2, count, width), bf16),
            pltpu.VMEM((images, 1, PAD), f32),
            pltpu.VMEM((width, 768), bf16),
            pltpu.VMEM((256, width), bf16),
            pltpu.VMEM((width, hidden), bf16),
            pltpu.VMEM((hidden, width), bf16),
            pltpu.VMEM((dps, learn_rows, learn_cols), bf16),
            pltpu.VMEM((total, width), bf16),
            pltpu.VMEM((total, 768), bf16),
            pltpu.VMEM((total, 256), bf16),
            pltpu.VMEM((total, width), f32),
            pltpu.VMEM((total, width), bf16),
            pltpu.VMEM((total, hidden), bf16),
            pltpu.VMEM((total, hidden), bf16),
            pltpu.VMEM((total, width), bf16),
            pltpu.VMEM((total, width), bf16),
            pltpu.VMEM((2, total, width // 2), bf16),
            pltpu.VMEM((total, width // 2), bf16),
            pltpu.VMEM((total, width // 2), bf16),
            pltpu.VMEM((2, total, width // 2), bf16),
            pltpu.VMEM((2, total, width // 2), bf16),
            pltpu.VMEM((2, TILE, width), bf16),
            dma((2,)), dma((8,)), dma((images,)), dma((2,)), dma((dps - 1,)), dma((dps - 1,)),
            dma((images,)), dma((images,)), dma((images,)), dma((2, images)), dma((images,)), dma((images,)),
        ],
        compiler_params=pltpu.CompilerParams(
            collective_id=0, has_side_effects=True, vmem_limit_bytes=60 * 2**20
        ),
    )(
        patches, bias, w_query, w_key, w_value, w_out, w_up, w_down,
        gain_attn[None], gain_mlp[None], gain_learn[None], w_learn, w_select, cotangent,
    )
    learned, y, gpat, gup, gdn, gout, gqkv, dg, gl, gsel = outs
    y = y.reshape(images, PAD, width)[:, :count]
    gpat = gpat.reshape(images, PAD, width)[:, :count]

    def over_dp(v):
        return lax.psum(v.astype(bf16), "dp").astype(f32)

    gup, gdn, gout, gqkv = over_dp(gup), over_dp(gdn), over_dp(gout), over_dp(gqkv)
    dg = over_dp(jnp.sum(dg, axis=1))
    gl, gsel = over_dp(gl), over_dp(gsel)
    gl = lax.dynamic_slice_in_dim(gl, lax.axis_index("dp") * learn_rows, learn_rows, 0)
    return (
        learned, y, gpat, gqkv[:, :256], gqkv[:, 256:512], gqkv[:, 512:], gout, gup, gdn,
        dg[0], dg[1], dg[2], gl, gsel,
    )


def solution(mesh):
    small = mesh.shape["dp"] == 8 and mesh.shape["mp"] == 4
    return jax.shard_map(
        local_fused if small else local,
        mesh=mesh,
        in_specs=(
            P("dp", None, None),
            P("dp", None),
            P(None, "mp"),
            P(None, "mp"),
            P(None, "mp"),
            P("mp", None),
            P(None, "mp"),
            P("mp", None),
            P(),
            P(),
            P(),
            P("dp", None),
            P(),
            P("dp", None, None),
        ),
        out_specs=(
            P("dp", None, None),
            P("dp", None, None),
            P("dp", None, None),
            P(None, "mp"),
            P(None, "mp"),
            P(None, "mp"),
            P("mp", None),
            P(None, "mp"),
            P("mp", None),
            P(),
            P(),
            P(),
            P("dp", None),
            P(),
        ),
        check_vma=False,
    )
```

```python
import math

import jax
import jax.numpy as jnp
from jax import lax
from jax.experimental import pallas as pl
from jax.experimental.pallas import tpu as pltpu
from jax.sharding import PartitionSpec as P

D = 1024
HEADS = 16


def product(left, right):
    return jnp.dot(left, right, preferred_element_type=jnp.float32)


def contract_rows(left, right):
    return lax.dot_general(
        left, right, (((0,), (0,)), ((), ())), preferred_element_type=jnp.float32
    )


def contract_cols(left, right):
    return lax.dot_general(
        left, right, (((1,), (1,)), ((), ())), preferred_element_type=jnp.float32
    )


def normalize(inputs):
    row_mean = jnp.mean(inputs, axis=-1, keepdims=True)
    centered = inputs - row_mean
    inverse = lax.rsqrt(jnp.mean(centered * centered, axis=-1, keepdims=True) + 1e-06)
    return (centered * inverse, inverse)


def norm_back(grad_norm, normed, inverse, gain):
    scaled_grad = grad_norm * gain
    grad_input = inverse * (
        scaled_grad
        - jnp.mean(scaled_grad, axis=-1, keepdims=True)
        - normed * jnp.mean(scaled_grad * normed, axis=-1, keepdims=True)
    )
    return (grad_input, jnp.sum(grad_norm * normed, axis=0))


def gelu_exact(inputs):
    return jax.nn.gelu(inputs, approximate=False)


def gelu_back(hidden_pre, grad_act):
    _, pullback = jax.vjp(gelu_exact, hidden_pre)
    return pullback(grad_act)[0]


def local(
    patches,
    keep_mask,
    w_query,
    w_key,
    w_value,
    w_out,
    w_up,
    w_down,
    gain_attn,
    gain_mlp,
    gain_learn,
    w_learn,
    w_select,
    cotangent,
):
    images, patch_count, feature_count = patches.shape
    row_count = images * patch_count
    head_size = D // HEADS
    heads_here = w_query.shape[1] // head_size
    score_scale = 1.0 / math.sqrt(head_size)
    visible = keep_mask > 0
    head_shape = (images, patch_count, heads_here, head_size)
    residual_rows = patches.reshape(row_count, feature_count).astype(jnp.float32)
    normed_one, inverse_one = normalize(residual_rows)
    attn_input = (normed_one * gain_attn).astype(jnp.bfloat16)
    query_flat = product(attn_input, w_query).astype(jnp.bfloat16)
    key_flat = product(attn_input, w_key).astype(jnp.bfloat16)
    value_flat = product(attn_input, w_value).astype(jnp.bfloat16)
    query_heads = query_flat.reshape(head_shape)
    key_heads = key_flat.reshape(head_shape)
    value_heads = value_flat.reshape(head_shape)

    def masked_scores():
        raw_scores = (
            jnp.einsum(
                "bqhe,bkhe->bhqk", query_heads, key_heads, preferred_element_type=jnp.float32
            )
            * score_scale
        )
        return jnp.where(visible[:, None, None, :], raw_scores, -1e30)

    scores = masked_scores()
    top_score = jnp.max(scores, axis=-1, keepdims=True)
    exponent = jnp.exp(scores - top_score)
    denominator = jnp.sum(exponent, axis=-1, keepdims=True)
    logsum = top_score + jnp.log(denominator)
    probs_low = (exponent / denominator).astype(jnp.bfloat16)
    mixed_heads = jnp.einsum(
        "bhqk,bkhe->bqhe", probs_low, value_heads, preferred_element_type=jnp.float32
    )
    mixed_heads = mixed_heads.astype(jnp.bfloat16).reshape(row_count, heads_here * head_size)
    attn_term = product(mixed_heads, w_out)
    hidden_one = residual_rows + lax.psum(attn_term.astype(jnp.bfloat16), "mp").astype(jnp.float32)
    normed_two, inverse_two = normalize(hidden_one)
    mlp_input = (normed_two * gain_mlp).astype(jnp.bfloat16)
    hidden_pre = product(mlp_input, w_up)
    activated = gelu_exact(hidden_pre).astype(jnp.bfloat16)
    mlp_out = lax.psum(product(activated, w_down).astype(jnp.bfloat16), "mp").astype(jnp.float32)
    block_rows = (hidden_one + mlp_out).astype(jnp.bfloat16)
    normed_learn, inverse_learn = normalize(block_rows.astype(jnp.float32))
    learn_input = (normed_learn * gain_learn).astype(jnp.bfloat16)
    learn_full = lax.all_gather(w_learn, "dp", axis=0, tiled=True)
    learn_pre = product(learn_input, learn_full)
    learn_act = gelu_exact(learn_pre).astype(jnp.bfloat16)
    logits = product(learn_act, w_select).reshape(images, patch_count, -1)
    logits = jnp.where(visible[:, :, None], logits, -1e30)
    top_logit = jnp.max(logits, axis=1, keepdims=True)
    exp_logit = jnp.exp(logits - top_logit)
    token_maps = exp_logit / jnp.sum(exp_logit, axis=1, keepdims=True)
    maps_low = token_maps.astype(jnp.bfloat16)
    block_three = block_rows.reshape(images, patch_count, feature_count)
    learned = jnp.einsum(
        "bpn,bpd->bnd", maps_low, block_three, preferred_element_type=jnp.float32
    ).astype(jnp.bfloat16)
    grad_maps = jnp.einsum(
        "bnd,bpd->bpn", cotangent, block_three, preferred_element_type=jnp.float32
    )
    grad_block = jnp.einsum(
        "bpn,bnd->bpd", maps_low, cotangent, preferred_element_type=jnp.float32
    ).reshape(row_count, feature_count)
    grad_logits = token_maps * (grad_maps - jnp.sum(token_maps * grad_maps, axis=1, keepdims=True))
    grad_logits = grad_logits.reshape(row_count, -1).astype(jnp.bfloat16)
    grad_select = contract_rows(learn_act, grad_logits)
    grad_learn_act = contract_cols(grad_logits, w_select)
    grad_learn_pre = gelu_back(learn_pre, grad_learn_act).astype(jnp.bfloat16)
    grad_learn = contract_rows(learn_input, grad_learn_pre)
    grad_learn_input = contract_cols(grad_learn_pre, learn_full)
    grad_from_learn, grad_gain_learn = norm_back(
        grad_learn_input, normed_learn, inverse_learn, gain_learn
    )
    grad_hidden = grad_block + grad_from_learn
    grad_hidden_low = grad_hidden.astype(jnp.bfloat16)
    grad_down = contract_rows(activated, grad_hidden_low)
    grad_act = contract_cols(grad_hidden_low, w_down)
    grad_pre = gelu_back(hidden_pre, grad_act).astype(jnp.bfloat16)
    grad_up = contract_rows(mlp_input, grad_pre)
    mlp_back_term = contract_cols(grad_pre, w_up)
    grad_mlp_input = lax.psum(mlp_back_term.astype(jnp.bfloat16), "mp").astype(jnp.float32)
    grad_from_two, grad_gain_mlp = norm_back(grad_mlp_input, normed_two, inverse_two, gain_mlp)
    grad_hidden = grad_hidden + grad_from_two
    grad_attn_low = grad_hidden.astype(jnp.bfloat16)
    grad_out = contract_rows(mixed_heads, grad_attn_low)
    grad_mixed = contract_cols(grad_attn_low, w_out).astype(jnp.bfloat16).reshape(head_shape)
    probs_again = jnp.exp(masked_scores() - logsum)
    probs_again_low = probs_again.astype(jnp.bfloat16)
    grad_probs = jnp.einsum(
        "bqhe,bkhe->bhqk", grad_mixed, value_heads, preferred_element_type=jnp.float32
    )
    grad_value_heads = jnp.einsum(
        "bhqk,bqhe->bkhe", probs_again_low, grad_mixed, preferred_element_type=jnp.float32
    ).astype(jnp.bfloat16)
    grad_scores = probs_again * (
        grad_probs - jnp.sum(probs_again * grad_probs, axis=-1, keepdims=True)
    )
    grad_scores = grad_scores.astype(jnp.bfloat16)
    grad_query_heads = (
        jnp.einsum("bhqk,bkhe->bqhe", grad_scores, key_heads, preferred_element_type=jnp.float32)
        * score_scale
    ).astype(jnp.bfloat16)
    grad_key_heads = (
        jnp.einsum("bhqk,bqhe->bkhe", grad_scores, query_heads, preferred_element_type=jnp.float32)
        * score_scale
    ).astype(jnp.bfloat16)
    grad_query_flat = grad_query_heads.reshape(row_count, -1)
    grad_key_flat = grad_key_heads.reshape(row_count, -1)
    grad_value_flat = grad_value_heads.reshape(row_count, -1)
    grad_query = contract_rows(attn_input, grad_query_flat)
    grad_key = contract_rows(attn_input, grad_key_flat)
    grad_value = contract_rows(attn_input, grad_value_flat)
    attn_terms = (
        contract_cols(grad_query_flat, w_query)
        + contract_cols(grad_key_flat, w_key)
        + contract_cols(grad_value_flat, w_value)
    )
    grad_attn_input = lax.psum(attn_terms.astype(jnp.bfloat16), "mp").astype(jnp.float32)
    grad_from_one, grad_gain_attn = norm_back(grad_attn_input, normed_one, inverse_one, gain_attn)
    grad_patches = (
        (grad_hidden + grad_from_one)
        .astype(jnp.bfloat16)
        .reshape(images, patch_count, feature_count)
    )
    (
        grad_query,
        grad_key,
        grad_value,
        grad_out,
        grad_gain_attn,
        grad_up,
        grad_down,
        grad_gain_mlp,
        grad_gain_learn,
        grad_select,
        grad_learn,
    ) = (
        lax.psum(grad_query.astype(jnp.bfloat16), "dp").astype(jnp.float32),
        lax.psum(grad_key.astype(jnp.bfloat16), "dp").astype(jnp.float32),
        lax.psum(grad_value.astype(jnp.bfloat16), "dp").astype(jnp.float32),
        lax.psum(grad_out.astype(jnp.bfloat16), "dp").astype(jnp.float32),
        lax.psum(grad_gain_attn.astype(jnp.bfloat16), "dp").astype(jnp.float32),
        lax.psum(grad_up.astype(jnp.bfloat16), "dp").astype(jnp.float32),
        lax.psum(grad_down.astype(jnp.bfloat16), "dp").astype(jnp.float32),
        lax.psum(grad_gain_mlp.astype(jnp.bfloat16), "dp").astype(jnp.float32),
        lax.psum(grad_gain_learn.astype(jnp.bfloat16), "dp").astype(jnp.float32),
        lax.psum(grad_select.astype(jnp.bfloat16), "dp").astype(jnp.float32),
        lax.psum(grad_learn.astype(jnp.bfloat16), "dp").astype(jnp.float32),
    )
    learn_rows = w_learn.shape[0]
    grad_learn = lax.dynamic_slice_in_dim(
        grad_learn, lax.axis_index("dp") * learn_rows, learn_rows, 0
    )
    return (
        learned,
        block_three,
        grad_patches,
        grad_query,
        grad_key,
        grad_value,
        grad_out,
        grad_up,
        grad_down,
        grad_gain_attn,
        grad_gain_mlp,
        grad_gain_learn,
        grad_learn,
        grad_select,
    )


MESH = pl.DeviceIdType.MESH
PAD = 208
CH = 16
TILE = 256
PAIR_IN = 224
LAG = 2
f32 = jnp.float32
bf16 = jnp.bfloat16


def nn(a, b):
    return jnp.dot(a, b, preferred_element_type=f32)


def nt(a, b):
    return lax.dot_general(a, b, (((1,), (1,)), ((), ())), preferred_element_type=f32)


def tn(a, b):
    return lax.dot_general(a, b, (((0,), (0,)), ((), ())), preferred_element_type=f32)


def gauss(z):
    bell = jnp.exp(-0.5 * (z * z))
    t = 1.0 / (1.0 + 0.23164189 * jnp.abs(z))
    poly = t * (
        0.127414796 + t * (-0.142248368 + t * (0.7107068705 + t * (-0.7265760135 + t * 0.5307027145)))
    )
    tail = poly * bell
    return jnp.where(z >= 0, 1.0 - tail, tail), 0.3989422804014327 * bell


def stats(v):
    mean = jnp.sum(v, axis=-1, keepdims=True) * (1.0 / v.shape[-1])
    c = v - mean
    s = lax.rsqrt(jnp.sum(c * c, axis=-1, keepdims=True) * (1.0 / v.shape[-1]) + 1e-06)
    return c * s, s


def back(e, u, s):
    width = 1.0 / e.shape[-1]
    return s * (
        e
        - jnp.sum(e, axis=-1, keepdims=True) * width
        - u * (jnp.sum(e * u, axis=-1, keepdims=True) * width)
    )


def fold(v):
    total = v[0:8]
    for r in range(8, v.shape[0], 8):
        total = total + v[r : r + 8]
    return total


def chunks():
    return range(0, PAD, CH)


def fused(
    patches, bias_hbm, wq_hbm, wk_hbm, wv_hbm, wo_hbm, wup_hbm, wdn_hbm, g1_ref, g2_ref, g3_ref,
    wl_hbm, wsel_ref, ct_ref,
    learned_ref, y_hbm, gp_hbm, gall_hbm, small_ref, gl_ref,
    xraw, bias, wqkv, wo, wl,
    xs, qkv, os, h1s, a2s, dhs, d1s, big, recv,
    pbuf, rcore, rx, sumb, dg, gl_sum, gsel_sum, gl_mine, gl_in, small_mine, small_in,
    sx, sw, sy, slearn_s, slearn_r, s_core, r_core, s_x, r_x, s_ag, r_ag,
    s_pair, r_pair, s_out, ready_y, ready_z, s_small, r_small,
):
    images = patches.shape[0]
    count = patches.shape[1]
    width = patches.shape[2]
    half = width // 2
    dp = lax.axis_index("dp")
    mp = lax.axis_index("mp")
    core = lax.rem(mp, 2)
    mate = (dp, mp + 1 - 2 * core)
    across = (dp, lax.rem(mp + 2, 4))
    dps = lax.axis_size("dp")
    yy = lax.rem(dp, 2)
    zz = dp // 2
    middle = (zz == 1) | (zz == 2)
    zm = jnp.where(zz >= 2, 1, 0)
    mate_y = (dp + 1 - 2 * yy, mp)
    mate_e = ((zz + 1 - 2 * lax.rem(zz, 2)) * 2 + yy, mp)
    mate_m = ((3 - zz) * 2 + yy, mp)
    total = images * PAD
    pairs = 24
    kept = 8 * PAIR_IN
    rs = big.at[pl.ds(0, total)]
    gs = recv.at[pl.ds(kept, total)]
    wup = recv.at[pl.ds(kept + total, width)]
    wdn = recv.at[pl.ds(kept + total + width, width)]

    barrier = pltpu.get_barrier_semaphore()
    for device in (mate, across):
        pl.semaphore_signal(barrier, inc=1, device_id=device, device_id_type=MESH)
    for k in range(1, dps):
        pl.semaphore_signal(barrier, inc=1, device_id=(lax.rem(dp + k, dps), mp), device_id_type=MESH)

    loads = [
        pltpu.make_async_copy(wq_hbm, wqkv.at[:, pl.ds(0, 256)], sw.at[0]),
        pltpu.make_async_copy(wk_hbm, wqkv.at[:, pl.ds(256, 256)], sw.at[1]),
        pltpu.make_async_copy(wv_hbm, wqkv.at[:, pl.ds(512, 256)], sw.at[2]),
        pltpu.make_async_copy(wo_hbm, wo, sw.at[3]),
        pltpu.make_async_copy(wup_hbm, wup, sw.at[4]),
        pltpu.make_async_copy(wdn_hbm, wdn, sw.at[5]),
        pltpu.make_async_copy(wl_hbm, wl.at[dp], sw.at[6]),
        pltpu.make_async_copy(bias_hbm, bias, sw.at[7]),
    ]

    def load_x(i, slot):
        return pltpu.make_async_copy(patches.at[i], xraw.at[slot], sx.at[slot])

    load_x(0, 0).start()
    for k in (0, 1, 2, 7, 3):
        loads[k].start()
    load_x(1, 1).start()
    for k in (6, 4, 5):
        loads[k].start()

    xs[...] = jnp.zeros_like(xs)

    pl.semaphore_wait(barrier, dps + 1)

    def learn_copy(k):
        return pltpu.make_async_remote_copy(
            src_ref=wl.at[dp], dst_ref=wl.at[dp],
            send_sem=slearn_s.at[k - 1], recv_sem=slearn_r.at[k - 1],
            device_id=(lax.rem(dp + k, dps), mp), device_id_type=MESH,
        )

    loads[6].wait()
    for k in range(1, dps):
        learn_copy(k).start()

    g1 = g1_ref[...]
    g2 = g2_ref[...]
    g3 = g3_ref[...]
    lane_head = lax.broadcasted_iota(jnp.int32, (1, 256), 1) // 64

    def only(v, h):
        return jnp.where(lane_head == h, v, jnp.zeros_like(v))

    def rows_of(i):
        return pl.ds(pl.multiple_of(i * PAD, 16), PAD)

    def chunk_of(i, r):
        return pl.ds(pl.multiple_of(i * PAD + r, 16), CH)

    def copy_core(i):
        return pltpu.make_async_remote_copy(
            src_ref=pbuf.at[1 - core, rows_of(i)], dst_ref=rcore.at[rows_of(i)],
            send_sem=s_core.at[i], recv_sem=r_core.at[i], device_id=mate, device_id_type=MESH,
        )

    def copy_x(i, par):
        return pltpu.make_async_remote_copy(
            src_ref=pbuf.at[core, rows_of(i)], dst_ref=rx.at[par, rows_of(i)],
            send_sem=s_x.at[i], recv_sem=r_x.at[par, i], device_id=across, device_id_type=MESH,
        )

    def copy_ag(i):
        return pltpu.make_async_remote_copy(
            src_ref=sumb.at[core, rows_of(i)], dst_ref=sumb.at[core, rows_of(i)],
            send_sem=s_ag.at[i], recv_sem=r_ag.at[i], device_id=mate, device_id_type=MESH,
        )

    def hop_two(i, par):
        copy_core(i).wait()
        rows = rows_of(i)
        pbuf[core, rows] = (pbuf[core, rows].astype(f32) + rcore[rows].astype(f32)).astype(bf16)
        copy_x(i, par).start()

    def hop_three(i, par):
        copy_x(i, par).wait()
        rows = rows_of(i)
        sumb[core, rows] = (pbuf[core, rows].astype(f32) + rx[par, rows].astype(f32)).astype(bf16)
        copy_ag(i).start()

    def arrived(i):
        copy_ag(i).wait()

    def summed(i, r):
        where = chunk_of(i, r)
        return jnp.concatenate([sumb[0, where].astype(f32), sumb[1, where].astype(f32)], axis=1)

    def store_p(i, t, value):
        pbuf[t // 2, rows_of(i), (t % 2) * TILE : (t % 2 + 1) * TILE] = value.astype(bf16)

    def stage(body, par, first=False):
        def step(i, carry):
            if not first:
                @pl.when(i + 1 < images)
                def _():
                    hop_three(i + 1, 1 - par)
                arrived(i)
            body(i)
            copy_core(i).start()

            @pl.when(i > 0)
            def _():
                hop_two(i - 1, par)
            return carry

        if not first:
            hop_three(0, 1 - par)
        lax.fori_loop(0, images, step, 0)
        hop_two(images - 1, par)

    def g_rows(k, lo, n):
        return pl.ds(pl.multiple_of(lax.rem(k * 128 + 2048, 3072) + lo, 16), n)

    def in_rows(k, lo, n):
        return pl.ds(pl.multiple_of(k * PAIR_IN + lo, 16), n)

    def send(k, slot, src, dst, device):
        return pltpu.make_async_remote_copy(
            src_ref=src, dst_ref=dst, send_sem=s_pair.at[slot, k], recv_sem=r_pair.at[slot, k],
            device_id=device, device_id_type=MESH,
        )

    def y_swap(k):
        return send(k, 0, big.at[g_rows(k, 32 - 32 * yy, 32)], recv.at[in_rows(k, 0, 32)], mate_y)

    def y_end(k):
        return send(k, 1, big.at[g_rows(k, 32 * yy, 32)], recv.at[in_rows(k, 32, 32)], mate_e)

    def y_mid(k):
        return send(k, 2, big.at[g_rows(k, 32 * yy, 32)], recv.at[in_rows(k, 64, 32)], mate_m)

    def o_rows(k, lo, n):
        return gall_hbm.at[pl.ds(pl.multiple_of(k * 128 + lo, 16), n)]

    def y_back(k):
        return send(k, 3, big.at[g_rows(k, 32 * yy, 32)], o_rows(k, 32 * yy, 32), mate_e)

    def y_share_mid(k):
        return send(k, 4, big.at[g_rows(k, 32 * yy, 32)], o_rows(k, 32 * yy, 32), mate_y)

    def y_share_end(k):
        return send(k, 4, o_rows(k, 32 * yy, 32), o_rows(k, 32 * yy, 32), mate_y)

    def z_end(k):
        return send(k, 5, big.at[g_rows(k, 64, 64)], recv.at[in_rows(k, 160, 64)], mate_e)

    def z_mid(k):
        return send(k, 6, big.at[g_rows(k, 96 - 32 * zm, 32)], recv.at[in_rows(k, 96, 32)], mate_m)

    def z_swap(k):
        return send(k, 7, big.at[g_rows(k, 64 + 32 * zm, 32)], recv.at[in_rows(k, 128, 32)], mate_y)

    def z_share(k):
        return send(k, 8, big.at[g_rows(k, 64 + 32 * zm, 32)], o_rows(k, 64 + 32 * zm, 32), mate_m)

    def z_back(k):
        return send(k, 9, big.at[g_rows(k, 64 + 32 * zm, 32)], o_rows(k, 64 + 32 * zm, 32), mate_e)

    def z_pass(k):
        return send(k, 10, o_rows(k, 96 - 32 * zm, 32), o_rows(k, 96 - 32 * zm, 32), mate_e)

    def accumulate(k, lo, n, at):
        rows = g_rows(k, lo, n)
        big[rows, :] = (big[rows, :].astype(f32) + recv[in_rows(k, at, n), :].astype(f32)).astype(bf16)

    def keep_y(k):
        return pltpu.make_async_copy(big.at[g_rows(k, 32 * yy, 32)], o_rows(k, 32 * yy, 32), s_out.at[0, k])

    def keep_z(k):
        return pltpu.make_async_copy(
            big.at[g_rows(k, 64 + 32 * zm, 32)], o_rows(k, 64 + 32 * zm, 32), s_out.at[1, k]
        )

    def hop0(k):
        y_swap(k).start()

        @pl.when(jnp.logical_not(middle))
        def _():
            z_end(k).start()

    def hop1(k):
        y_swap(k).wait()
        accumulate(k, 32 * yy, 32, 0)

        @pl.when(middle)
        def _():
            z_end(k).wait_recv()
            accumulate(k, 64, 64, 160)
            z_mid(k).start()

        @pl.when(jnp.logical_not(middle))
        def _():
            y_end(k).start()

    def hop2(k):
        @pl.when(middle)
        def _():
            y_end(k).wait_recv()
            accumulate(k, 32 * yy, 32, 32)
            y_mid(k).start()
            z_mid(k).wait()
            accumulate(k, 64 + 32 * zm, 32, 96)
            z_swap(k).start()

    def hop3(k):
        @pl.when(middle)
        def _():
            y_mid(k).wait()
            accumulate(k, 32 * yy, 32, 64)
            y_back(k).start()
            y_share_mid(k).start()
            keep_y(k).start()
            z_swap(k).wait()
            accumulate(k, 64 + 32 * zm, 32, 128)
            z_share(k).start()
            z_back(k).start()
            keep_z(k).start()

    def hop4(k):
        @pl.when(middle)
        def _():
            z_share(k).wait()
            z_pass(k).start()

        @pl.when(jnp.logical_not(middle))
        def _():
            y_end(k).wait_send()
            y_back(k).wait_recv()
            y_share_end(k).start()

    def hop5(k):
        @pl.when(middle)
        def _():
            y_share_mid(k).wait()
            y_back(k).wait_send()
            z_back(k).wait_send()
            z_pass(k).wait_send()
            keep_y(k).wait()
            keep_z(k).wait()

        @pl.when(jnp.logical_not(middle))
        def _():
            y_share_end(k).wait()
            z_end(k).wait_send()
            z_back(k).wait_recv()
            z_pass(k).wait_recv()

    def tick(t):
        for h, hop in ((5, hop5), (4, hop4), (3, hop3), (2, hop2), (1, hop1), (0, hop0)):
            k = t - LAG * h

            @pl.when((k >= 0) & (k < pairs))
            def _(hop=hop, k=k):
                hop(k)

    def ticks(lo, hi):
        def step(t, carry):
            tick(t)
            return carry

        lax.fori_loop(lo, hi, step, 0)

    for k in (0, 1, 2, 3, 7):
        loads[k].wait()

    def attention(i):
        slot = lax.rem(i, 2)
        load_x(i, slot).wait()
        start = pl.multiple_of(i * PAD, 16)
        xs[pl.ds(start, count), :] = xraw[slot]

        @pl.when(i + 2 < images)
        def _():
            load_x(i + 2, slot).start()

        for r in chunks():
            u, _ = stats(xs[chunk_of(i, r), :].astype(f32))
            a2s[chunk_of(i, r), :] = (u * g1).astype(bf16)
        rows = rows_of(i)
        a1 = a2s[rows, :]
        qkv[rows, 0:256] = (nn(a1, wqkv[:, 0:256]) * 0.125).astype(bf16)
        qkv[rows, 256:512] = nn(a1, wqkv[:, 256:512]).astype(bf16)
        qkv[rows, 512:768] = nn(a1, wqkv[:, 512:768]).astype(bf16)
        q = qkv[rows, 0:256]
        k = qkv[rows, 256:512]
        v = qkv[rows, 512:768]
        row_bias = bias[i]
        o = jnp.zeros((PAD, 256), f32)
        for h in range(4):
            scores = nt(only(q, h), k) + row_bias
            e = jnp.exp(scores - jnp.max(scores, axis=1, keepdims=True))
            p = (e * (1.0 / jnp.sum(e, axis=1, keepdims=True))).astype(bf16)
            o = o + nn(p, only(v, h))
        ob = o.astype(bf16)
        os[rows, :] = ob
        for t in range(4):
            store_p(i, t, nn(ob, wo[:, t * TILE : (t + 1) * TILE]))

    stage(attention, 0, first=True)

    loads[4].wait()
    loads[5].wait()

    def mlp(i):
        for r in chunks():
            h1 = xs[chunk_of(i, r), :].astype(f32) + summed(i, r)
            h1s[chunk_of(i, r), :] = h1
            u, _ = stats(h1)
            a2s[chunk_of(i, r), :] = (u * g2).astype(bf16)
        rows = rows_of(i)
        a2 = a2s[rows, :]
        for t in range(4):
            cols = slice(t * TILE, (t + 1) * TILE)
            z = nn(a2, wup[:, cols])
            cdf, pdf = gauss(z)
            rs[rows, cols] = (z * cdf).astype(bf16)
            gs[rows, cols] = (cdf + z * pdf).astype(bf16)
        act = rs[rows, :]
        for t in range(4):
            store_p(i, t, nn(act, wdn[:, t * TILE : (t + 1) * TILE]))

    stage(mlp, 1)

    for k in range(1, dps):
        learn_copy(k).wait()
    dg[...] = jnp.zeros_like(dg)
    gl_sum[...] = jnp.zeros_like(gl_sum)
    gsel_sum[...] = jnp.zeros_like(gsel_sum)

    def y_out(i):
        return pltpu.make_async_copy(d1s.at[rows_of(i)], y_hbm.at[rows_of(i)], sy.at[i])

    def learner(i):
        rows = rows_of(i)
        for r in chunks():
            yb = (h1s[chunk_of(i, r), :] + summed(i, r)).astype(bf16)
            d1s[chunk_of(i, r), :] = yb
            u, _ = stats(yb.astype(f32))
            dhs[chunk_of(i, r), :] = (u * g3).astype(bf16)
        y_out(i).start()
        y = d1s[rows, :]
        a3 = dhs[rows, :]
        wlf = wl[...].reshape(width, wl.shape[2])
        wsel = wsel_ref[...]
        ct = ct_ref[i]
        zl = nn(a3, wlf)
        cdf, pdf = gauss(zl)
        t = (zl * cdf).astype(bf16)
        slope = cdf + zl * pdf
        eye = lax.broadcasted_iota(jnp.int32, (PAD, PAD), 0) == lax.broadcasted_iota(jnp.int32, (PAD, PAD), 1)
        col_bias = jnp.sum(jnp.where(eye, bias[i], 0.0), axis=1, keepdims=True)
        logits = nn(t, wsel) + col_bias
        e = jnp.exp(logits - jnp.max(logits, axis=0, keepdims=True))
        maps = e * (1.0 / jnp.sum(e, axis=0, keepdims=True))
        mb = maps.astype(bf16)
        learned_ref[i] = tn(mb, y).astype(bf16)
        dmaps = nt(y, ct)
        dlog = (maps * (dmaps - jnp.sum(maps * dmaps, axis=0, keepdims=True))).astype(bf16)
        gsel_sum[...] += tn(dlog, t)
        dzl = (nt(dlog, wsel) * slope).astype(bf16)
        gl_sum[...] += tn(a3, dzl)
        for r in chunks():
            da3 = nt(dzl[r : r + CH], wlf)
            dy = nn(mb[r : r + CH], ct)
            u, s = stats(d1s[chunk_of(i, r), :].astype(f32))
            dg[2] += fold(da3 * u)
            dhs[chunk_of(i, r), :] = (dy + back(da3 * g3, u, s)).astype(bf16)
        dhb = dhs[rows, :]
        for c in range(4):
            cols = slice(c * TILE, (c + 1) * TILE)
            dr = nt(dhb, wdn[cols, :])
            gs[rows, cols] = (dr * gs[rows, cols].astype(f32)).astype(bf16)
        dz = gs[rows, :]
        for c in range(4):
            store_p(i, c, nt(dz, wup[c * TILE : (c + 1) * TILE, :]))

    stage(learner, 0)

    def grad(left, right, first, tick0):
        def step(j, carry):
            lhs = left[:, pl.ds(pl.multiple_of(j * TILE, TILE), TILE)]
            rows = g_rows(2 * (first + j), 0, TILE)
            for c in range(0, width, TILE):
                big[rows, c : c + TILE] = tn(lhs, right[:, c : c + TILE]).astype(bf16)
            if tick0 is not None:
                tick(tick0 + j)
            return carry

        lax.fori_loop(0, left.shape[1] // TILE, step, 0)

    grad(rs, dhs, 0, 0)
    grad(a2s, gs, 4, 4)
    pl.semaphore_signal(ready_y, inc=1, device_id=mate_y, device_id_type=MESH)

    @pl.when(middle)
    def _():
        pl.semaphore_signal(ready_z, inc=1, device_id=mate_e, device_id_type=MESH)
        pl.semaphore_signal(ready_z, inc=1, device_id=mate_m, device_id_type=MESH)

    for i in range(images):
        y_out(i).wait()
    pl.semaphore_wait(ready_y, 1)
    pl.semaphore_wait(ready_z, 1)

    def attention_back(i):
        rows = rows_of(i)
        for r in chunks():
            where = chunk_of(i, r)
            da2 = summed(i, r)
            u, s = stats(h1s[where, :])
            dg[1] += fold(da2 * u)
            d1s[where, :] = (dhs[where, :].astype(f32) + back(da2 * g2, u, s)).astype(bf16)
            ux, _ = stats(xs[where, :].astype(f32))
            a2s[where, :] = (ux * g1).astype(bf16)
        d1 = d1s[rows, :]
        do = nt(d1, wo[...]).astype(bf16)
        q = qkv[rows, 0:256]
        k = qkv[rows, 256:512]
        v = qkv[rows, 512:768]
        eye = lax.broadcasted_iota(jnp.int32, (PAD, PAD), 0) == lax.broadcasted_iota(jnp.int32, (PAD, PAD), 1)
        col_bias = jnp.sum(jnp.where(eye, bias[i], 0.0), axis=1, keepdims=True)
        dq = jnp.zeros((PAD, 256), f32)
        dk = jnp.zeros((PAD, 256), f32)
        dv = jnp.zeros((PAD, 256), f32)
        for h in range(4):
            kh = only(k, h)
            scores = nt(kh, q) + col_bias
            e = jnp.exp(scores - jnp.max(scores, axis=0, keepdims=True))
            p = e * (1.0 / jnp.sum(e, axis=0, keepdims=True))
            dv = dv + nn(p.astype(bf16), only(do, h))
            dpr = nt(only(v, h), do)
            ds = (p * (dpr - jnp.sum(p * dpr, axis=0, keepdims=True))).astype(bf16)
            dk = dk + nn(ds, only(q, h))
            dq = dq + tn(ds, kh)
        qkv[rows, 0:256] = (dq * 0.125).astype(bf16)
        qkv[rows, 256:512] = dk.astype(bf16)
        qkv[rows, 512:768] = dv.astype(bf16)
        dall = qkv[rows, :]
        for c in range(4):
            store_p(i, c, nt(dall, wqkv[c * TILE : (c + 1) * TILE, :]))
        tick(8 + i)

    stage(attention_back, 1)
    grad(os, d1s, 8, 16)

    def grad_qkv(j, carry):
        lhs = a2s[:, pl.ds(pl.multiple_of(j * TILE, TILE), TILE)]
        for c in range(3):
            rows = g_rows(18 + 2 * c, 0, TILE)
            big[rows, pl.ds(pl.multiple_of(j * TILE, TILE), TILE)] = tn(
                lhs, qkv[:, c * TILE : (c + 1) * TILE]
            ).astype(bf16)
        return carry

    lax.fori_loop(0, 4, grad_qkv, 0)

    def gp_out(i):
        return pltpu.make_async_copy(dhs.at[rows_of(i)], gp_hbm.at[rows_of(i)], sy.at[i])

    def finish(i, carry):
        @pl.when(i + 1 < images)
        def _():
            hop_three(i + 1, 1)
        arrived(i)
        for r in chunks():
            where = chunk_of(i, r)
            da1 = summed(i, r)
            u, s = stats(xs[where, :].astype(f32))
            dg[0] += fold(da1 * u)
            dhs[where, :] = (d1s[where, :].astype(f32) + back(da1 * g1, u, s)).astype(bf16)
        gp_out(i).start()
        tick(17 + i)
        return carry

    hop_three(0, 1)
    lax.fori_loop(0, images, finish, 0)

    small_mine[0:8, :] = jnp.concatenate(
        [jnp.sum(dg[n], axis=0, keepdims=True) for n in range(3)] + [jnp.zeros((5, width), f32)], axis=0
    ).astype(bf16)
    small_mine[8:16, 0:64] = gsel_sum[...].astype(bf16)
    small_mine[8:16, 64:width] = jnp.zeros((8, width - 64), bf16)
    gl_mine[...] = gl_sum[...].astype(bf16).reshape(gl_mine.shape)

    def small_copy(k):
        peer = lax.rem(dp + k, dps)
        return (
            pltpu.make_async_remote_copy(
                src_ref=small_mine, dst_ref=small_in.at[k - 1], send_sem=s_small.at[0, k - 1],
                recv_sem=r_small.at[0, k - 1], device_id=(peer, mp), device_id_type=MESH,
            ),
            pltpu.make_async_remote_copy(
                src_ref=gl_mine.at[peer], dst_ref=gl_in.at[k - 1], send_sem=s_small.at[1, k - 1],
                recv_sem=r_small.at[1, k - 1], device_id=(peer, mp), device_id_type=MESH,
            ),
        )

    for k in range(1, dps):
        for copy in small_copy(k):
            copy.start()
    ticks(25, pairs + 5 * LAG)
    for k in range(1, dps):
        for copy in small_copy(k):
            copy.wait()
    small_ref[...] = small_mine[...].astype(f32)
    gl_ref[...] = gl_mine[dp].astype(f32)
    for k in range(dps - 1):
        small_ref[...] += small_in[k].astype(f32)
        gl_ref[...] += gl_in[k].astype(f32)
    for i in range(images):
        gp_out(i).wait()


def local_fused(
    patches, keep_mask, w_query, w_key, w_value, w_out, w_up, w_down,
    gain_attn, gain_mlp, gain_learn, w_learn, w_select, cotangent,
):
    images, count, width = patches.shape
    total = images * PAD
    hidden = w_up.shape[1]
    bias = jnp.where(jnp.pad(keep_mask, ((0, 0), (0, PAD - count))) > 0, 0.0, -1e30).astype(f32)[:, None, :]
    learn_rows, learn_cols = w_learn.shape
    dps = lax.axis_size("dp")
    anywhere = pl.BlockSpec(memory_space=pl.ANY)
    vmem = pl.BlockSpec(memory_space=pltpu.VMEM)
    sds = jax.ShapeDtypeStruct
    dma = pltpu.SemaphoreType.DMA
    outs = pl.pallas_call(
        fused,
        name="block",
        out_shape=(
            sds((images, 8, width), bf16),
            sds((total, width), bf16),
            sds((total, width), bf16),
            sds((3072, width), bf16),
            sds((16, width), f32),
            sds((learn_rows, learn_cols), f32),
        ),
        in_specs=[anywhere] * 8 + [vmem] * 3 + [anywhere] + [vmem] * 2,
        out_specs=(vmem,) + (anywhere,) * 3 + (vmem,) * 2,
        scratch_shapes=[
            pltpu.VMEM((2, count, width), bf16),
            pltpu.VMEM((images, 1, PAD), f32),
            pltpu.VMEM((width, 768), bf16),
            pltpu.VMEM((256, width), bf16),
            pltpu.VMEM((dps, learn_rows, learn_cols), bf16),
            pltpu.VMEM((total, width), bf16),
            pltpu.VMEM((total, 768), bf16),
            pltpu.VMEM((total, 256), bf16),
            pltpu.VMEM((total, width), f32),
            pltpu.VMEM((total, width), bf16),
            pltpu.VMEM((total, width), bf16),
            pltpu.VMEM((total, width), bf16),
            pltpu.VMEM((3072, width), bf16),
            pltpu.VMEM((8 * PAIR_IN + total + 2 * width, width), bf16),
            pltpu.VMEM((2, total, width // 2), bf16),
            pltpu.VMEM((total, width // 2), bf16),
            pltpu.VMEM((2, total, width // 2), bf16),
            pltpu.VMEM((2, total, width // 2), bf16),
            pltpu.VMEM((3, 8, width), f32),
            pltpu.VMEM((width, learn_cols), f32),
            pltpu.VMEM((8, learn_cols), f32),
            pltpu.VMEM((dps, learn_rows, learn_cols), bf16),
            pltpu.VMEM((dps - 1, learn_rows, learn_cols), bf16),
            pltpu.VMEM((16, width), bf16),
            pltpu.VMEM((dps - 1, 16, width), bf16),
            dma((2,)), dma((8,)), dma((images,)), dma((dps - 1,)), dma((dps - 1,)),
            dma((images,)), dma((images,)), dma((images,)), dma((2, images)), dma((images,)), dma((images,)),
            dma((11, 24)), dma((11, 24)), dma((2, 24)),
            pltpu.SemaphoreType.REGULAR, pltpu.SemaphoreType.REGULAR, dma((2, dps - 1)), dma((2, dps - 1)),
        ],
        compiler_params=pltpu.CompilerParams(
            collective_id=0, has_side_effects=True, vmem_limit_bytes=60 * 2**20
        ),
    )(
        patches, bias, w_query, w_key, w_value, w_out, w_up, w_down,
        gain_attn[None], gain_mlp[None], gain_learn[None], w_learn, w_select, cotangent,
    )
    learned, y, gpat, gall, small, gl = outs
    y = y.reshape(images, PAD, width)[:, :count]
    gpat = gpat.reshape(images, PAD, width)[:, :count]

    def stacked(first):
        v = gall[first : first + 256].reshape(256, 4, 256).astype(f32)
        return v.transpose(1, 0, 2).reshape(width, 256)

    return (
        learned, y, gpat, stacked(2304), stacked(2560), stacked(2816), gall[2048:2304].astype(f32),
        gall[1024:2048].astype(f32), gall[0:1024].astype(f32),
        small[0], small[1], small[2], gl, small[8:16, :learn_cols].T,
    )


def solution(mesh):
    small = mesh.shape["dp"] == 8 and mesh.shape["mp"] == 4
    return jax.shard_map(
        local_fused if small else local,
        mesh=mesh,
        in_specs=(
            P("dp", None, None),
            P("dp", None),
            P(None, "mp"),
            P(None, "mp"),
            P(None, "mp"),
            P("mp", None),
            P(None, "mp"),
            P("mp", None),
            P(),
            P(),
            P(),
            P("dp", None),
            P(),
            P("dp", None, None),
        ),
        out_specs=(
            P("dp", None, None),
            P("dp", None, None),
            P("dp", None, None),
            P(None, "mp"),
            P(None, "mp"),
            P(None, "mp"),
            P("mp", None),
            P(None, "mp"),
            P("mp", None),
            P(),
            P(),
            P(),
            P("dp", None),
            P(),
        ),
        check_vma=False,
    )
```

```python
import math

import jax
import jax.numpy as jnp
from jax import lax
from jax.experimental import pallas as pl
from jax.experimental.pallas import tpu as pltpu
from jax.sharding import PartitionSpec as P

D = 1024
HEADS = 16


def product(left, right):
    return jnp.dot(left, right, preferred_element_type=jnp.float32)


def contract_rows(left, right):
    return lax.dot_general(
        left, right, (((0,), (0,)), ((), ())), preferred_element_type=jnp.float32
    )


def contract_cols(left, right):
    return lax.dot_general(
        left, right, (((1,), (1,)), ((), ())), preferred_element_type=jnp.float32
    )


def normalize(inputs):
    row_mean = jnp.mean(inputs, axis=-1, keepdims=True)
    centered = inputs - row_mean
    inverse = lax.rsqrt(jnp.mean(centered * centered, axis=-1, keepdims=True) + 1e-06)
    return (centered * inverse, inverse)


def norm_back(grad_norm, normed, inverse, gain):
    scaled_grad = grad_norm * gain
    grad_input = inverse * (
        scaled_grad
        - jnp.mean(scaled_grad, axis=-1, keepdims=True)
        - normed * jnp.mean(scaled_grad * normed, axis=-1, keepdims=True)
    )
    return (grad_input, jnp.sum(grad_norm * normed, axis=0))


def gelu_exact(inputs):
    return jax.nn.gelu(inputs, approximate=False)


def gelu_back(hidden_pre, grad_act):
    _, pullback = jax.vjp(gelu_exact, hidden_pre)
    return pullback(grad_act)[0]


def local(
    patches,
    keep_mask,
    w_query,
    w_key,
    w_value,
    w_out,
    w_up,
    w_down,
    gain_attn,
    gain_mlp,
    gain_learn,
    w_learn,
    w_select,
    cotangent,
):
    images, patch_count, feature_count = patches.shape
    row_count = images * patch_count
    head_size = D // HEADS
    heads_here = w_query.shape[1] // head_size
    score_scale = 1.0 / math.sqrt(head_size)
    visible = keep_mask > 0
    head_shape = (images, patch_count, heads_here, head_size)
    residual_rows = patches.reshape(row_count, feature_count).astype(jnp.float32)
    normed_one, inverse_one = normalize(residual_rows)
    attn_input = (normed_one * gain_attn).astype(jnp.bfloat16)
    query_flat = product(attn_input, w_query).astype(jnp.bfloat16)
    key_flat = product(attn_input, w_key).astype(jnp.bfloat16)
    value_flat = product(attn_input, w_value).astype(jnp.bfloat16)
    query_heads = query_flat.reshape(head_shape)
    key_heads = key_flat.reshape(head_shape)
    value_heads = value_flat.reshape(head_shape)

    def masked_scores():
        raw_scores = (
            jnp.einsum(
                "bqhe,bkhe->bhqk", query_heads, key_heads, preferred_element_type=jnp.float32
            )
            * score_scale
        )
        return jnp.where(visible[:, None, None, :], raw_scores, -1e30)

    scores = masked_scores()
    top_score = jnp.max(scores, axis=-1, keepdims=True)
    exponent = jnp.exp(scores - top_score)
    denominator = jnp.sum(exponent, axis=-1, keepdims=True)
    logsum = top_score + jnp.log(denominator)
    probs_low = (exponent / denominator).astype(jnp.bfloat16)
    mixed_heads = jnp.einsum(
        "bhqk,bkhe->bqhe", probs_low, value_heads, preferred_element_type=jnp.float32
    )
    mixed_heads = mixed_heads.astype(jnp.bfloat16).reshape(row_count, heads_here * head_size)
    attn_term = product(mixed_heads, w_out)
    hidden_one = residual_rows + lax.psum(attn_term.astype(jnp.bfloat16), "mp").astype(jnp.float32)
    normed_two, inverse_two = normalize(hidden_one)
    mlp_input = (normed_two * gain_mlp).astype(jnp.bfloat16)
    hidden_pre = product(mlp_input, w_up)
    activated = gelu_exact(hidden_pre).astype(jnp.bfloat16)
    mlp_out = lax.psum(product(activated, w_down).astype(jnp.bfloat16), "mp").astype(jnp.float32)
    block_rows = (hidden_one + mlp_out).astype(jnp.bfloat16)
    normed_learn, inverse_learn = normalize(block_rows.astype(jnp.float32))
    learn_input = (normed_learn * gain_learn).astype(jnp.bfloat16)
    learn_full = lax.all_gather(w_learn, "dp", axis=0, tiled=True)
    learn_pre = product(learn_input, learn_full)
    learn_act = gelu_exact(learn_pre).astype(jnp.bfloat16)
    logits = product(learn_act, w_select).reshape(images, patch_count, -1)
    logits = jnp.where(visible[:, :, None], logits, -1e30)
    top_logit = jnp.max(logits, axis=1, keepdims=True)
    exp_logit = jnp.exp(logits - top_logit)
    token_maps = exp_logit / jnp.sum(exp_logit, axis=1, keepdims=True)
    maps_low = token_maps.astype(jnp.bfloat16)
    block_three = block_rows.reshape(images, patch_count, feature_count)
    learned = jnp.einsum(
        "bpn,bpd->bnd", maps_low, block_three, preferred_element_type=jnp.float32
    ).astype(jnp.bfloat16)
    grad_maps = jnp.einsum(
        "bnd,bpd->bpn", cotangent, block_three, preferred_element_type=jnp.float32
    )
    grad_block = jnp.einsum(
        "bpn,bnd->bpd", maps_low, cotangent, preferred_element_type=jnp.float32
    ).reshape(row_count, feature_count)
    grad_logits = token_maps * (grad_maps - jnp.sum(token_maps * grad_maps, axis=1, keepdims=True))
    grad_logits = grad_logits.reshape(row_count, -1).astype(jnp.bfloat16)
    grad_select = contract_rows(learn_act, grad_logits)
    grad_learn_act = contract_cols(grad_logits, w_select)
    grad_learn_pre = gelu_back(learn_pre, grad_learn_act).astype(jnp.bfloat16)
    grad_learn = contract_rows(learn_input, grad_learn_pre)
    grad_learn_input = contract_cols(grad_learn_pre, learn_full)
    grad_from_learn, grad_gain_learn = norm_back(
        grad_learn_input, normed_learn, inverse_learn, gain_learn
    )
    grad_hidden = grad_block + grad_from_learn
    grad_hidden_low = grad_hidden.astype(jnp.bfloat16)
    grad_down = contract_rows(activated, grad_hidden_low)
    grad_act = contract_cols(grad_hidden_low, w_down)
    grad_pre = gelu_back(hidden_pre, grad_act).astype(jnp.bfloat16)
    grad_up = contract_rows(mlp_input, grad_pre)
    mlp_back_term = contract_cols(grad_pre, w_up)
    grad_mlp_input = lax.psum(mlp_back_term.astype(jnp.bfloat16), "mp").astype(jnp.float32)
    grad_from_two, grad_gain_mlp = norm_back(grad_mlp_input, normed_two, inverse_two, gain_mlp)
    grad_hidden = grad_hidden + grad_from_two
    grad_attn_low = grad_hidden.astype(jnp.bfloat16)
    grad_out = contract_rows(mixed_heads, grad_attn_low)
    grad_mixed = contract_cols(grad_attn_low, w_out).astype(jnp.bfloat16).reshape(head_shape)
    probs_again = jnp.exp(masked_scores() - logsum)
    probs_again_low = probs_again.astype(jnp.bfloat16)
    grad_probs = jnp.einsum(
        "bqhe,bkhe->bhqk", grad_mixed, value_heads, preferred_element_type=jnp.float32
    )
    grad_value_heads = jnp.einsum(
        "bhqk,bqhe->bkhe", probs_again_low, grad_mixed, preferred_element_type=jnp.float32
    ).astype(jnp.bfloat16)
    grad_scores = probs_again * (
        grad_probs - jnp.sum(probs_again * grad_probs, axis=-1, keepdims=True)
    )
    grad_scores = grad_scores.astype(jnp.bfloat16)
    grad_query_heads = (
        jnp.einsum("bhqk,bkhe->bqhe", grad_scores, key_heads, preferred_element_type=jnp.float32)
        * score_scale
    ).astype(jnp.bfloat16)
    grad_key_heads = (
        jnp.einsum("bhqk,bqhe->bkhe", grad_scores, query_heads, preferred_element_type=jnp.float32)
        * score_scale
    ).astype(jnp.bfloat16)
    grad_query_flat = grad_query_heads.reshape(row_count, -1)
    grad_key_flat = grad_key_heads.reshape(row_count, -1)
    grad_value_flat = grad_value_heads.reshape(row_count, -1)
    grad_query = contract_rows(attn_input, grad_query_flat)
    grad_key = contract_rows(attn_input, grad_key_flat)
    grad_value = contract_rows(attn_input, grad_value_flat)
    attn_terms = (
        contract_cols(grad_query_flat, w_query)
        + contract_cols(grad_key_flat, w_key)
        + contract_cols(grad_value_flat, w_value)
    )
    grad_attn_input = lax.psum(attn_terms.astype(jnp.bfloat16), "mp").astype(jnp.float32)
    grad_from_one, grad_gain_attn = norm_back(grad_attn_input, normed_one, inverse_one, gain_attn)
    grad_patches = (
        (grad_hidden + grad_from_one)
        .astype(jnp.bfloat16)
        .reshape(images, patch_count, feature_count)
    )
    (
        grad_query,
        grad_key,
        grad_value,
        grad_out,
        grad_gain_attn,
        grad_up,
        grad_down,
        grad_gain_mlp,
        grad_gain_learn,
        grad_select,
        grad_learn,
    ) = (
        lax.psum(grad_query.astype(jnp.bfloat16), "dp").astype(jnp.float32),
        lax.psum(grad_key.astype(jnp.bfloat16), "dp").astype(jnp.float32),
        lax.psum(grad_value.astype(jnp.bfloat16), "dp").astype(jnp.float32),
        lax.psum(grad_out.astype(jnp.bfloat16), "dp").astype(jnp.float32),
        lax.psum(grad_gain_attn.astype(jnp.bfloat16), "dp").astype(jnp.float32),
        lax.psum(grad_up.astype(jnp.bfloat16), "dp").astype(jnp.float32),
        lax.psum(grad_down.astype(jnp.bfloat16), "dp").astype(jnp.float32),
        lax.psum(grad_gain_mlp.astype(jnp.bfloat16), "dp").astype(jnp.float32),
        lax.psum(grad_gain_learn.astype(jnp.bfloat16), "dp").astype(jnp.float32),
        lax.psum(grad_select.astype(jnp.bfloat16), "dp").astype(jnp.float32),
        lax.psum(grad_learn.astype(jnp.bfloat16), "dp").astype(jnp.float32),
    )
    learn_rows = w_learn.shape[0]
    grad_learn = lax.dynamic_slice_in_dim(
        grad_learn, lax.axis_index("dp") * learn_rows, learn_rows, 0
    )
    return (
        learned,
        block_three,
        grad_patches,
        grad_query,
        grad_key,
        grad_value,
        grad_out,
        grad_up,
        grad_down,
        grad_gain_attn,
        grad_gain_mlp,
        grad_gain_learn,
        grad_learn,
        grad_select,
    )


MESH = pl.DeviceIdType.MESH
PAD = 208
CH = 16
TILE = 256
PAIR_IN = 224
LAG = 2
f32 = jnp.float32
bf16 = jnp.bfloat16


def nn(a, b):
    return jnp.dot(a, b, preferred_element_type=f32)


def nt(a, b):
    return lax.dot_general(a, b, (((1,), (1,)), ((), ())), preferred_element_type=f32)


def tn(a, b):
    return lax.dot_general(a, b, (((0,), (0,)), ((), ())), preferred_element_type=f32)


def gauss(z):
    bell = jnp.exp(-0.5 * (z * z))
    t = 1.0 / (1.0 + 0.23164189 * jnp.abs(z))
    poly = t * (
        0.127414796 + t * (-0.142248368 + t * (0.7107068705 + t * (-0.7265760135 + t * 0.5307027145)))
    )
    tail = poly * bell
    return jnp.where(z >= 0, 1.0 - tail, tail), 0.3989422804014327 * bell


def stats(v):
    mean = jnp.sum(v, axis=-1, keepdims=True) * (1.0 / v.shape[-1])
    c = v - mean
    s = lax.rsqrt(jnp.sum(c * c, axis=-1, keepdims=True) * (1.0 / v.shape[-1]) + 1e-06)
    return c * s, s


def back(e, u, s):
    width = 1.0 / e.shape[-1]
    return s * (
        e
        - jnp.sum(e, axis=-1, keepdims=True) * width
        - u * (jnp.sum(e * u, axis=-1, keepdims=True) * width)
    )


def fold(v):
    total = v[0:8]
    for r in range(8, v.shape[0], 8):
        total = total + v[r : r + 8]
    return total


def chunks():
    return range(0, PAD, CH)


def fused(
    patches, keep_ref, wq_hbm, wk_hbm, wv_hbm, wo_hbm, wup_hbm, wdn_hbm, g1_ref, g2_ref, g3_ref,
    wl_hbm, wsel_ref, ct_ref,
    learned_ref, y_hbm, gp_hbm, gall_hbm, small_ref, gl_ref,
    bias, wqkv, wo, wl,
    xs, qkv, os, h1s, a2s, dhs, d1s, big, recv,
    pbuf, rcore, rx, sumb, dg, gl_sum, gsel_sum, gl_mine, gl_in, small_mine, small_in,
    sx, sw, sy, slearn_s, slearn_r, s_core, r_core, s_x, r_x, s_ag, r_ag,
    s_pair, r_pair, s_out, ready_y, ready_z, s_small, r_small,
):
    images, count = keep_ref.shape
    width = patches.shape[1]
    half = width // 2
    dp = lax.axis_index("dp")
    mp = lax.axis_index("mp")
    core = lax.rem(mp, 2)
    mate = (dp, mp + 1 - 2 * core)
    across = (dp, lax.rem(mp + 2, 4))
    dps = lax.axis_size("dp")
    yy = lax.rem(dp, 2)
    zz = dp // 2
    middle = (zz == 1) | (zz == 2)
    zm = jnp.where(zz >= 2, 1, 0)
    mate_y = (dp + 1 - 2 * yy, mp)
    mate_e = ((zz + 1 - 2 * lax.rem(zz, 2)) * 2 + yy, mp)
    mate_m = ((3 - zz) * 2 + yy, mp)
    total = images * PAD
    pairs = 24
    kept = 8 * PAIR_IN
    rs = big.at[pl.ds(0, total)]
    wup = recv.at[pl.ds(kept, width)]
    wdn = recv.at[pl.ds(kept + width, width)]
    gs = recv.at[pl.ds(kept + 2 * width, total)]

    barrier = pltpu.get_barrier_semaphore()
    for device in (mate, across):
        pl.semaphore_signal(barrier, inc=1, device_id=device, device_id_type=MESH)
    for k in range(1, dps):
        pl.semaphore_signal(barrier, inc=1, device_id=(lax.rem(dp + k, dps), mp), device_id_type=MESH)

    def wl_part(d):
        return wl.at[:, pl.ds(pl.multiple_of(d * wl_hbm.shape[1], 128), wl_hbm.shape[1])]

    loads = [
        pltpu.make_async_copy(wq_hbm, wqkv.at[:, pl.ds(0, 256)], sw.at[0]),
        pltpu.make_async_copy(wk_hbm, wqkv.at[:, pl.ds(256, 256)], sw.at[1]),
        pltpu.make_async_copy(wv_hbm, wqkv.at[:, pl.ds(512, 256)], sw.at[2]),
        pltpu.make_async_copy(wo_hbm, wo, sw.at[3]),
        pltpu.make_async_copy(wup_hbm, wup, sw.at[4]),
        pltpu.make_async_copy(wdn_hbm, wdn, sw.at[5]),
        pltpu.make_async_copy(wl_hbm, wl_part(dp), sw.at[6]),
    ]

    load_x = pltpu.make_async_copy(patches, dhs.at[pl.ds(0, images * count)], sx)
    load_x.start()
    for k in (0, 1, 2, 3, 6, 4, 5):
        loads[k].start()

    xs[...] = jnp.zeros_like(xs)
    bias[...] = jnp.full(bias.shape, -1e30, f32)
    for i in range(images):
        bias[i, :, 0:count] = jnp.where(keep_ref[i : i + 1, :] > 0, 0.0, -1e30)

    pl.semaphore_wait(barrier, dps + 1)

    def learn_copy(k):
        return pltpu.make_async_remote_copy(
            src_ref=wl_part(dp), dst_ref=wl_part(dp),
            send_sem=slearn_s.at[k - 1], recv_sem=slearn_r.at[k - 1],
            device_id=(lax.rem(dp + k, dps), mp), device_id_type=MESH,
        )

    loads[6].wait()
    for k in range(1, dps):
        learn_copy(k).start()

    g1 = g1_ref[...]
    g2 = g2_ref[...]
    g3 = g3_ref[...]
    lane_head = lax.broadcasted_iota(jnp.int32, (1, 256), 1) // 64

    def only(v, h):
        return jnp.where(lane_head == h, v, jnp.zeros_like(v))

    def put_wide(where, value):
        for c in range(width // 128):
            h1s[c, where, :] = value[:, c * 128 : (c + 1) * 128]

    def get_wide(where):
        return jnp.concatenate([h1s[c, where, :] for c in range(width // 128)], axis=1)

    def rows_of(i):
        return pl.ds(pl.multiple_of(i * PAD, 16), PAD)

    def chunk_of(i, r):
        return pl.ds(pl.multiple_of(i * PAD + r, 16), CH)

    def copy_core(i):
        return pltpu.make_async_remote_copy(
            src_ref=pbuf.at[1 - core, rows_of(i)], dst_ref=rcore.at[rows_of(i)],
            send_sem=s_core.at[i], recv_sem=r_core.at[i], device_id=mate, device_id_type=MESH,
        )

    def copy_x(i, par):
        return pltpu.make_async_remote_copy(
            src_ref=pbuf.at[core, rows_of(i)], dst_ref=rx.at[par, rows_of(i)],
            send_sem=s_x.at[i], recv_sem=r_x.at[par, i], device_id=across, device_id_type=MESH,
        )

    def copy_ag(i):
        return pltpu.make_async_remote_copy(
            src_ref=sumb.at[core, rows_of(i)], dst_ref=sumb.at[core, rows_of(i)],
            send_sem=s_ag.at[i], recv_sem=r_ag.at[i], device_id=mate, device_id_type=MESH,
        )

    def hop_two(i, par):
        copy_core(i).wait()
        rows = rows_of(i)
        pbuf[core, rows] = (pbuf[core, rows].astype(f32) + rcore[rows].astype(f32)).astype(bf16)
        copy_x(i, par).start()

    def hop_three(i, par):
        copy_x(i, par).wait()
        rows = rows_of(i)
        sumb[core, rows] = (pbuf[core, rows].astype(f32) + rx[par, rows].astype(f32)).astype(bf16)
        copy_ag(i).start()

    def arrived(i):
        copy_ag(i).wait()

    def summed(i, r):
        where = chunk_of(i, r)
        return jnp.concatenate([sumb[0, where].astype(f32), sumb[1, where].astype(f32)], axis=1)

    def store_p(i, t, value):
        pbuf[t // 2, rows_of(i), (t % 2) * TILE : (t % 2 + 1) * TILE] = value.astype(bf16)

    def stage(body, lo, hi, second, before=None):
        def step(i, carry):
            if before is not None:
                before(i, hi)
            body(i)
            copy_core(i).start()

            @pl.when(i > lo)
            def _():
                second(i - 1)
            return carry

        lax.fori_loop(lo, hi, step, 0)
        second(hi - 1)

    def far(par):
        return lambda i: hop_two(i, par)

    def from_far(par):
        def before(i, hi):
            @pl.when(i + 1 < hi)
            def _():
                hop_three(i + 1, par)
            arrived(i)
        return before

    def each(body, lo, hi, before=None):
        def step(i, carry):
            if before is not None:
                before(i, hi)
            body(i)
            return carry

        lax.fori_loop(lo, hi, step, 0)

    def g_rows(k, lo, n):
        return pl.ds(pl.multiple_of(lax.rem(k * 128 + 2048, 3072) + lo, 16), n)

    def in_rows(k, lo, n):
        return pl.ds(pl.multiple_of(k * PAIR_IN + lo, 16), n)

    def send(k, slot, src, dst, device):
        return pltpu.make_async_remote_copy(
            src_ref=src, dst_ref=dst, send_sem=s_pair.at[slot, k], recv_sem=r_pair.at[slot, k],
            device_id=device, device_id_type=MESH,
        )

    def y_swap(k):
        return send(k, 0, big.at[g_rows(k, 32 - 32 * yy, 32)], recv.at[in_rows(k, 0, 32)], mate_y)

    def y_end(k):
        return send(k, 1, big.at[g_rows(k, 32 * yy, 32)], recv.at[in_rows(k, 32, 32)], mate_e)

    def y_mid(k):
        return send(k, 2, big.at[g_rows(k, 32 * yy, 32)], recv.at[in_rows(k, 64, 32)], mate_m)

    def o_rows(k, lo, n):
        return gall_hbm.at[pl.ds(pl.multiple_of(k * 128 + lo, 16), n)]

    def y_back(k):
        return send(k, 3, big.at[g_rows(k, 32 * yy, 32)], o_rows(k, 32 * yy, 32), mate_e)

    def y_share_mid(k):
        return send(k, 4, big.at[g_rows(k, 32 * yy, 32)], o_rows(k, 32 * yy, 32), mate_y)

    def y_share_end(k):
        return send(k, 4, o_rows(k, 32 * yy, 32), o_rows(k, 32 * yy, 32), mate_y)

    def z_end(k):
        return send(k, 5, big.at[g_rows(k, 64, 64)], recv.at[in_rows(k, 160, 64)], mate_e)

    def z_mid(k):
        return send(k, 6, big.at[g_rows(k, 96 - 32 * zm, 32)], recv.at[in_rows(k, 96, 32)], mate_m)

    def z_swap(k):
        return send(k, 7, big.at[g_rows(k, 64 + 32 * zm, 32)], recv.at[in_rows(k, 128, 32)], mate_y)

    def z_share(k):
        return send(k, 8, big.at[g_rows(k, 64 + 32 * zm, 32)], o_rows(k, 64 + 32 * zm, 32), mate_m)

    def z_back(k):
        return send(k, 9, big.at[g_rows(k, 64 + 32 * zm, 32)], o_rows(k, 64 + 32 * zm, 32), mate_e)

    def z_pass(k):
        return send(k, 10, o_rows(k, 96 - 32 * zm, 32), o_rows(k, 96 - 32 * zm, 32), mate_e)

    def accumulate(k, lo, n, at):
        rows = g_rows(k, lo, n)
        big[rows, :] = (big[rows, :].astype(f32) + recv[in_rows(k, at, n), :].astype(f32)).astype(bf16)

    def keep_y(k):
        return pltpu.make_async_copy(big.at[g_rows(k, 32 * yy, 32)], o_rows(k, 32 * yy, 32), s_out.at[0, k])

    def keep_z(k):
        return pltpu.make_async_copy(
            big.at[g_rows(k, 64 + 32 * zm, 32)], o_rows(k, 64 + 32 * zm, 32), s_out.at[1, k]
        )

    def hop0(k):
        y_swap(k).start()

        @pl.when(jnp.logical_not(middle))
        def _():
            z_end(k).start()

    def hop1(k):
        y_swap(k).wait()
        accumulate(k, 32 * yy, 32, 0)

        @pl.when(middle)
        def _():
            z_end(k).wait_recv()
            accumulate(k, 64, 64, 160)
            z_mid(k).start()

        @pl.when(jnp.logical_not(middle))
        def _():
            y_end(k).start()

    def hop2(k):
        @pl.when(middle)
        def _():
            y_end(k).wait_recv()
            accumulate(k, 32 * yy, 32, 32)
            y_mid(k).start()
            z_mid(k).wait()
            accumulate(k, 64 + 32 * zm, 32, 96)
            z_swap(k).start()

    def hop3(k):
        @pl.when(middle)
        def _():
            y_mid(k).wait()
            accumulate(k, 32 * yy, 32, 64)
            y_back(k).start()
            y_share_mid(k).start()
            keep_y(k).start()
            z_swap(k).wait()
            accumulate(k, 64 + 32 * zm, 32, 128)
            z_share(k).start()
            z_back(k).start()
            keep_z(k).start()

    def hop4(k):
        @pl.when(middle)
        def _():
            z_share(k).wait()
            z_pass(k).start()

        @pl.when(jnp.logical_not(middle))
        def _():
            y_end(k).wait_send()
            y_back(k).wait_recv()
            y_share_end(k).start()

    def hop5(k):
        @pl.when(middle)
        def _():
            y_share_mid(k).wait()
            y_back(k).wait_send()
            z_back(k).wait_send()
            z_pass(k).wait_send()
            keep_y(k).wait()
            keep_z(k).wait()

        @pl.when(jnp.logical_not(middle))
        def _():
            y_share_end(k).wait()
            z_end(k).wait_send()
            z_back(k).wait_recv()
            z_pass(k).wait_recv()

    def tick(t):
        for h, hop in ((5, hop5), (4, hop4), (3, hop3), (2, hop2), (1, hop1), (0, hop0)):
            k = t - LAG * h

            @pl.when((k >= 0) & (k < pairs))
            def _(hop=hop, k=k):
                hop(k)

    def ticks(lo, hi):
        def step(t, carry):
            tick(t)
            return carry

        lax.fori_loop(lo, hi, step, 0)

    load_x.wait()
    for r in range(0, images * count, 8 * CH):
        top = min(r + 8 * CH, images * count)
        put_wide(pl.ds(r, top - r), dhs[r:top, :].astype(f32))
    for k in (0, 1, 2, 3):
        loads[k].wait()

    def attend(q, k, v, row_bias):
        o = jnp.zeros((PAD, 256), f32)
        for h in range(4):
            scores = nt(only(q, h), k) + row_bias
            e = jnp.exp(scores - jnp.max(scores, axis=1, keepdims=True))
            p = (e * (1.0 / jnp.sum(e, axis=1, keepdims=True))).astype(bf16)
            o = o + nn(p, only(v, h))
        return o.astype(bf16)

    def attention(i):
        start = pl.multiple_of(i * PAD, 16)
        for c in range(width // 128):
            xs[pl.ds(start, count), c * 128 : (c + 1) * 128] = h1s[c, pl.ds(i, count, stride=images), :].astype(bf16)
        for r in chunks():
            u, _ = stats(xs[chunk_of(i, r), :].astype(f32))
            a2s[chunk_of(i, r), :] = (u * g1).astype(bf16)
        rows = rows_of(i)
        a1 = a2s[rows, :]
        qkv[rows, 0:256] = (nn(a1, wqkv[:, 0:256]) * 0.125).astype(bf16)
        qkv[rows, 256:512] = nn(a1, wqkv[:, 256:512]).astype(bf16)
        qkv[rows, 512:768] = nn(a1, wqkv[:, 512:768]).astype(bf16)
        os[rows, :] = attend(qkv[rows, 0:256], qkv[rows, 256:512], qkv[rows, 512:768], bias[i])

    def attention_sent(i):
        attention(i)
        ob = os[rows_of(i), :]
        for t in range(4):
            store_p(i, t, nn(ob, wo[:, t * TILE : (t + 1) * TILE]))

    stage(attention_sent, 0, images, far(0))

    loads[4].wait()
    loads[5].wait()

    def mlp(i):
        for r in chunks():
            h1 = xs[chunk_of(i, r), :].astype(f32) + summed(i, r)
            put_wide(chunk_of(i, r), h1)
            u, _ = stats(h1)
            a2s[chunk_of(i, r), :] = (u * g2).astype(bf16)
        rows = rows_of(i)
        a2 = a2s[rows, :]
        for t in range(4):
            cols = slice(t * TILE, (t + 1) * TILE)
            z = nn(a2, wup[:, cols])
            cdf, pdf = gauss(z)
            rs[rows, cols] = (z * cdf).astype(bf16)
            gs[rows, cols] = (cdf + z * pdf).astype(bf16)
        act = rs[rows, :]
        for t in range(4):
            store_p(i, t, nn(act, wdn[:, t * TILE : (t + 1) * TILE]))

    hop_three(0, 0)
    stage(mlp, 0, images, far(1), from_far(0))

    for k in range(1, dps):
        learn_copy(k).wait()
    dg[...] = jnp.zeros_like(dg)
    gl_sum[...] = jnp.zeros_like(gl_sum)
    gsel_sum[...] = jnp.zeros_like(gsel_sum)

    def y_out(i):
        return pltpu.make_async_copy(d1s.at[rows_of(i)], y_hbm.at[rows_of(i)], sy.at[i])

    def learner(i):
        rows = rows_of(i)
        for r in chunks():
            yb = (get_wide(chunk_of(i, r)) + summed(i, r)).astype(bf16)
            d1s[chunk_of(i, r), :] = yb
            u, _ = stats(yb.astype(f32))
            dhs[chunk_of(i, r), :] = (u * g3).astype(bf16)
        y_out(i).start()
        y = d1s[rows, :]
        a3 = dhs[rows, :]
        wlf = wl[...]
        wsel = wsel_ref[...]
        ct = ct_ref[i]
        zl = nt(a3, wlf)
        cdf, pdf = gauss(zl)
        t = (zl * cdf).astype(bf16)
        slope = cdf + zl * pdf
        eye = lax.broadcasted_iota(jnp.int32, (PAD, PAD), 0) == lax.broadcasted_iota(jnp.int32, (PAD, PAD), 1)
        col_bias = jnp.sum(jnp.where(eye, bias[i], 0.0), axis=1, keepdims=True)
        logits = nt(t, wsel) + col_bias
        e = jnp.exp(logits - jnp.max(logits, axis=0, keepdims=True))
        maps = e * (1.0 / jnp.sum(e, axis=0, keepdims=True))
        mb = maps.astype(bf16)
        learned_ref[i] = tn(mb, y).astype(bf16)
        dmaps = nt(y, ct)
        dlog = (maps * (dmaps - jnp.sum(maps * dmaps, axis=0, keepdims=True))).astype(bf16)
        gsel_sum[...] += tn(dlog, t)
        dzl = (nn(dlog, wsel) * slope).astype(bf16)
        gl_sum[...] += tn(dzl, a3)
        for r in chunks():
            da3 = nn(dzl[r : r + CH], wlf)
            dy = nn(mb[r : r + CH], ct)
            u, s = stats(d1s[chunk_of(i, r), :].astype(f32))
            dg[2] += fold(da3 * u)
            dhs[chunk_of(i, r), :] = (dy + back(da3 * g3, u, s)).astype(bf16)

    def mlp_back(i):
        rows = rows_of(i)
        dhb = dhs[rows, :]
        for c in range(4):
            cols = slice(c * TILE, (c + 1) * TILE)
            dr = nt(dhb, wdn[cols, :])
            gs[rows, cols] = (dr * gs[rows, cols].astype(f32)).astype(bf16)
        dz = gs[rows, :]
        for c in range(4):
            store_p(i, c, nt(dz, wup[c * TILE : (c + 1) * TILE, :]))

    def learner_mlp(i):
        learner(i)
        mlp_back(i)

    hop_three(0, 1)
    stage(learner_mlp, 0, images, far(0), from_far(1))

    def grad(left, right, first, tick0):
        def step(j, carry):
            lhs = left[:, pl.ds(pl.multiple_of(j * TILE, TILE), TILE)]
            rows = g_rows(2 * (first + j), 0, TILE)
            for c in range(0, width, TILE):
                big[rows, c : c + TILE] = tn(lhs, right[:, c : c + TILE]).astype(bf16)
            if tick0 is not None:
                tick(tick0 + j)
            return carry

        lax.fori_loop(0, left.shape[1] // TILE, step, 0)

    def ready():
        pl.semaphore_signal(ready_y, inc=1, device_id=mate_y, device_id_type=MESH)

        @pl.when(middle)
        def _():
            pl.semaphore_signal(ready_z, inc=1, device_id=mate_e, device_id_type=MESH)
            pl.semaphore_signal(ready_z, inc=1, device_id=mate_m, device_id_type=MESH)

    def both_ready():
        pl.semaphore_wait(ready_y, 1)
        pl.semaphore_wait(ready_z, 1)

    grad(rs, dhs, 0, 0)
    grad(a2s, gs, 4, 4)
    ready()
    for i in range(images):
        y_out(i).wait()

    def attention_back(i):
        rows = rows_of(i)
        for r in chunks():
            where = chunk_of(i, r)
            da2 = summed(i, r)
            u, s = stats(get_wide(where))
            dg[1] += fold(da2 * u)
            d1s[where, :] = (dhs[where, :].astype(f32) + back(da2 * g2, u, s)).astype(bf16)
            ux, _ = stats(xs[where, :].astype(f32))
            a2s[where, :] = (ux * g1).astype(bf16)
        d1 = d1s[rows, :]
        do = nt(d1, wo[...]).astype(bf16)
        q = qkv[rows, 0:256]
        k = qkv[rows, 256:512]
        v = qkv[rows, 512:768]
        eye = lax.broadcasted_iota(jnp.int32, (PAD, PAD), 0) == lax.broadcasted_iota(jnp.int32, (PAD, PAD), 1)
        col_bias = jnp.sum(jnp.where(eye, bias[i], 0.0), axis=1, keepdims=True)
        dq = jnp.zeros((PAD, 256), f32)
        dk = jnp.zeros((PAD, 256), f32)
        dv = jnp.zeros((PAD, 256), f32)
        for h in range(4):
            kh = only(k, h)
            scores = nt(kh, q) + col_bias
            e = jnp.exp(scores - jnp.max(scores, axis=0, keepdims=True))
            p = e * (1.0 / jnp.sum(e, axis=0, keepdims=True))
            dv = dv + nn(p.astype(bf16), only(do, h))
            dpr = nt(only(v, h), do)
            ds = (p * (dpr - jnp.sum(p * dpr, axis=0, keepdims=True))).astype(bf16)
            dk = dk + nn(ds, only(q, h))
            dq = dq + tn(ds, kh)
        qkv[rows, 0:256] = (dq * 0.125).astype(bf16)
        qkv[rows, 256:512] = dk.astype(bf16)
        qkv[rows, 512:768] = dv.astype(bf16)
        dall = qkv[rows, :]
        for c in range(4):
            store_p(i, c, nt(dall, wqkv[c * TILE : (c + 1) * TILE, :]))
        tick(8 + i)

    hop_three(0, 0)
    both_ready()
    stage(attention_back, 0, images, far(1), from_far(0))
    grad(os, d1s, 8, 16)

    def grad_qkv(j, carry):
        lhs = a2s[:, pl.ds(pl.multiple_of(j * TILE, TILE), TILE)]
        for n in range(3):
            value = tn(lhs, qkv[:, n * TILE : (n + 1) * TILE]).astype(bf16)
            rows = pl.ds(pl.multiple_of(1280 + j * 192 + n * 64, 16), 64)
            for c in range(4):
                big[rows, c * TILE : (c + 1) * TILE] = value[c * 64 : (c + 1) * 64]
        tick(17 + j)
        return carry

    lax.fori_loop(0, 4, grad_qkv, 0)

    def gp_out(i):
        return pltpu.make_async_copy(dhs.at[rows_of(i)], gp_hbm.at[rows_of(i)], sy.at[i])

    def finish(i, carry):
        @pl.when(i + 1 < images)
        def _():
            hop_three(i + 1, 1)
        arrived(i)
        for r in chunks():
            where = chunk_of(i, r)
            da1 = summed(i, r)
            u, s = stats(xs[where, :].astype(f32))
            dg[0] += fold(da1 * u)
            dhs[where, :] = (d1s[where, :].astype(f32) + back(da1 * g1, u, s)).astype(bf16)
        gp_out(i).start()
        tick(21 + i)
        return carry

    hop_three(0, 1)
    lax.fori_loop(0, images, finish, 0)

    small_mine[0:8, :] = jnp.concatenate(
        [jnp.sum(dg[n], axis=0, keepdims=True) for n in range(3)] + [jnp.zeros((5, width), f32)], axis=0
    ).astype(bf16)
    small_mine[8:16, 0:64] = gsel_sum[...].astype(bf16)
    small_mine[8:16, 64:width] = jnp.zeros((8, width - 64), bf16)
    gl_mine[...] = gl_sum[...].astype(bf16)
    part = wl_hbm.shape[1]

    def gl_part(d):
        return pl.ds(pl.multiple_of(d * part, 128), part)

    def small_copy(k):
        peer = lax.rem(dp + k, dps)
        return (
            pltpu.make_async_remote_copy(
                src_ref=small_mine, dst_ref=small_in.at[k - 1], send_sem=s_small.at[0, k - 1],
                recv_sem=r_small.at[0, k - 1], device_id=(peer, mp), device_id_type=MESH,
            ),
            pltpu.make_async_remote_copy(
                src_ref=gl_mine.at[:, gl_part(peer)], dst_ref=gl_in.at[k - 1], send_sem=s_small.at[1, k - 1],
                recv_sem=r_small.at[1, k - 1], device_id=(peer, mp), device_id_type=MESH,
            ),
        )

    for k in range(1, dps):
        for copy in small_copy(k):
            copy.start()
    ticks(29, pairs + 5 * LAG)
    for k in range(1, dps):
        for copy in small_copy(k):
            copy.wait()
    small_ref[...] = small_mine[...].astype(f32)
    gl_ref[...] = gl_mine[:, gl_part(dp)].astype(f32)
    for k in range(dps - 1):
        small_ref[...] += small_in[k].astype(f32)
        gl_ref[...] += gl_in[k].astype(f32)
    for i in range(images):
        gp_out(i).wait()


def finish_up(
    gall, y, gp, learned, small, gl,
    learned_ref, y_ref, gp_ref, gq_ref, gk_ref, gv_ref, gout_ref, gup_ref, gdn_ref, d1_ref, d2_ref, d3_ref,
    gl_ref, gsel_ref,
    tiles, y_in, gp_in, wide, square, y_turned, gp_turned, strip, s_tile, s_in, s_wide, s_square, s_turned,
):
    count = y_ref.shape[0]

    def tile_in(j):
        rows = pl.ds(j * TILE, TILE)
        return pltpu.make_async_copy(gall.at[rows], tiles.at[rows], s_tile.at[j])

    ins = [pltpu.make_async_copy(y, y_in, s_in.at[0]), pltpu.make_async_copy(gp, gp_in, s_in.at[1])]
    for j in range(4):
        tile_in(j).start()
    for copy in ins:
        copy.start()
    for j in range(4, 12):
        tile_in(j).start()
    outs = []

    def tile_out(j):
        tile_in(j).wait()
        rows = slice(j * TILE, (j + 1) * TILE)
        wide[rows, :] = tiles[rows, :].astype(f32)
        ref, first = ((gdn_ref, 0), (gup_ref, 4), (gout_ref, 8))[j // 4]
        copy = pltpu.make_async_copy(
            wide.at[pl.ds(j * TILE, TILE)], ref.at[pl.ds((j - first) * TILE, TILE)], s_wide.at[j]
        )
        copy.start()
        outs.append(copy)

    def turn(n, src, dst, ref):
        ins[n].wait()
        for block in range(0, count, CH):
            rows = min(CH, count - block)
            for c in range(src.shape[2] // 128):
                cols = slice(c * 128, (c + 1) * 128)
                slot = strip.at[c]
                slot[...] = src[:, block : block + CH, cols].astype(f32).reshape(slot.shape)
                for r in range(rows):
                    dst[block + r, :, cols] = slot[pl.ds(r, dst.shape[1], stride=CH), :].astype(bf16)
            copy = pltpu.make_async_copy(
                dst.at[pl.ds(block, rows)], ref.at[pl.ds(block, rows)], s_turned.at[n, block // CH]
            )
            copy.start()
            outs.append(copy)

    for j in range(4):
        tile_out(j)
    turn(0, y_in, y_turned, y_ref)
    for j in range(4, 9):
        tile_out(j)
    turn(1, gp_in, gp_turned, gp_ref)
    for j in range(9, 12):
        tile_in(j).wait()
    for n, ref in enumerate((gq_ref, gk_ref, gv_ref)):
        for j in range(4):
            for c in range(4):
                square[n, j * TILE + c * 64 : j * TILE + (c + 1) * 64, :] = tiles[
                    9 * TILE + j * 192 + n * 64 : 9 * TILE + j * 192 + (n + 1) * 64, c * TILE : (c + 1) * TILE
                ].astype(f32)
        copy = pltpu.make_async_copy(square.at[n], ref, s_square.at[n])
        copy.start()
        outs.append(copy)
    learned_ref[...] = learned[...]
    for n, ref in enumerate((d1_ref, d2_ref, d3_ref)):
        ref[...] = small[n : n + 1, :]
    gl_ref[...] = gl[...]
    gsel_ref[...] = small[8:16, 0 : gsel_ref.shape[1]]
    for copy in outs:
        copy.wait()


def local_fused(
    patches, keep_mask, w_query, w_key, w_value, w_out, w_up, w_down,
    gain_attn, gain_mlp, gain_learn, w_learn, w_select, cotangent,
):
    images, count, width = patches.shape
    total = images * PAD
    hidden = w_up.shape[1]
    learn_rows, learn_cols = w_learn.shape
    dps = lax.axis_size("dp")
    anywhere = pl.BlockSpec(memory_space=pl.ANY)
    vmem = pl.BlockSpec(memory_space=pltpu.VMEM)
    sds = jax.ShapeDtypeStruct
    dma = pltpu.SemaphoreType.DMA
    outs = pl.pallas_call(
        fused,
        name="block",
        out_shape=(
            sds((images, 8, width), bf16),
            sds((total, width), bf16),
            sds((total, width), bf16),
            sds((3072, width), bf16),
            sds((16, width), f32),
            sds((learn_cols, learn_rows), f32),
        ),
        in_specs=[anywhere, vmem] + [anywhere] * 6 + [vmem] * 3 + [anywhere] + [vmem] * 2,
        out_specs=(vmem,) + (anywhere,) * 3 + (vmem,) * 2,
        scratch_shapes=[
            pltpu.VMEM((images, 1, PAD), f32),
            pltpu.VMEM((width, 768), bf16),
            pltpu.VMEM((256, width), bf16),
            pltpu.VMEM((learn_cols, width), bf16),
            pltpu.VMEM((total, width), bf16),
            pltpu.VMEM((total, 768), bf16),
            pltpu.VMEM((total, 256), bf16),
            pltpu.VMEM((width // 128, total, 128), f32),
            pltpu.VMEM((total, width), bf16),
            pltpu.VMEM((total, width), bf16),
            pltpu.VMEM((total, width), bf16),
            pltpu.VMEM((3072, width), bf16),
            pltpu.VMEM((8 * PAIR_IN + total + 2 * width, width), bf16),
            pltpu.VMEM((2, total, width // 2), bf16),
            pltpu.VMEM((total, width // 2), bf16),
            pltpu.VMEM((2, total, width // 2), bf16),
            pltpu.VMEM((2, total, width // 2), bf16),
            pltpu.VMEM((3, 8, width), f32),
            pltpu.VMEM((learn_cols, width), f32),
            pltpu.VMEM((8, learn_cols), f32),
            pltpu.VMEM((learn_cols, width), bf16),
            pltpu.VMEM((dps - 1, learn_cols, learn_rows), bf16),
            pltpu.VMEM((16, width), bf16),
            pltpu.VMEM((dps - 1, 16, width), bf16),
            dma(()), dma((7,)), dma((images,)), dma((dps - 1,)), dma((dps - 1,)),
            dma((images,)), dma((images,)), dma((images,)), dma((2, images)), dma((images,)), dma((images,)),
            dma((11, 24)), dma((11, 24)), dma((2, 24)),
            pltpu.SemaphoreType.REGULAR, pltpu.SemaphoreType.REGULAR, dma((2, dps - 1)), dma((2, dps - 1)),
        ],
        compiler_params=pltpu.CompilerParams(
            collective_id=0, has_side_effects=True, vmem_limit_bytes=60 * 2**20
        ),
    )(
        patches.transpose(1, 0, 2).reshape(count * images, width), keep_mask, w_query, w_key, w_value, w_out, w_up, w_down,
        gain_attn[None], gain_mlp[None], gain_learn[None], w_learn.T, w_select.T, cotangent,
    )
    learned, y, gpat, gall, small, gl = outs

    square = (width, TILE)
    row = (1, width)
    blocks = -(-count // CH)
    outs = pl.pallas_call(
        finish_up,
        name="finish",
        out_shape=(
            sds((images, 8, width), bf16), sds((count, images, width), bf16), sds((count, images, width), bf16),
            sds(square, f32), sds(square, f32), sds(square, f32),
            sds((TILE, width), f32), sds((width, hidden), f32), sds((hidden, width), f32),
            sds(row, f32), sds(row, f32), sds(row, f32),
            sds((learn_cols, learn_rows), f32), sds((8, learn_cols), f32),
        ),
        in_specs=[anywhere] * 3 + [vmem] * 3,
        out_specs=(vmem,) + (anywhere,) * 8 + (vmem,) * 5,
        scratch_shapes=[
            pltpu.VMEM((3072, width), bf16),
            pltpu.VMEM((images, PAD, width), bf16),
            pltpu.VMEM((images, PAD, width), bf16),
            pltpu.VMEM((9 * TILE, width), f32),
            pltpu.VMEM((3,) + square, f32),
            pltpu.VMEM((count, images, width), bf16),
            pltpu.VMEM((count, images, width), bf16),
            pltpu.VMEM((width // 128, images * CH, 128), f32),
            dma((12,)), dma((2,)), dma((9,)), dma((3,)), dma((2, blocks)),
        ],
        compiler_params=pltpu.CompilerParams(vmem_limit_bytes=60 * 2**20),
    )(gall, y.reshape(images, PAD, width), gpat.reshape(images, PAD, width), learned, small, gl)
    learned, y, gpat, gq, gk, gv, gout, gup, gdn, d1, d2, d3, gl, gsel = outs
    return (
        learned, y.transpose(1, 0, 2), gpat.transpose(1, 0, 2), gq, gk, gv, gout, gup, gdn,
        d1[0], d2[0], d3[0], gl.T, gsel.T,
    )


def solution(mesh):
    small = mesh.shape["dp"] == 8 and mesh.shape["mp"] == 4
    return jax.shard_map(
        local_fused if small else local,
        mesh=mesh,
        in_specs=(
            P("dp", None, None),
            P("dp", None),
            P(None, "mp"),
            P(None, "mp"),
            P(None, "mp"),
            P("mp", None),
            P(None, "mp"),
            P("mp", None),
            P(),
            P(),
            P(),
            P("dp", None),
            P(),
            P("dp", None, None),
        ),
        out_specs=(
            P("dp", None, None),
            P("dp", None, None),
            P("dp", None, None),
            P(None, "mp"),
            P(None, "mp"),
            P(None, "mp"),
            P("mp", None),
            P(None, "mp"),
            P("mp", None),
            P(),
            P(),
            P(),
            P("dp", None),
            P(),
        ),
        check_vma=False,
    )
```

```python
import math

import jax
import jax.numpy as jnp
from jax import lax
from jax.experimental import pallas as pl
from jax.experimental.pallas import tpu as pltpu
from jax.sharding import PartitionSpec as P

D = 1024
HEADS = 16


def product(left, right):
    return jnp.dot(left, right, preferred_element_type=jnp.float32)


def contract_rows(left, right):
    return lax.dot_general(
        left, right, (((0,), (0,)), ((), ())), preferred_element_type=jnp.float32
    )


def contract_cols(left, right):
    return lax.dot_general(
        left, right, (((1,), (1,)), ((), ())), preferred_element_type=jnp.float32
    )


def normalize(inputs):
    row_mean = jnp.mean(inputs, axis=-1, keepdims=True)
    centered = inputs - row_mean
    inverse = lax.rsqrt(jnp.mean(centered * centered, axis=-1, keepdims=True) + 1e-06)
    return (centered * inverse, inverse)


def norm_back(grad_norm, normed, inverse, gain):
    scaled_grad = grad_norm * gain
    grad_input = inverse * (
        scaled_grad
        - jnp.mean(scaled_grad, axis=-1, keepdims=True)
        - normed * jnp.mean(scaled_grad * normed, axis=-1, keepdims=True)
    )
    return (grad_input, jnp.sum(grad_norm * normed, axis=0))


def gelu_exact(inputs):
    return jax.nn.gelu(inputs, approximate=False)


def gelu_back(hidden_pre, grad_act):
    _, pullback = jax.vjp(gelu_exact, hidden_pre)
    return pullback(grad_act)[0]


def local(
    patches,
    keep_mask,
    w_query,
    w_key,
    w_value,
    w_out,
    w_up,
    w_down,
    gain_attn,
    gain_mlp,
    gain_learn,
    w_learn,
    w_select,
    cotangent,
):
    images, patch_count, feature_count = patches.shape
    row_count = images * patch_count
    head_size = D // HEADS
    heads_here = w_query.shape[1] // head_size
    score_scale = 1.0 / math.sqrt(head_size)
    visible = keep_mask > 0
    head_shape = (images, patch_count, heads_here, head_size)
    residual_rows = patches.reshape(row_count, feature_count).astype(jnp.float32)
    normed_one, inverse_one = normalize(residual_rows)
    attn_input = (normed_one * gain_attn).astype(jnp.bfloat16)
    query_flat = product(attn_input, w_query).astype(jnp.bfloat16)
    key_flat = product(attn_input, w_key).astype(jnp.bfloat16)
    value_flat = product(attn_input, w_value).astype(jnp.bfloat16)
    query_heads = query_flat.reshape(head_shape)
    key_heads = key_flat.reshape(head_shape)
    value_heads = value_flat.reshape(head_shape)

    def masked_scores():
        raw_scores = (
            jnp.einsum(
                "bqhe,bkhe->bhqk", query_heads, key_heads, preferred_element_type=jnp.float32
            )
            * score_scale
        )
        return jnp.where(visible[:, None, None, :], raw_scores, -1e30)

    scores = masked_scores()
    top_score = jnp.max(scores, axis=-1, keepdims=True)
    exponent = jnp.exp(scores - top_score)
    denominator = jnp.sum(exponent, axis=-1, keepdims=True)
    logsum = top_score + jnp.log(denominator)
    probs_low = (exponent / denominator).astype(jnp.bfloat16)
    mixed_heads = jnp.einsum(
        "bhqk,bkhe->bqhe", probs_low, value_heads, preferred_element_type=jnp.float32
    )
    mixed_heads = mixed_heads.astype(jnp.bfloat16).reshape(row_count, heads_here * head_size)
    attn_term = product(mixed_heads, w_out)
    hidden_one = residual_rows + lax.psum(attn_term.astype(jnp.bfloat16), "mp").astype(jnp.float32)
    normed_two, inverse_two = normalize(hidden_one)
    mlp_input = (normed_two * gain_mlp).astype(jnp.bfloat16)
    hidden_pre = product(mlp_input, w_up)
    activated = gelu_exact(hidden_pre).astype(jnp.bfloat16)
    mlp_out = lax.psum(product(activated, w_down).astype(jnp.bfloat16), "mp").astype(jnp.float32)
    block_rows = (hidden_one + mlp_out).astype(jnp.bfloat16)
    normed_learn, inverse_learn = normalize(block_rows.astype(jnp.float32))
    learn_input = (normed_learn * gain_learn).astype(jnp.bfloat16)
    learn_full = lax.all_gather(w_learn, "dp", axis=0, tiled=True)
    learn_pre = product(learn_input, learn_full)
    learn_act = gelu_exact(learn_pre).astype(jnp.bfloat16)
    logits = product(learn_act, w_select).reshape(images, patch_count, -1)
    logits = jnp.where(visible[:, :, None], logits, -1e30)
    top_logit = jnp.max(logits, axis=1, keepdims=True)
    exp_logit = jnp.exp(logits - top_logit)
    token_maps = exp_logit / jnp.sum(exp_logit, axis=1, keepdims=True)
    maps_low = token_maps.astype(jnp.bfloat16)
    block_three = block_rows.reshape(images, patch_count, feature_count)
    learned = jnp.einsum(
        "bpn,bpd->bnd", maps_low, block_three, preferred_element_type=jnp.float32
    ).astype(jnp.bfloat16)
    grad_maps = jnp.einsum(
        "bnd,bpd->bpn", cotangent, block_three, preferred_element_type=jnp.float32
    )
    grad_block = jnp.einsum(
        "bpn,bnd->bpd", maps_low, cotangent, preferred_element_type=jnp.float32
    ).reshape(row_count, feature_count)
    grad_logits = token_maps * (grad_maps - jnp.sum(token_maps * grad_maps, axis=1, keepdims=True))
    grad_logits = grad_logits.reshape(row_count, -1).astype(jnp.bfloat16)
    grad_select = contract_rows(learn_act, grad_logits)
    grad_learn_act = contract_cols(grad_logits, w_select)
    grad_learn_pre = gelu_back(learn_pre, grad_learn_act).astype(jnp.bfloat16)
    grad_learn = contract_rows(learn_input, grad_learn_pre)
    grad_learn_input = contract_cols(grad_learn_pre, learn_full)
    grad_from_learn, grad_gain_learn = norm_back(
        grad_learn_input, normed_learn, inverse_learn, gain_learn
    )
    grad_hidden = grad_block + grad_from_learn
    grad_hidden_low = grad_hidden.astype(jnp.bfloat16)
    grad_down = contract_rows(activated, grad_hidden_low)
    grad_act = contract_cols(grad_hidden_low, w_down)
    grad_pre = gelu_back(hidden_pre, grad_act).astype(jnp.bfloat16)
    grad_up = contract_rows(mlp_input, grad_pre)
    mlp_back_term = contract_cols(grad_pre, w_up)
    grad_mlp_input = lax.psum(mlp_back_term.astype(jnp.bfloat16), "mp").astype(jnp.float32)
    grad_from_two, grad_gain_mlp = norm_back(grad_mlp_input, normed_two, inverse_two, gain_mlp)
    grad_hidden = grad_hidden + grad_from_two
    grad_attn_low = grad_hidden.astype(jnp.bfloat16)
    grad_out = contract_rows(mixed_heads, grad_attn_low)
    grad_mixed = contract_cols(grad_attn_low, w_out).astype(jnp.bfloat16).reshape(head_shape)
    probs_again = jnp.exp(masked_scores() - logsum)
    probs_again_low = probs_again.astype(jnp.bfloat16)
    grad_probs = jnp.einsum(
        "bqhe,bkhe->bhqk", grad_mixed, value_heads, preferred_element_type=jnp.float32
    )
    grad_value_heads = jnp.einsum(
        "bhqk,bqhe->bkhe", probs_again_low, grad_mixed, preferred_element_type=jnp.float32
    ).astype(jnp.bfloat16)
    grad_scores = probs_again * (
        grad_probs - jnp.sum(probs_again * grad_probs, axis=-1, keepdims=True)
    )
    grad_scores = grad_scores.astype(jnp.bfloat16)
    grad_query_heads = (
        jnp.einsum("bhqk,bkhe->bqhe", grad_scores, key_heads, preferred_element_type=jnp.float32)
        * score_scale
    ).astype(jnp.bfloat16)
    grad_key_heads = (
        jnp.einsum("bhqk,bqhe->bkhe", grad_scores, query_heads, preferred_element_type=jnp.float32)
        * score_scale
    ).astype(jnp.bfloat16)
    grad_query_flat = grad_query_heads.reshape(row_count, -1)
    grad_key_flat = grad_key_heads.reshape(row_count, -1)
    grad_value_flat = grad_value_heads.reshape(row_count, -1)
    grad_query = contract_rows(attn_input, grad_query_flat)
    grad_key = contract_rows(attn_input, grad_key_flat)
    grad_value = contract_rows(attn_input, grad_value_flat)
    attn_terms = (
        contract_cols(grad_query_flat, w_query)
        + contract_cols(grad_key_flat, w_key)
        + contract_cols(grad_value_flat, w_value)
    )
    grad_attn_input = lax.psum(attn_terms.astype(jnp.bfloat16), "mp").astype(jnp.float32)
    grad_from_one, grad_gain_attn = norm_back(grad_attn_input, normed_one, inverse_one, gain_attn)
    grad_patches = (
        (grad_hidden + grad_from_one)
        .astype(jnp.bfloat16)
        .reshape(images, patch_count, feature_count)
    )
    (
        grad_query,
        grad_key,
        grad_value,
        grad_out,
        grad_gain_attn,
        grad_up,
        grad_down,
        grad_gain_mlp,
        grad_gain_learn,
        grad_select,
        grad_learn,
    ) = (
        lax.psum(grad_query.astype(jnp.bfloat16), "dp").astype(jnp.float32),
        lax.psum(grad_key.astype(jnp.bfloat16), "dp").astype(jnp.float32),
        lax.psum(grad_value.astype(jnp.bfloat16), "dp").astype(jnp.float32),
        lax.psum(grad_out.astype(jnp.bfloat16), "dp").astype(jnp.float32),
        lax.psum(grad_gain_attn.astype(jnp.bfloat16), "dp").astype(jnp.float32),
        lax.psum(grad_up.astype(jnp.bfloat16), "dp").astype(jnp.float32),
        lax.psum(grad_down.astype(jnp.bfloat16), "dp").astype(jnp.float32),
        lax.psum(grad_gain_mlp.astype(jnp.bfloat16), "dp").astype(jnp.float32),
        lax.psum(grad_gain_learn.astype(jnp.bfloat16), "dp").astype(jnp.float32),
        lax.psum(grad_select.astype(jnp.bfloat16), "dp").astype(jnp.float32),
        lax.psum(grad_learn.astype(jnp.bfloat16), "dp").astype(jnp.float32),
    )
    learn_rows = w_learn.shape[0]
    grad_learn = lax.dynamic_slice_in_dim(
        grad_learn, lax.axis_index("dp") * learn_rows, learn_rows, 0
    )
    return (
        learned,
        block_three,
        grad_patches,
        grad_query,
        grad_key,
        grad_value,
        grad_out,
        grad_up,
        grad_down,
        grad_gain_attn,
        grad_gain_mlp,
        grad_gain_learn,
        grad_learn,
        grad_select,
    )


MESH = pl.DeviceIdType.MESH
PAD = 208
CH = 16
TILE = 256
PAIR_IN = 224
LAG = 2
LAG_END = 2
f32 = jnp.float32
bf16 = jnp.bfloat16


def nn(a, b):
    return jnp.dot(a, b, preferred_element_type=f32)


def nt(a, b):
    return lax.dot_general(a, b, (((1,), (1,)), ((), ())), preferred_element_type=f32)


def tn(a, b):
    return lax.dot_general(a, b, (((0,), (0,)), ((), ())), preferred_element_type=f32)


def gauss(z):
    bell = jnp.exp(-0.5 * (z * z))
    t = 1.0 / (1.0 + 0.23164189 * jnp.abs(z))
    poly = t * (
        0.127414796 + t * (-0.142248368 + t * (0.7107068705 + t * (-0.7265760135 + t * 0.5307027145)))
    )
    tail = poly * bell
    return jnp.where(z >= 0, 1.0 - tail, tail), 0.3989422804014327 * bell


def stats(v):
    mean = jnp.sum(v, axis=-1, keepdims=True) * (1.0 / v.shape[-1])
    c = v - mean
    s = lax.rsqrt(jnp.sum(c * c, axis=-1, keepdims=True) * (1.0 / v.shape[-1]) + 1e-06)
    return c * s, s


def back(e, u, s):
    width = 1.0 / e.shape[-1]
    return s * (
        e
        - jnp.sum(e, axis=-1, keepdims=True) * width
        - u * (jnp.sum(e * u, axis=-1, keepdims=True) * width)
    )


def fold(v):
    total = v[0:8]
    for r in range(8, v.shape[0], 8):
        total = total + v[r : r + 8]
    return total


def chunks():
    return range(0, PAD, CH)


def fused(
    patches, keep_ref, wq_hbm, wk_hbm, wv_hbm, wo_hbm, wup_hbm, wdn_hbm, g1_ref, g2_ref, g3_ref,
    wl_hbm, wsel_ref, ct_ref,
    learned_ref, y_hbm, gp_hbm, gall_hbm, small_ref, gl_ref,
    bias, wqkv, wo, wl,
    xs, qkv, os, h1s, a2s, dhs, d1s, big, recv,
    pbuf, rcore, rx, sumb, dg, gl_sum, gsel_sum, gl_mine, gl_in, small_mine, small_in, col, centre, scale, part_a, part_b,
    sx, sw, sy, slearn_s, slearn_r, s_core, r_core, s_x, r_x, s_ag, r_ag,
    s_pair, r_pair, s_out, ready_y, ready_z, s_small, r_small,
):
    images, count = keep_ref.shape
    width = patches.shape[1]
    half = width // 2
    dp = lax.axis_index("dp")
    mp = lax.axis_index("mp")
    core = lax.rem(mp, 2)
    mate = (dp, mp + 1 - 2 * core)
    across = (dp, lax.rem(mp + 2, 4))
    dps = lax.axis_size("dp")
    yy = lax.rem(dp, 2)
    zz = dp // 2
    middle = (zz == 1) | (zz == 2)
    zm = jnp.where(zz >= 2, 1, 0)
    mate_y = (dp + 1 - 2 * yy, mp)
    mate_e = ((zz + 1 - 2 * lax.rem(zz, 2)) * 2 + yy, mp)
    mate_m = ((3 - zz) * 2 + yy, mp)
    total = images * PAD
    pairs = 24
    kept = 8 * PAIR_IN
    rs = big.at[pl.ds(0, total)]
    wup = recv.at[pl.ds(kept, width)]
    wdn = recv.at[pl.ds(kept + width, width)]
    gs = recv.at[pl.ds(kept + 2 * width, total)]

    barrier = pltpu.get_barrier_semaphore()
    for device in (mate, across):
        pl.semaphore_signal(barrier, inc=1, device_id=device, device_id_type=MESH)
    for k in range(1, dps):
        pl.semaphore_signal(barrier, inc=1, device_id=(lax.rem(dp + k, dps), mp), device_id_type=MESH)

    def wl_part(d):
        return wl.at[:, pl.ds(pl.multiple_of(d * wl_hbm.shape[1], 128), wl_hbm.shape[1])]

    loads = [
        pltpu.make_async_copy(wq_hbm, wqkv.at[:, pl.ds(0, 256)], sw.at[0]),
        pltpu.make_async_copy(wk_hbm, wqkv.at[:, pl.ds(256, 256)], sw.at[1]),
        pltpu.make_async_copy(wv_hbm, wqkv.at[:, pl.ds(512, 256)], sw.at[2]),
        pltpu.make_async_copy(wo_hbm, wo, sw.at[3]),
        pltpu.make_async_copy(wup_hbm, wup, sw.at[4]),
        pltpu.make_async_copy(wdn_hbm, wdn, sw.at[5]),
        pltpu.make_async_copy(wl_hbm, wl_part(dp), sw.at[6]),
    ]

    load_x = [
        pltpu.make_async_copy(
            patches.at[:, pl.ds(c * TILE, TILE)], dhs.at[pl.ds(0, images * count), pl.ds(c * TILE, TILE)], sx.at[c]
        )
        for c in range(4)
    ]
    for copy in load_x:
        copy.start()
    for k in (0, 1, 2, 3, 6):
        loads[k].start()

    for i in range(images):
        xs[i * PAD + PAD - 16 : (i + 1) * PAD, :] = jnp.zeros((16, width), bf16)
    bias[...] = jnp.full(bias.shape, -1e30, f32)
    for i in range(images):
        bias[i, :, 0:count] = jnp.where(keep_ref[i : i + 1, :] > 0, 0.0, -1e30)
    turned = jnp.transpose(bias[...].reshape(images, PAD))
    for i in range(images):
        col[i * PAD : (i + 1) * PAD, :] = turned[:, i : i + 1]
    for c in range(4):
        load_x[c].wait()
        for r in range(0, images * count, 8 * CH):
            top = min(r + 8 * CH, images * count)
            for n in (2 * c, 2 * c + 1):
                h1s[n, r:top, :] = dhs[r:top, n * 128 : (n + 1) * 128].astype(f32)

    g1 = g1_ref[...]
    g2 = g2_ref[...]
    g3 = g3_ref[...]
    lane_head = lax.broadcasted_iota(jnp.int32, (1, 256), 1) // 64

    def only(v, h):
        return jnp.where(lane_head == h, v, jnp.zeros_like(v))

    def put_wide(where, value):
        for c in range(width // 128):
            h1s[c, where, :] = value[:, c * 128 : (c + 1) * 128]

    def get_wide(where):
        return jnp.concatenate([h1s[c, where, :] for c in range(width // 128)], axis=1)

    def rows_of(i):
        return pl.ds(pl.multiple_of(i * PAD, 16), PAD)

    def chunk_of(i, r):
        return pl.ds(pl.multiple_of(i * PAD + r, 16), CH)

    def copy_core(i):
        return pltpu.make_async_remote_copy(
            src_ref=pbuf.at[1 - core, rows_of(i)], dst_ref=rcore.at[rows_of(i)],
            send_sem=s_core.at[i], recv_sem=r_core.at[i], device_id=mate, device_id_type=MESH,
        )

    def copy_x(i, par):
        return pltpu.make_async_remote_copy(
            src_ref=pbuf.at[core, rows_of(i)], dst_ref=rx.at[par, rows_of(i)],
            send_sem=s_x.at[i], recv_sem=r_x.at[par, i], device_id=across, device_id_type=MESH,
        )

    def copy_ag(i):
        return pltpu.make_async_remote_copy(
            src_ref=sumb.at[core, rows_of(i)], dst_ref=sumb.at[core, rows_of(i)],
            send_sem=s_ag.at[i], recv_sem=r_ag.at[i], device_id=mate, device_id_type=MESH,
        )

    def hop_two(i, par):
        copy_core(i).wait()
        rows = rows_of(i)
        pbuf[core, rows] = (pbuf[core, rows].astype(f32) + rcore[rows].astype(f32)).astype(bf16)
        copy_x(i, par).start()

    def hop_three(i, par):
        copy_x(i, par).wait()
        rows = rows_of(i)
        sumb[core, rows] = (pbuf[core, rows].astype(f32) + rx[par, rows].astype(f32)).astype(bf16)
        copy_ag(i).start()

    def arrived(i):
        copy_ag(i).wait()

    def summed(i, r):
        where = chunk_of(i, r)
        return jnp.concatenate([sumb[0, where].astype(f32), sumb[1, where].astype(f32)], axis=1)

    def store_p(i, t, value):
        pbuf[t // 2, rows_of(i), (t % 2) * TILE : (t % 2 + 1) * TILE] = value.astype(bf16)

    def stage(body, lo, hi, second, before=None, begun=False):
        def step(i, carry):
            if before is not None:
                before(i, hi)
            body(i)
            copy_core(i).start()

            @pl.when((i > lo) | begun)
            def _():
                second(i - 1)
            return carry

        lax.fori_loop(lo, hi, step, 0)
        second(hi - 1)

    def far(par):
        return lambda i: hop_two(i, par)

    def from_far(par):
        def before(i, hi):
            @pl.when(i + 1 < hi)
            def _():
                hop_three(i + 1, par)
            arrived(i)
        return before

    def each(body, lo, hi, before=None):
        def step(i, carry):
            if before is not None:
                before(i, hi)
            body(i)
            return carry

        lax.fori_loop(lo, hi, step, 0)

    def g_rows(k, lo, n):
        return pl.ds(pl.multiple_of(lax.rem(k * 128 + 2048, 3072) + lo, 16), n)

    def in_rows(k, lo, n):
        return pl.ds(pl.multiple_of(k * PAIR_IN + lo, 16), n)

    def send(k, slot, src, dst, device):
        return pltpu.make_async_remote_copy(
            src_ref=src, dst_ref=dst, send_sem=s_pair.at[slot, k], recv_sem=r_pair.at[slot, k],
            device_id=device, device_id_type=MESH,
        )

    def y_swap(k):
        return send(k, 0, big.at[g_rows(k, 32 - 32 * yy, 32)], recv.at[in_rows(k, 0, 32)], mate_y)

    def y_end(k):
        return send(k, 1, big.at[g_rows(k, 32 * yy, 32)], recv.at[in_rows(k, 32, 32)], mate_e)

    def y_mid(k):
        return send(k, 2, big.at[g_rows(k, 32 * yy, 32)], recv.at[in_rows(k, 64, 32)], mate_m)

    def o_rows(k, lo, n):
        return gall_hbm.at[pl.ds(pl.multiple_of(k * 128 + lo, 16), n)]

    def y_back(k):
        return send(k, 3, big.at[g_rows(k, 32 * yy, 32)], o_rows(k, 32 * yy, 32), mate_e)

    def y_share_mid(k):
        return send(k, 4, big.at[g_rows(k, 32 * yy, 32)], o_rows(k, 32 * yy, 32), mate_y)

    def y_share_end(k):
        return send(k, 4, o_rows(k, 32 * yy, 32), o_rows(k, 32 * yy, 32), mate_y)

    def z_end(k):
        return send(k, 5, big.at[g_rows(k, 64, 64)], recv.at[in_rows(k, 160, 64)], mate_e)

    def z_mid(k):
        return send(k, 6, big.at[g_rows(k, 96 - 32 * zm, 32)], recv.at[in_rows(k, 96, 32)], mate_m)

    def z_swap(k):
        return send(k, 7, big.at[g_rows(k, 64 + 32 * zm, 32)], recv.at[in_rows(k, 128, 32)], mate_y)

    def z_share(k):
        return send(k, 8, big.at[g_rows(k, 64 + 32 * zm, 32)], o_rows(k, 64 + 32 * zm, 32), mate_m)

    def z_back(k):
        return send(k, 9, big.at[g_rows(k, 64 + 32 * zm, 32)], o_rows(k, 64 + 32 * zm, 32), mate_e)

    def z_pass(k):
        return send(k, 10, o_rows(k, 96 - 32 * zm, 32), o_rows(k, 96 - 32 * zm, 32), mate_e)

    def accumulate(k, lo, n, at):
        rows = g_rows(k, lo, n)
        big[rows, :] = (big[rows, :].astype(f32) + recv[in_rows(k, at, n), :].astype(f32)).astype(bf16)

    def keep_y(k):
        return pltpu.make_async_copy(big.at[g_rows(k, 32 * yy, 32)], o_rows(k, 32 * yy, 32), s_out.at[0, k])

    def keep_z(k):
        return pltpu.make_async_copy(
            big.at[g_rows(k, 64 + 32 * zm, 32)], o_rows(k, 64 + 32 * zm, 32), s_out.at[1, k]
        )

    def hop0(k):
        y_swap(k).start()

        @pl.when(jnp.logical_not(middle))
        def _():
            z_end(k).start()

    def hop1(k):
        y_swap(k).wait()
        accumulate(k, 32 * yy, 32, 0)

        @pl.when(middle)
        def _():
            z_end(k).wait_recv()
            accumulate(k, 64, 64, 160)
            z_mid(k).start()

        @pl.when(jnp.logical_not(middle))
        def _():
            y_end(k).start()

    def hop2(k):
        @pl.when(middle)
        def _():
            y_end(k).wait_recv()
            accumulate(k, 32 * yy, 32, 32)
            y_mid(k).start()
            z_mid(k).wait()
            accumulate(k, 64 + 32 * zm, 32, 96)
            z_swap(k).start()

    def hop3(k):
        @pl.when(middle)
        def _():
            y_mid(k).wait()
            accumulate(k, 32 * yy, 32, 64)
            y_back(k).start()
            y_share_mid(k).start()
            keep_y(k).start()
            z_swap(k).wait()
            accumulate(k, 64 + 32 * zm, 32, 128)
            z_share(k).start()
            z_back(k).start()
            keep_z(k).start()

    def hop4(k):
        @pl.when(middle)
        def _():
            z_share(k).wait()
            z_pass(k).start()

        @pl.when(jnp.logical_not(middle))
        def _():
            y_end(k).wait_send()
            y_back(k).wait_recv()
            y_share_end(k).start()

    def hop5(k):
        @pl.when(middle)
        def _():
            y_share_mid(k).wait()
            y_back(k).wait_send()
            z_back(k).wait_send()
            z_pass(k).wait_send()
            keep_y(k).wait()
            keep_z(k).wait()

        @pl.when(jnp.logical_not(middle))
        def _():
            y_share_end(k).wait()
            z_end(k).wait_send()
            z_back(k).wait_recv()
            z_pass(k).wait_recv()

    hops = ((5, hop5), (4, hop4), (3, hop3), (2, hop2), (1, hop1), (0, hop0))

    def tick(t, low, high, lag):
        for h, hop in hops:
            k = low + t - lag * h

            @pl.when((k >= low) & (k < high))
            def _(hop=hop, k=k):
                hop(k)

    def tick_mlp(t):
        tick(t, 0, 16, LAG)

    def tick_attention(t):
        tick(t, 16, pairs, LAG_END)

    def ticks(run, lo, hi):
        def step(t, carry):
            run(t)
            return carry

        lax.fori_loop(lo, hi, step, 0)

    for k in (0, 1, 2, 3):
        loads[k].wait()
    loads[4].start()
    loads[5].start()


    def attend(q, k, v, row_bias):
        o = jnp.zeros((PAD, 256), f32)
        for h in range(4):
            scores = nt(only(q, h), k) + row_bias
            e = jnp.exp(scores - jnp.max(scores, axis=1, keepdims=True))
            p = (e * (1.0 / jnp.sum(e, axis=1, keepdims=True))).astype(bf16)
            o = o + nn(p, only(v, h))
        return o.astype(bf16)

    def attention(i):
        start = pl.multiple_of(i * PAD, 16)
        for c in range(width // 128):
            xs[pl.ds(start, count), c * 128 : (c + 1) * 128] = h1s[c, pl.ds(i, count, stride=images), :].astype(bf16)
        for r in chunks():
            u, _ = stats(xs[chunk_of(i, r), :].astype(f32))
            a2s[chunk_of(i, r), :] = (u * g1).astype(bf16)
        rows = rows_of(i)
        a1 = a2s[rows, :]
        qkv[rows, 0:256] = (nn(a1, wqkv[:, 0:256]) * 0.125).astype(bf16)
        qkv[rows, 256:512] = nn(a1, wqkv[:, 256:512]).astype(bf16)
        qkv[rows, 512:768] = nn(a1, wqkv[:, 512:768]).astype(bf16)
        os[rows, :] = attend(qkv[rows, 0:256], qkv[rows, 256:512], qkv[rows, 512:768], bias[i])

    def attention_sent(i):
        attention(i)
        ob = os[rows_of(i), :]
        for t in range(4):
            store_p(i, t, nn(ob, wo[:, t * TILE : (t + 1) * TILE]))

    attention_sent(0)

    pl.semaphore_wait(barrier, dps + 1)

    def learn_copy(k):
        return pltpu.make_async_remote_copy(
            src_ref=wl_part(dp), dst_ref=wl_part(dp),
            send_sem=slearn_s.at[k - 1], recv_sem=slearn_r.at[k - 1],
            device_id=(lax.rem(dp + k, dps), mp), device_id_type=MESH,
        )

    loads[6].wait()
    for k in range(1, dps):
        learn_copy(k).start()

    copy_core(0).start()
    stage(attention_sent, 1, images, far(0), begun=True)

    loads[4].wait()
    loads[5].wait()

    def mlp(i):
        for r in chunks():
            h1 = xs[chunk_of(i, r), :].astype(f32) + summed(i, r)
            put_wide(chunk_of(i, r), h1)
            u, _ = stats(h1)
            a2s[chunk_of(i, r), :] = (u * g2).astype(bf16)
        rows = rows_of(i)
        a2 = a2s[rows, :]
        for t in range(4):
            cols = slice(t * TILE, (t + 1) * TILE)
            z = nn(a2, wup[:, cols])
            cdf, pdf = gauss(z)
            rs[rows, cols] = (z * cdf).astype(bf16)
            gs[rows, cols] = (cdf + z * pdf).astype(bf16)
        act = rs[rows, :]
        for t in range(4):
            store_p(i, t, nn(act, wdn[:, t * TILE : (t + 1) * TILE]))

    hop_three(0, 0)
    stage(mlp, 0, images, far(1), from_far(0))

    for k in range(1, dps):
        learn_copy(k).wait()
    dg[...] = jnp.zeros_like(dg)
    gl_sum[...] = jnp.zeros_like(gl_sum)
    gsel_sum[...] = jnp.zeros_like(gsel_sum)

    def y_out(i):
        return pltpu.make_async_copy(d1s.at[rows_of(i)], y_hbm.at[rows_of(i)], sy.at[i])

    def learner(i):
        rows = rows_of(i)
        for r in chunks():
            yb = (get_wide(chunk_of(i, r)) + summed(i, r)).astype(bf16)
            d1s[chunk_of(i, r), :] = yb
            v = yb.astype(f32)
            mean = jnp.sum(v, axis=-1, keepdims=True) * (1.0 / width)
            v = v - mean
            s = lax.rsqrt(jnp.sum(v * v, axis=-1, keepdims=True) * (1.0 / width) + 1e-06)
            centre[r : r + CH, :] = mean
            scale[r : r + CH, :] = s
            dhs[chunk_of(i, r), :] = (v * s * g3).astype(bf16)
        y_out(i).start()
        y = d1s[rows, :]
        a3 = dhs[rows, :]
        wlf = wl[...]
        wsel = wsel_ref[...]
        ct = ct_ref[i]
        zl = nt(a3, wlf)
        cdf, pdf = gauss(zl)
        t = (zl * cdf).astype(bf16)
        slope = cdf + zl * pdf
        col_bias = col[rows, :]
        logits = nt(t, wsel) + col_bias
        e = jnp.exp(logits - jnp.max(logits, axis=0, keepdims=True))
        maps = e * (1.0 / jnp.sum(e, axis=0, keepdims=True))
        mb = maps.astype(bf16)
        learned_ref[i] = tn(mb, y).astype(bf16)
        dmaps = nt(y, ct)
        dlog = (maps * (dmaps - jnp.sum(maps * dmaps, axis=0, keepdims=True))).astype(bf16)
        gsel_sum[...] += tn(dlog, t)
        dzl = (nn(dlog, wsel) * slope).astype(bf16)
        gl_sum[...] += tn(dzl, a3)
        part_a[...] = nn(dzl, wlf)
        part_b[...] = nn(mb, ct)
        for r in chunks():
            da3 = part_a[r : r + CH, :]
            dy = part_b[r : r + CH, :]
            s = scale[r : r + CH, :]
            u = (d1s[chunk_of(i, r), :].astype(f32) - centre[r : r + CH, :]) * s
            dg[2] += fold(da3 * u)
            dhs[chunk_of(i, r), :] = (dy + back(da3 * g3, u, s)).astype(bf16)

    def mlp_back(i):
        rows = rows_of(i)
        dhb = dhs[rows, :]
        for c in range(4):
            cols = slice(c * TILE, (c + 1) * TILE)
            dr = nt(dhb, wdn[cols, :])
            gs[rows, cols] = (dr * gs[rows, cols].astype(f32)).astype(bf16)
        dz = gs[rows, :]
        for c in range(4):
            store_p(i, c, nt(dz, wup[c * TILE : (c + 1) * TILE, :]))

    early = images // 2

    def learner_mlp(i):
        learner(i)

        @pl.when(i < early)
        def _():
            mlp_back(i)
            copy_core(i).start()

        @pl.when((i > 0) & (i <= early))
        def _():
            hop_two(i - 1, 0)

    hop_three(0, 1)
    each(learner_mlp, 0, images, from_far(1))

    def grad(left, right, first, after):
        def step(j, carry):
            lhs = left[:, pl.ds(pl.multiple_of(j * TILE, TILE), TILE)]
            rows = g_rows(2 * (first + j), 0, TILE)
            for c in range(0, width, TILE):
                big[rows, c : c + TILE] = tn(lhs, right[:, c : c + TILE]).astype(bf16)
            if after is not None:
                after(j)
            return carry

        lax.fori_loop(0, left.shape[1] // TILE, step, 0)

    def ready():
        pl.semaphore_signal(ready_y, inc=1, device_id=mate_y, device_id_type=MESH)

        @pl.when(middle)
        def _():
            pl.semaphore_signal(ready_z, inc=1, device_id=mate_e, device_id_type=MESH)
            pl.semaphore_signal(ready_z, inc=1, device_id=mate_m, device_id_type=MESH)

    def both_ready():
        pl.semaphore_wait(ready_y, 1)
        pl.semaphore_wait(ready_z, 1)

    grad(rs, dhs, 0, tick_mlp)

    def mlp_back_tick(i):
        mlp_back(i)

        @pl.when(lax.rem(i, 2) == 1)
        def _():
            tick_mlp(4 + (i - early) // 2)

    stage(mlp_back_tick, early, images, far(0))
    def after_up(j):
        @pl.when(lax.rem(j, 2) == 1)
        def _():
            tick_mlp(6 + j // 2)

    grad(a2s, gs, 4, after_up)
    ready()
    for i in range(images):
        y_out(i).wait()

    def attention_back(i):
        rows = rows_of(i)
        for r in chunks():
            where = chunk_of(i, r)
            da2 = summed(i, r)
            u, s = stats(get_wide(where))
            dg[1] += fold(da2 * u)
            d1s[where, :] = (dhs[where, :].astype(f32) + back(da2 * g2, u, s)).astype(bf16)
            ux, _ = stats(xs[where, :].astype(f32))
            a2s[where, :] = (ux * g1).astype(bf16)
        d1 = d1s[rows, :]
        do = nt(d1, wo[...]).astype(bf16)
        q = qkv[rows, 0:256]
        k = qkv[rows, 256:512]
        v = qkv[rows, 512:768]
        col_bias = col[rows, :]
        dq = jnp.zeros((PAD, 256), f32)
        dk = jnp.zeros((PAD, 256), f32)
        dv = jnp.zeros((PAD, 256), f32)
        for h in range(4):
            kh = only(k, h)
            scores = nt(kh, q) + col_bias
            e = jnp.exp(scores - jnp.max(scores, axis=0, keepdims=True))
            p = e * (1.0 / jnp.sum(e, axis=0, keepdims=True))
            dv = dv + nn(p.astype(bf16), only(do, h))
            dpr = nt(only(v, h), do)
            ds = (p * (dpr - jnp.sum(p * dpr, axis=0, keepdims=True))).astype(bf16)
            dk = dk + nn(ds, only(q, h))
            dq = dq + tn(ds, kh)
        qkv[rows, 0:256] = (dq * 0.125).astype(bf16)
        qkv[rows, 256:512] = dk.astype(bf16)
        qkv[rows, 512:768] = dv.astype(bf16)
        dall = qkv[rows, :]
        for c in range(4):
            store_p(i, c, nt(dall, wqkv[c * TILE : (c + 1) * TILE, :]))
        tick_mlp(8 + i)

    hop_three(0, 0)
    both_ready()
    stage(attention_back, 0, images, far(1), from_far(0))
    grad(os, d1s, 8, lambda j: tick_mlp(16))
    tick_attention(0)
    tick_attention(1)

    def grad_qkv(j, carry):
        lhs = a2s[:, pl.ds(pl.multiple_of(j * TILE, TILE), TILE)]
        for n in range(3):
            value = tn(lhs, qkv[:, n * TILE : (n + 1) * TILE]).astype(bf16)
            rows = pl.ds(pl.multiple_of(1280 + j * 192 + n * 64, 16), 64)
            for c in range(4):
                big[rows, c * TILE : (c + 1) * TILE] = value[c * 64 : (c + 1) * 64]
        tick_mlp(17 + j)
        tick_attention(2 + j)
        return carry

    lax.fori_loop(0, 4, grad_qkv, 0)

    def gp_out(i):
        return pltpu.make_async_copy(dhs.at[rows_of(i)], gp_hbm.at[rows_of(i)], sy.at[i])

    def finish(i, carry):
        @pl.when(i + 1 < images)
        def _():
            hop_three(i + 1, 1)
        arrived(i)
        for r in chunks():
            where = chunk_of(i, r)
            da1 = summed(i, r)
            u, s = stats(xs[where, :].astype(f32))
            dg[0] += fold(da1 * u)
            dhs[where, :] = (d1s[where, :].astype(f32) + back(da1 * g1, u, s)).astype(bf16)
        gp_out(i).start()
        tick_mlp(21 + i)
        tick_attention(6 + i)
        return carry

    hop_three(0, 1)
    lax.fori_loop(0, images, finish, 0)

    small_mine[0:8, :] = jnp.concatenate(
        [jnp.sum(dg[n], axis=0, keepdims=True) for n in range(3)] + [jnp.zeros((5, width), f32)], axis=0
    ).astype(bf16)
    small_mine[8:16, 0:64] = gsel_sum[...].astype(bf16)
    small_mine[8:16, 64:width] = jnp.zeros((8, width - 64), bf16)
    gl_mine[...] = gl_sum[...].astype(bf16)
    part = wl_hbm.shape[1]

    def gl_part(d):
        return pl.ds(pl.multiple_of(d * part, 128), part)

    def small_copy(k):
        peer = lax.rem(dp + k, dps)
        return (
            pltpu.make_async_remote_copy(
                src_ref=small_mine, dst_ref=small_in.at[k - 1], send_sem=s_small.at[0, k - 1],
                recv_sem=r_small.at[0, k - 1], device_id=(peer, mp), device_id_type=MESH,
            ),
            pltpu.make_async_remote_copy(
                src_ref=gl_mine.at[:, gl_part(peer)], dst_ref=gl_in.at[k - 1], send_sem=s_small.at[1, k - 1],
                recv_sem=r_small.at[1, k - 1], device_id=(peer, mp), device_id_type=MESH,
            ),
        )

    for k in range(1, dps):
        for copy in small_copy(k):
            copy.start()
    ticks(tick_mlp, 29, 16 + 5 * LAG)
    ticks(tick_attention, 14, 8 + 5 * LAG_END)
    for k in range(1, dps):
        for copy in small_copy(k):
            copy.wait()
    small_ref[...] = small_mine[...].astype(f32)
    gl_ref[...] = gl_mine[:, gl_part(dp)].astype(f32)
    for k in range(dps - 1):
        small_ref[...] += small_in[k].astype(f32)
        gl_ref[...] += gl_in[k].astype(f32)
    for i in range(images):
        gp_out(i).wait()


def finish_up(
    gall, y, gp, learned, small, gl,
    learned_ref, y_ref, gp_ref, gq_ref, gk_ref, gv_ref, gout_ref, gup_ref, gdn_ref, d1_ref, d2_ref, d3_ref,
    gl_ref, gsel_ref,
    tiles, y_in, gp_in, wide, square, y_turned, gp_turned, strip, s_tile, s_in, s_wide, s_square, s_turned,
):
    count = y_ref.shape[0]

    def tile_in(j):
        rows = pl.ds(j * TILE, TILE)
        return pltpu.make_async_copy(gall.at[rows], tiles.at[rows], s_tile.at[j])

    ins = [pltpu.make_async_copy(y, y_in, s_in.at[0]), pltpu.make_async_copy(gp, gp_in, s_in.at[1])]
    for j in range(4):
        tile_in(j).start()
    for copy in ins:
        copy.start()
    for j in range(4, 12):
        tile_in(j).start()
    outs = []

    def tile_out(j):
        tile_in(j).wait()
        rows = slice(j * TILE, (j + 1) * TILE)
        wide[rows, :] = tiles[rows, :].astype(f32)
        ref, first = ((gdn_ref, 0), (gup_ref, 4), (gout_ref, 8))[j // 4]
        copy = pltpu.make_async_copy(
            wide.at[pl.ds(j * TILE, TILE)], ref.at[pl.ds((j - first) * TILE, TILE)], s_wide.at[j]
        )
        copy.start()
        outs.append(copy)

    def turn(n, src, dst, ref):
        ins[n].wait()
        for block in range(0, count, CH):
            rows = min(CH, count - block)
            for c in range(src.shape[2] // 128):
                cols = slice(c * 128, (c + 1) * 128)
                slot = strip.at[c]
                slot[...] = src[:, block : block + CH, cols].astype(f32).reshape(slot.shape)
                for r in range(rows):
                    dst[block + r, :, cols] = slot[pl.ds(r, dst.shape[1], stride=CH), :].astype(bf16)
            copy = pltpu.make_async_copy(
                dst.at[pl.ds(block, rows)], ref.at[pl.ds(block, rows)], s_turned.at[n, block // CH]
            )
            copy.start()
            outs.append(copy)

    for j in range(4):
        tile_out(j)
    turn(0, y_in, y_turned, y_ref)
    for j in range(4, 9):
        tile_out(j)
    turn(1, gp_in, gp_turned, gp_ref)
    for j in range(9, 12):
        tile_in(j).wait()
    for n, ref in enumerate((gq_ref, gk_ref, gv_ref)):
        for j in range(4):
            for c in range(4):
                square[n, j * TILE + c * 64 : j * TILE + (c + 1) * 64, :] = tiles[
                    9 * TILE + j * 192 + n * 64 : 9 * TILE + j * 192 + (n + 1) * 64, c * TILE : (c + 1) * TILE
                ].astype(f32)
        copy = pltpu.make_async_copy(square.at[n], ref, s_square.at[n])
        copy.start()
        outs.append(copy)
    learned_ref[...] = learned[...]
    for n, ref in enumerate((d1_ref, d2_ref, d3_ref)):
        ref[...] = small[n : n + 1, :]
    gl_ref[...] = gl[...]
    gsel_ref[...] = small[8:16, 0 : gsel_ref.shape[1]]
    for copy in outs:
        copy.wait()


def local_fused(
    patches, keep_mask, w_query, w_key, w_value, w_out, w_up, w_down,
    gain_attn, gain_mlp, gain_learn, w_learn, w_select, cotangent,
):
    images, count, width = patches.shape
    total = images * PAD
    hidden = w_up.shape[1]
    learn_rows, learn_cols = w_learn.shape
    dps = lax.axis_size("dp")
    anywhere = pl.BlockSpec(memory_space=pl.ANY)
    vmem = pl.BlockSpec(memory_space=pltpu.VMEM)
    sds = jax.ShapeDtypeStruct
    dma = pltpu.SemaphoreType.DMA
    outs = pl.pallas_call(
        fused,
        name="block",
        out_shape=(
            sds((images, 8, width), bf16),
            sds((total, width), bf16),
            sds((total, width), bf16),
            sds((3072, width), bf16),
            sds((16, width), f32),
            sds((learn_cols, learn_rows), f32),
        ),
        in_specs=[anywhere, vmem] + [anywhere] * 6 + [vmem] * 3 + [anywhere] + [vmem] * 2,
        out_specs=(vmem,) + (anywhere,) * 3 + (vmem,) * 2,
        scratch_shapes=[
            pltpu.VMEM((images, 1, PAD), f32),
            pltpu.VMEM((width, 768), bf16),
            pltpu.VMEM((256, width), bf16),
            pltpu.VMEM((learn_cols, width), bf16),
            pltpu.VMEM((total, width), bf16),
            pltpu.VMEM((total, 768), bf16),
            pltpu.VMEM((total, 256), bf16),
            pltpu.VMEM((width // 128, total, 128), f32),
            pltpu.VMEM((total, width), bf16),
            pltpu.VMEM((total, width), bf16),
            pltpu.VMEM((total, width), bf16),
            pltpu.VMEM((3072, width), bf16),
            pltpu.VMEM((8 * PAIR_IN + total + 2 * width, width), bf16),
            pltpu.VMEM((2, total, width // 2), bf16),
            pltpu.VMEM((total, width // 2), bf16),
            pltpu.VMEM((2, total, width // 2), bf16),
            pltpu.VMEM((2, total, width // 2), bf16),
            pltpu.VMEM((3, 8, width), f32),
            pltpu.VMEM((learn_cols, width), f32),
            pltpu.VMEM((8, learn_cols), f32),
            pltpu.VMEM((learn_cols, width), bf16),
            pltpu.VMEM((dps - 1, learn_cols, learn_rows), bf16),
            pltpu.VMEM((16, width), bf16),
            pltpu.VMEM((dps - 1, 16, width), bf16),
            pltpu.VMEM((total, 1), f32),
            pltpu.VMEM((PAD, 1), f32),
            pltpu.VMEM((PAD, 1), f32),
            pltpu.VMEM((PAD, width), f32),
            pltpu.VMEM((PAD, width), f32),
            dma((4,)), dma((7,)), dma((images,)), dma((dps - 1,)), dma((dps - 1,)),
            dma((images,)), dma((images,)), dma((images,)), dma((2, images)), dma((images,)), dma((images,)),
            dma((11, 24)), dma((11, 24)), dma((2, 24)),
            pltpu.SemaphoreType.REGULAR, pltpu.SemaphoreType.REGULAR, dma((2, dps - 1)), dma((2, dps - 1)),
        ],
        compiler_params=pltpu.CompilerParams(
            collective_id=0, has_side_effects=True, vmem_limit_bytes=60 * 2**20
        ),
    )(
        patches.transpose(1, 0, 2).reshape(count * images, width), keep_mask, w_query, w_key, w_value, w_out, w_up, w_down,
        gain_attn[None], gain_mlp[None], gain_learn[None], w_learn.T, w_select.T, cotangent,
    )
    learned, y, gpat, gall, small, gl = outs

    square = (width, TILE)
    row = (1, width)
    blocks = -(-count // CH)
    outs = pl.pallas_call(
        finish_up,
        name="finish",
        out_shape=(
            sds((images, 8, width), bf16), sds((count, images, width), bf16), sds((count, images, width), bf16),
            sds(square, f32), sds(square, f32), sds(square, f32),
            sds((TILE, width), f32), sds((width, hidden), f32), sds((hidden, width), f32),
            sds(row, f32), sds(row, f32), sds(row, f32),
            sds((learn_cols, learn_rows), f32), sds((8, learn_cols), f32),
        ),
        in_specs=[anywhere] * 3 + [vmem] * 3,
        out_specs=(vmem,) + (anywhere,) * 8 + (vmem,) * 5,
        scratch_shapes=[
            pltpu.VMEM((3072, width), bf16),
            pltpu.VMEM((images, PAD, width), bf16),
            pltpu.VMEM((images, PAD, width), bf16),
            pltpu.VMEM((9 * TILE, width), f32),
            pltpu.VMEM((3,) + square, f32),
            pltpu.VMEM((count, images, width), bf16),
            pltpu.VMEM((count, images, width), bf16),
            pltpu.VMEM((width // 128, images * CH, 128), f32),
            dma((12,)), dma((2,)), dma((9,)), dma((3,)), dma((2, blocks)),
        ],
        compiler_params=pltpu.CompilerParams(vmem_limit_bytes=60 * 2**20),
    )(gall, y.reshape(images, PAD, width), gpat.reshape(images, PAD, width), learned, small, gl)
    learned, y, gpat, gq, gk, gv, gout, gup, gdn, d1, d2, d3, gl, gsel = outs
    return (
        learned, y.transpose(1, 0, 2), gpat.transpose(1, 0, 2), gq, gk, gv, gout, gup, gdn,
        d1[0], d2[0], d3[0], gl.T, gsel.T,
    )


def solution(mesh):
    small = mesh.shape["dp"] == 8 and mesh.shape["mp"] == 4
    return jax.shard_map(
        local_fused if small else local,
        mesh=mesh,
        in_specs=(
            P("dp", None, None),
            P("dp", None),
            P(None, "mp"),
            P(None, "mp"),
            P(None, "mp"),
            P("mp", None),
            P(None, "mp"),
            P("mp", None),
            P(),
            P(),
            P(),
            P("dp", None),
            P(),
            P("dp", None, None),
        ),
        out_specs=(
            P("dp", None, None),
            P("dp", None, None),
            P("dp", None, None),
            P(None, "mp"),
            P(None, "mp"),
            P(None, "mp"),
            P("mp", None),
            P(None, "mp"),
            P("mp", None),
            P(),
            P(),
            P(),
            P("dp", None),
            P(),
        ),
        check_vma=False,
    )
```

```python
import math

import jax
import jax.numpy as jnp
from jax import lax
from jax.experimental import pallas as pl
from jax.experimental.pallas import tpu as pltpu
from jax.sharding import PartitionSpec as P

D = 1024
HEADS = 16


def product(left, right):
    return jnp.dot(left, right, preferred_element_type=jnp.float32)


def contract_rows(left, right):
    return lax.dot_general(
        left, right, (((0,), (0,)), ((), ())), preferred_element_type=jnp.float32
    )


def contract_cols(left, right):
    return lax.dot_general(
        left, right, (((1,), (1,)), ((), ())), preferred_element_type=jnp.float32
    )


def normalize(inputs):
    row_mean = jnp.mean(inputs, axis=-1, keepdims=True)
    centered = inputs - row_mean
    inverse = lax.rsqrt(jnp.mean(centered * centered, axis=-1, keepdims=True) + 1e-06)
    return (centered * inverse, inverse)


def norm_back(grad_norm, normed, inverse, gain):
    scaled_grad = grad_norm * gain
    grad_input = inverse * (
        scaled_grad
        - jnp.mean(scaled_grad, axis=-1, keepdims=True)
        - normed * jnp.mean(scaled_grad * normed, axis=-1, keepdims=True)
    )
    return (grad_input, jnp.sum(grad_norm * normed, axis=0))


def gelu_exact(inputs):
    return jax.nn.gelu(inputs, approximate=False)


def gelu_back(hidden_pre, grad_act):
    _, pullback = jax.vjp(gelu_exact, hidden_pre)
    return pullback(grad_act)[0]


def local(
    patches,
    keep_mask,
    w_query,
    w_key,
    w_value,
    w_out,
    w_up,
    w_down,
    gain_attn,
    gain_mlp,
    gain_learn,
    w_learn,
    w_select,
    cotangent,
):
    images, patch_count, feature_count = patches.shape
    row_count = images * patch_count
    head_size = D // HEADS
    heads_here = w_query.shape[1] // head_size
    score_scale = 1.0 / math.sqrt(head_size)
    visible = keep_mask > 0
    head_shape = (images, patch_count, heads_here, head_size)
    residual_rows = patches.reshape(row_count, feature_count).astype(jnp.float32)
    normed_one, inverse_one = normalize(residual_rows)
    attn_input = (normed_one * gain_attn).astype(jnp.bfloat16)
    query_flat = product(attn_input, w_query).astype(jnp.bfloat16)
    key_flat = product(attn_input, w_key).astype(jnp.bfloat16)
    value_flat = product(attn_input, w_value).astype(jnp.bfloat16)
    query_heads = query_flat.reshape(head_shape)
    key_heads = key_flat.reshape(head_shape)
    value_heads = value_flat.reshape(head_shape)

    def masked_scores():
        raw_scores = (
            jnp.einsum(
                "bqhe,bkhe->bhqk", query_heads, key_heads, preferred_element_type=jnp.float32
            )
            * score_scale
        )
        return jnp.where(visible[:, None, None, :], raw_scores, -1e30)

    scores = masked_scores()
    top_score = jnp.max(scores, axis=-1, keepdims=True)
    exponent = jnp.exp(scores - top_score)
    denominator = jnp.sum(exponent, axis=-1, keepdims=True)
    logsum = top_score + jnp.log(denominator)
    probs_low = (exponent / denominator).astype(jnp.bfloat16)
    mixed_heads = jnp.einsum(
        "bhqk,bkhe->bqhe", probs_low, value_heads, preferred_element_type=jnp.float32
    )
    mixed_heads = mixed_heads.astype(jnp.bfloat16).reshape(row_count, heads_here * head_size)
    attn_term = product(mixed_heads, w_out)
    hidden_one = residual_rows + lax.psum(attn_term.astype(jnp.bfloat16), "mp").astype(jnp.float32)
    normed_two, inverse_two = normalize(hidden_one)
    mlp_input = (normed_two * gain_mlp).astype(jnp.bfloat16)
    hidden_pre = product(mlp_input, w_up)
    activated = gelu_exact(hidden_pre).astype(jnp.bfloat16)
    mlp_out = lax.psum(product(activated, w_down).astype(jnp.bfloat16), "mp").astype(jnp.float32)
    block_rows = (hidden_one + mlp_out).astype(jnp.bfloat16)
    normed_learn, inverse_learn = normalize(block_rows.astype(jnp.float32))
    learn_input = (normed_learn * gain_learn).astype(jnp.bfloat16)
    learn_full = lax.all_gather(w_learn, "dp", axis=0, tiled=True)
    learn_pre = product(learn_input, learn_full)
    learn_act = gelu_exact(learn_pre).astype(jnp.bfloat16)
    logits = product(learn_act, w_select).reshape(images, patch_count, -1)
    logits = jnp.where(visible[:, :, None], logits, -1e30)
    top_logit = jnp.max(logits, axis=1, keepdims=True)
    exp_logit = jnp.exp(logits - top_logit)
    token_maps = exp_logit / jnp.sum(exp_logit, axis=1, keepdims=True)
    maps_low = token_maps.astype(jnp.bfloat16)
    block_three = block_rows.reshape(images, patch_count, feature_count)
    learned = jnp.einsum(
        "bpn,bpd->bnd", maps_low, block_three, preferred_element_type=jnp.float32
    ).astype(jnp.bfloat16)
    grad_maps = jnp.einsum(
        "bnd,bpd->bpn", cotangent, block_three, preferred_element_type=jnp.float32
    )
    grad_block = jnp.einsum(
        "bpn,bnd->bpd", maps_low, cotangent, preferred_element_type=jnp.float32
    ).reshape(row_count, feature_count)
    grad_logits = token_maps * (grad_maps - jnp.sum(token_maps * grad_maps, axis=1, keepdims=True))
    grad_logits = grad_logits.reshape(row_count, -1).astype(jnp.bfloat16)
    grad_select = contract_rows(learn_act, grad_logits)
    grad_learn_act = contract_cols(grad_logits, w_select)
    grad_learn_pre = gelu_back(learn_pre, grad_learn_act).astype(jnp.bfloat16)
    grad_learn = contract_rows(learn_input, grad_learn_pre)
    grad_learn_input = contract_cols(grad_learn_pre, learn_full)
    grad_from_learn, grad_gain_learn = norm_back(
        grad_learn_input, normed_learn, inverse_learn, gain_learn
    )
    grad_hidden = grad_block + grad_from_learn
    grad_hidden_low = grad_hidden.astype(jnp.bfloat16)
    grad_down = contract_rows(activated, grad_hidden_low)
    grad_act = contract_cols(grad_hidden_low, w_down)
    grad_pre = gelu_back(hidden_pre, grad_act).astype(jnp.bfloat16)
    grad_up = contract_rows(mlp_input, grad_pre)
    mlp_back_term = contract_cols(grad_pre, w_up)
    grad_mlp_input = lax.psum(mlp_back_term.astype(jnp.bfloat16), "mp").astype(jnp.float32)
    grad_from_two, grad_gain_mlp = norm_back(grad_mlp_input, normed_two, inverse_two, gain_mlp)
    grad_hidden = grad_hidden + grad_from_two
    grad_attn_low = grad_hidden.astype(jnp.bfloat16)
    grad_out = contract_rows(mixed_heads, grad_attn_low)
    grad_mixed = contract_cols(grad_attn_low, w_out).astype(jnp.bfloat16).reshape(head_shape)
    probs_again = jnp.exp(masked_scores() - logsum)
    probs_again_low = probs_again.astype(jnp.bfloat16)
    grad_probs = jnp.einsum(
        "bqhe,bkhe->bhqk", grad_mixed, value_heads, preferred_element_type=jnp.float32
    )
    grad_value_heads = jnp.einsum(
        "bhqk,bqhe->bkhe", probs_again_low, grad_mixed, preferred_element_type=jnp.float32
    ).astype(jnp.bfloat16)
    grad_scores = probs_again * (
        grad_probs - jnp.sum(probs_again * grad_probs, axis=-1, keepdims=True)
    )
    grad_scores = grad_scores.astype(jnp.bfloat16)
    grad_query_heads = (
        jnp.einsum("bhqk,bkhe->bqhe", grad_scores, key_heads, preferred_element_type=jnp.float32)
        * score_scale
    ).astype(jnp.bfloat16)
    grad_key_heads = (
        jnp.einsum("bhqk,bqhe->bkhe", grad_scores, query_heads, preferred_element_type=jnp.float32)
        * score_scale
    ).astype(jnp.bfloat16)
    grad_query_flat = grad_query_heads.reshape(row_count, -1)
    grad_key_flat = grad_key_heads.reshape(row_count, -1)
    grad_value_flat = grad_value_heads.reshape(row_count, -1)
    grad_query = contract_rows(attn_input, grad_query_flat)
    grad_key = contract_rows(attn_input, grad_key_flat)
    grad_value = contract_rows(attn_input, grad_value_flat)
    attn_terms = (
        contract_cols(grad_query_flat, w_query)
        + contract_cols(grad_key_flat, w_key)
        + contract_cols(grad_value_flat, w_value)
    )
    grad_attn_input = lax.psum(attn_terms.astype(jnp.bfloat16), "mp").astype(jnp.float32)
    grad_from_one, grad_gain_attn = norm_back(grad_attn_input, normed_one, inverse_one, gain_attn)
    grad_patches = (
        (grad_hidden + grad_from_one)
        .astype(jnp.bfloat16)
        .reshape(images, patch_count, feature_count)
    )
    (
        grad_query,
        grad_key,
        grad_value,
        grad_out,
        grad_gain_attn,
        grad_up,
        grad_down,
        grad_gain_mlp,
        grad_gain_learn,
        grad_select,
        grad_learn,
    ) = (
        lax.psum(grad_query.astype(jnp.bfloat16), "dp").astype(jnp.float32),
        lax.psum(grad_key.astype(jnp.bfloat16), "dp").astype(jnp.float32),
        lax.psum(grad_value.astype(jnp.bfloat16), "dp").astype(jnp.float32),
        lax.psum(grad_out.astype(jnp.bfloat16), "dp").astype(jnp.float32),
        lax.psum(grad_gain_attn.astype(jnp.bfloat16), "dp").astype(jnp.float32),
        lax.psum(grad_up.astype(jnp.bfloat16), "dp").astype(jnp.float32),
        lax.psum(grad_down.astype(jnp.bfloat16), "dp").astype(jnp.float32),
        lax.psum(grad_gain_mlp.astype(jnp.bfloat16), "dp").astype(jnp.float32),
        lax.psum(grad_gain_learn.astype(jnp.bfloat16), "dp").astype(jnp.float32),
        lax.psum(grad_select.astype(jnp.bfloat16), "dp").astype(jnp.float32),
        lax.psum(grad_learn.astype(jnp.bfloat16), "dp").astype(jnp.float32),
    )
    learn_rows = w_learn.shape[0]
    grad_learn = lax.dynamic_slice_in_dim(
        grad_learn, lax.axis_index("dp") * learn_rows, learn_rows, 0
    )
    return (
        learned,
        block_three,
        grad_patches,
        grad_query,
        grad_key,
        grad_value,
        grad_out,
        grad_up,
        grad_down,
        grad_gain_attn,
        grad_gain_mlp,
        grad_gain_learn,
        grad_learn,
        grad_select,
    )


MESH = pl.DeviceIdType.MESH
PAD = 208
CH = 16
TILE = 256
PAIR_IN = 224
LAG = 2
LAG_END = 2
QB = 32
AHEAD = 7
f32 = jnp.float32
bf16 = jnp.bfloat16


def nn(a, b):
    return jnp.dot(a, b, preferred_element_type=f32)


def nt(a, b):
    return lax.dot_general(a, b, (((1,), (1,)), ((), ())), preferred_element_type=f32)


def tn(a, b):
    return lax.dot_general(a, b, (((0,), (0,)), ((), ())), preferred_element_type=f32)


def gauss(z):
    bell = jnp.exp(-0.5 * (z * z))
    t = 1.0 / (1.0 + 0.23164189 * jnp.abs(z))
    poly = t * (
        0.127414796 + t * (-0.142248368 + t * (0.7107068705 + t * (-0.7265760135 + t * 0.5307027145)))
    )
    tail = poly * bell
    return jnp.where(z >= 0, 1.0 - tail, tail), 0.3989422804014327 * bell


def stats(v):
    mean = jnp.sum(v, axis=-1, keepdims=True) * (1.0 / v.shape[-1])
    c = v - mean
    s = lax.rsqrt(jnp.sum(c * c, axis=-1, keepdims=True) * (1.0 / v.shape[-1]) + 1e-06)
    return c * s, mean, s


def back(e, u, s):
    width = 1.0 / e.shape[-1]
    return s * (
        e
        - jnp.sum(e, axis=-1, keepdims=True) * width
        - u * (jnp.sum(e * u, axis=-1, keepdims=True) * width)
    )


def fold(v):
    total = v[0:8]
    for r in range(8, v.shape[0], 8):
        total = total + v[r : r + 8]
    return total


def chunks():
    return range(0, PAD, CH)


def fused(
    patches, keep_ref, wq_hbm, wk_hbm, wv_hbm, wo_hbm, wup_hbm, wdn_hbm, g1_ref, g2_ref, g3_ref,
    wl_hbm, wsel_ref, ct_ref,
    learned_ref, y_hbm, gp_hbm, gall_hbm, small_ref, gl_ref,
    bias, wqkv, wo, wl,
    xs, qkv, os, h1s, a2s, dhs, d1s, big, recv,
    pbuf, rcore, rx, sumb, dg, gl_sum, gsel_sum, gl_mine, gl_in, small_mine, small_in, col, centre, scale, part_a, part_b,
    sx, sw, sy, slearn_s, slearn_r, s_core, r_core, s_x, r_x, s_ag, r_ag,
    s_pair, r_pair, s_out, ready_y, ready_z, s_small, r_small,
):
    images, count = keep_ref.shape
    width = patches.shape[1]
    half = width // 2
    dp = lax.axis_index("dp")
    mp = lax.axis_index("mp")
    core = lax.rem(mp, 2)
    mate = (dp, mp + 1 - 2 * core)
    across = (dp, lax.rem(mp + 2, 4))
    dps = lax.axis_size("dp")
    yy = lax.rem(dp, 2)
    zz = dp // 2
    middle = (zz == 1) | (zz == 2)
    zm = jnp.where(zz >= 2, 1, 0)
    mate_y = (dp + 1 - 2 * yy, mp)
    mate_e = ((zz + 1 - 2 * lax.rem(zz, 2)) * 2 + yy, mp)
    mate_m = ((3 - zz) * 2 + yy, mp)
    total = images * PAD
    kept = 8 * PAIR_IN
    rs = big.at[pl.ds(0, total)]
    wup = recv.at[pl.ds(kept, width)]
    wdn = recv.at[pl.ds(kept + width, width)]
    gs = recv.at[pl.ds(kept + 2 * width, total)]

    barrier = pltpu.get_barrier_semaphore()
    for device in (mate, across):
        pl.semaphore_signal(barrier, inc=1, device_id=device, device_id_type=MESH)
    for k in range(1, dps):
        pl.semaphore_signal(barrier, inc=1, device_id=(lax.rem(dp + k, dps), mp), device_id_type=MESH)

    def wl_part(d):
        return wl.at[:, pl.ds(pl.multiple_of(d * wl_hbm.shape[1], 128), wl_hbm.shape[1])]

    loads = [
        pltpu.make_async_copy(wq_hbm, wqkv.at[:, pl.ds(0, 256)], sw.at[0]),
        pltpu.make_async_copy(wk_hbm, wqkv.at[:, pl.ds(256, 256)], sw.at[1]),
        pltpu.make_async_copy(wv_hbm, wqkv.at[:, pl.ds(512, 256)], sw.at[2]),
        pltpu.make_async_copy(wo_hbm, wo, sw.at[3]),
        pltpu.make_async_copy(wup_hbm, wup, sw.at[4]),
        pltpu.make_async_copy(wdn_hbm, wdn, sw.at[5]),
        pltpu.make_async_copy(wl_hbm, wl_part(dp), sw.at[6]),
    ]

    load_x = [
        pltpu.make_async_copy(
            patches.at[:, pl.ds(c * TILE, TILE)], dhs.at[pl.ds(0, images * count), pl.ds(c * TILE, TILE)], sx.at[c]
        )
        for c in range(4)
    ]
    for copy in load_x:
        copy.start()
    for k in (0, 1, 2, 3, 6):
        loads[k].start()

    for i in range(images):
        xs[i * PAD + PAD - 16 : (i + 1) * PAD, :] = jnp.zeros((16, width), bf16)
    bias[...] = jnp.full(bias.shape, -1e30, f32)
    for i in range(images):
        bias[i, :, 0:count] = jnp.where(keep_ref[i : i + 1, :] > 0, 0.0, -1e30)
    turned = jnp.transpose(bias[...].reshape(images, PAD))
    for i in range(images):
        col[i * PAD : (i + 1) * PAD, 0:1] = turned[:, i : i + 1]
    for c in range(4):
        load_x[c].wait()
        for r in range(0, images * count, 8 * CH):
            top = min(r + 8 * CH, images * count)
            for n in (2 * c, 2 * c + 1):
                h1s[n, r:top, :] = dhs[r:top, n * 128 : (n + 1) * 128].astype(f32)

    g1 = g1_ref[...]
    g2 = g2_ref[...]
    g3 = g3_ref[...]
    lane_head = lax.broadcasted_iota(jnp.int32, (1, 256), 1) // 64

    def only(v, h):
        return jnp.where(lane_head == h, v, jnp.zeros_like(v))

    def put_wide(where, value):
        for c in range(width // 128):
            h1s[c, where, :] = value[:, c * 128 : (c + 1) * 128]

    def get_wide(where):
        return jnp.concatenate([h1s[c, where, :] for c in range(width // 128)], axis=1)

    def rows_of(i):
        return pl.ds(pl.multiple_of(i * PAD, 16), PAD)

    def chunk_of(i, r):
        return pl.ds(pl.multiple_of(i * PAD + r, 16), CH)

    def copy_core(i):
        return pltpu.make_async_remote_copy(
            src_ref=pbuf.at[1 - core, rows_of(i)], dst_ref=rcore.at[rows_of(i)],
            send_sem=s_core.at[i], recv_sem=r_core.at[i], device_id=mate, device_id_type=MESH,
        )

    def copy_x(i, par):
        return pltpu.make_async_remote_copy(
            src_ref=pbuf.at[core, rows_of(i)], dst_ref=rx.at[par, rows_of(i)],
            send_sem=s_x.at[i], recv_sem=r_x.at[par, i], device_id=across, device_id_type=MESH,
        )

    def copy_ag(i):
        return pltpu.make_async_remote_copy(
            src_ref=sumb.at[core, rows_of(i)], dst_ref=sumb.at[core, rows_of(i)],
            send_sem=s_ag.at[i], recv_sem=r_ag.at[i], device_id=mate, device_id_type=MESH,
        )

    def hop_two(i, par):
        copy_core(i).wait()
        rows = rows_of(i)
        pbuf[core, rows] = (pbuf[core, rows].astype(f32) + rcore[rows].astype(f32)).astype(bf16)
        copy_x(i, par).start()

    def hop_three(i, par):
        copy_x(i, par).wait()
        rows = rows_of(i)
        sumb[core, rows] = (pbuf[core, rows].astype(f32) + rx[par, rows].astype(f32)).astype(bf16)
        copy_ag(i).start()

    def arrived(i):
        copy_ag(i).wait()

    def summed(i, r):
        where = chunk_of(i, r)
        return jnp.concatenate([sumb[0, where].astype(f32), sumb[1, where].astype(f32)], axis=1)

    def store_p(i, t, value):
        pbuf[t // 2, rows_of(i), (t % 2) * TILE : (t % 2 + 1) * TILE] = value.astype(bf16)

    def stage(body, lo, hi, second, before=None, begun=False):
        def step(i, carry):
            if before is not None:
                before(i, hi)
            body(i)
            copy_core(i).start()

            @pl.when((i > lo) | begun)
            def _():
                second(i - 1)
            return carry

        lax.fori_loop(lo, hi, step, 0)
        second(hi - 1)

    def far(par):
        return lambda i: hop_two(i, par)

    def from_far(par):
        def before(i, hi):
            @pl.when(i + 1 < hi)
            def _():
                hop_three(i + 1, par)
            arrived(i)
        return before

    def each(body, lo, hi, before=None):
        def step(i, carry):
            if before is not None:
                before(i, hi)
            body(i)
            return carry

        lax.fori_loop(lo, hi, step, 0)

    def g_tile(j):
        return pl.ds(pl.multiple_of(lax.rem(j * TILE + 2048, 3072), 16), TILE)

    def pieces(q, count_of, first, number, lag):
        def g_rows(k, lo, n):
            return pl.ds(pl.multiple_of(lax.rem(k * (4 * q) + first + 2048, 3072) + lo, 16), n)

        def in_rows(k, lo, n):
            return pl.ds(pl.multiple_of(k * (7 * q) + first // 128 * PAIR_IN + lo, 16), n)

        def send(k, slot, src, dst, device):
            return pltpu.make_async_remote_copy(
                src_ref=src, dst_ref=dst, send_sem=s_pair.at[slot, k + number], recv_sem=r_pair.at[slot, k + number],
                device_id=device, device_id_type=MESH,
            )

        def y_swap(k):
            return send(k, 0, big.at[g_rows(k, q - q * yy, q)], recv.at[in_rows(k, 0, q)], mate_y)

        def y_end(k):
            return send(k, 1, big.at[g_rows(k, q * yy, q)], recv.at[in_rows(k, q, q)], mate_e)

        def y_mid(k):
            return send(k, 2, big.at[g_rows(k, q * yy, q)], recv.at[in_rows(k, 2 * q, q)], mate_m)

        def o_rows(k, lo, n):
            return gall_hbm.at[pl.ds(pl.multiple_of(k * (4 * q) + first + lo, 16), n)]

        def y_back(k):
            return send(k, 3, big.at[g_rows(k, q * yy, q)], o_rows(k, q * yy, q), mate_e)

        def y_share_mid(k):
            return send(k, 4, big.at[g_rows(k, q * yy, q)], o_rows(k, q * yy, q), mate_y)

        def y_share_end(k):
            return send(k, 4, o_rows(k, q * yy, q), o_rows(k, q * yy, q), mate_y)

        def z_end(k):
            return send(k, 5, big.at[g_rows(k, 2 * q, 2 * q)], recv.at[in_rows(k, 5 * q, 2 * q)], mate_e)

        def z_mid(k):
            return send(k, 6, big.at[g_rows(k, 3 * q - q * zm, q)], recv.at[in_rows(k, 3 * q, q)], mate_m)

        def z_swap(k):
            return send(k, 7, big.at[g_rows(k, 2 * q + q * zm, q)], recv.at[in_rows(k, 4 * q, q)], mate_y)

        def z_share(k):
            return send(k, 8, big.at[g_rows(k, 2 * q + q * zm, q)], o_rows(k, 2 * q + q * zm, q), mate_m)

        def z_back(k):
            return send(k, 9, big.at[g_rows(k, 2 * q + q * zm, q)], o_rows(k, 2 * q + q * zm, q), mate_e)

        def z_pass(k):
            return send(k, 10, o_rows(k, 3 * q - q * zm, q), o_rows(k, 3 * q - q * zm, q), mate_e)

        def accumulate(k, lo, n, at):
            rows = g_rows(k, lo, n)
            big[rows, :] = (big[rows, :].astype(f32) + recv[in_rows(k, at, n), :].astype(f32)).astype(bf16)

        def keep_y(k):
            return pltpu.make_async_copy(big.at[g_rows(k, q * yy, q)], o_rows(k, q * yy, q), s_out.at[0, k + number])

        def keep_z(k):
            return pltpu.make_async_copy(
                big.at[g_rows(k, 2 * q + q * zm, q)], o_rows(k, 2 * q + q * zm, q), s_out.at[1, k + number]
            )

        def hop0(k):
            y_swap(k).start()

            @pl.when(jnp.logical_not(middle))
            def _():
                z_end(k).start()

        def hop1(k):
            y_swap(k).wait()
            accumulate(k, q * yy, q, 0)

            @pl.when(middle)
            def _():
                z_end(k).wait_recv()
                accumulate(k, 2 * q, 2 * q, 5 * q)
                z_mid(k).start()

            @pl.when(jnp.logical_not(middle))
            def _():
                y_end(k).start()

        def hop2(k):
            @pl.when(middle)
            def _():
                y_end(k).wait_recv()
                accumulate(k, q * yy, q, q)
                y_mid(k).start()
                z_mid(k).wait()
                accumulate(k, 2 * q + q * zm, q, 3 * q)
                z_swap(k).start()

        def hop3(k):
            @pl.when(middle)
            def _():
                y_mid(k).wait()
                accumulate(k, q * yy, q, 2 * q)
                y_back(k).start()
                y_share_mid(k).start()
                keep_y(k).start()
                z_swap(k).wait()
                accumulate(k, 2 * q + q * zm, q, 4 * q)
                z_share(k).start()
                z_back(k).start()
                keep_z(k).start()

        def hop4(k):
            @pl.when(middle)
            def _():
                z_share(k).wait()
                z_pass(k).start()

            @pl.when(jnp.logical_not(middle))
            def _():
                y_end(k).wait_send()
                y_back(k).wait_recv()
                y_share_end(k).start()

        def hop5(k):
            @pl.when(middle)
            def _():
                y_share_mid(k).wait()
                y_back(k).wait_send()
                z_back(k).wait_send()
                z_pass(k).wait_send()
                keep_y(k).wait()
                keep_z(k).wait()

            @pl.when(jnp.logical_not(middle))
            def _():
                y_share_end(k).wait()
                z_end(k).wait_send()
                z_back(k).wait_recv()
                z_pass(k).wait_recv()

        hops = ((5, hop5), (4, hop4), (3, hop3), (2, hop2), (1, hop1), (0, hop0))

        def tick(t):
            for h, hop in hops:
                k = t - lag * h

                @pl.when((k >= 0) & (k < count_of))
                def _(hop=hop, k=k):
                    hop(k)

        return tick

    tick_mlp = pieces(32, 16, 0, 0, LAG)
    tick_attention = pieces(QB, 256 // QB, 2048, 16, LAG_END)

    def ticks(run, lo, hi):
        def step(t, carry):
            run(t)
            return carry

        lax.fori_loop(lo, hi, step, 0)

    for k in (0, 1, 2, 3):
        loads[k].wait()
    loads[4].start()
    loads[5].start()


    def attend(q, k, v, row_bias):
        o = jnp.zeros((PAD, 256), f32)
        for h in range(4):
            scores = nt(only(q, h), k) + row_bias
            e = jnp.exp(scores - jnp.max(scores, axis=1, keepdims=True))
            p = (e * (1.0 / jnp.sum(e, axis=1, keepdims=True))).astype(bf16)
            o = o + nn(p, only(v, h))
        return o.astype(bf16)

    def attention(i):
        start = pl.multiple_of(i * PAD, 16)
        for c in range(width // 128):
            xs[pl.ds(start, count), c * 128 : (c + 1) * 128] = h1s[c, pl.ds(i, count, stride=images), :].astype(bf16)
        for r in chunks():
            u, mean, s = stats(xs[chunk_of(i, r), :].astype(f32))
            col[chunk_of(i, r), 1:2] = mean
            col[chunk_of(i, r), 2:3] = s
            a2s[chunk_of(i, r), :] = (u * g1).astype(bf16)
        rows = rows_of(i)
        a1 = a2s[rows, :]
        qkv[rows, 0:256] = (nn(a1, wqkv[:, 0:256]) * 0.125).astype(bf16)
        qkv[rows, 256:512] = nn(a1, wqkv[:, 256:512]).astype(bf16)
        qkv[rows, 512:768] = nn(a1, wqkv[:, 512:768]).astype(bf16)
        os[rows, :] = attend(qkv[rows, 0:256], qkv[rows, 256:512], qkv[rows, 512:768], bias[i])

    def attention_sent(i):
        attention(i)
        ob = os[rows_of(i), :]
        for t in range(4):
            store_p(i, t, nn(ob, wo[:, t * TILE : (t + 1) * TILE]))

    attention_sent(0)

    pl.semaphore_wait(barrier, dps + 1)

    def learn_copy(k):
        return pltpu.make_async_remote_copy(
            src_ref=wl_part(dp), dst_ref=wl_part(dp),
            send_sem=slearn_s.at[k - 1], recv_sem=slearn_r.at[k - 1],
            device_id=(lax.rem(dp + k, dps), mp), device_id_type=MESH,
        )

    loads[6].wait()
    for k in range(1, dps):
        learn_copy(k).start()

    copy_core(0).start()
    stage(attention_sent, 1, images, far(0), begun=True)

    loads[4].wait()
    loads[5].wait()

    def mlp(i):
        for r in chunks():
            h1 = xs[chunk_of(i, r), :].astype(f32) + summed(i, r)
            put_wide(chunk_of(i, r), h1)
            u, mean, s = stats(h1)
            col[chunk_of(i, r), 3:4] = mean
            col[chunk_of(i, r), 4:5] = s
            a2s[chunk_of(i, r), :] = (u * g2).astype(bf16)
        rows = rows_of(i)
        a2 = a2s[rows, :]
        for t in range(4):
            cols = slice(t * TILE, (t + 1) * TILE)
            z = nn(a2, wup[:, cols])
            cdf, pdf = gauss(z)
            rs[rows, cols] = (z * cdf).astype(bf16)
            gs[rows, cols] = (cdf + z * pdf).astype(bf16)
        act = rs[rows, :]
        for t in range(4):
            store_p(i, t, nn(act, wdn[:, t * TILE : (t + 1) * TILE]))

    hop_three(0, 0)
    stage(mlp, 0, images, far(1), from_far(0))

    for k in range(1, dps):
        learn_copy(k).wait()
    dg[...] = jnp.zeros_like(dg)
    gl_sum[...] = jnp.zeros_like(gl_sum)
    gsel_sum[...] = jnp.zeros_like(gsel_sum)

    def y_out(i):
        return pltpu.make_async_copy(d1s.at[rows_of(i)], y_hbm.at[rows_of(i)], sy.at[i])

    def learner(i):
        rows = rows_of(i)
        for r in chunks():
            yb = (get_wide(chunk_of(i, r)) + summed(i, r)).astype(bf16)
            d1s[chunk_of(i, r), :] = yb
            v = yb.astype(f32)
            mean = jnp.sum(v, axis=-1, keepdims=True) * (1.0 / width)
            v = v - mean
            s = lax.rsqrt(jnp.sum(v * v, axis=-1, keepdims=True) * (1.0 / width) + 1e-06)
            centre[r : r + CH, :] = mean
            scale[r : r + CH, :] = s
            dhs[chunk_of(i, r), :] = (v * s * g3).astype(bf16)
        y_out(i).start()
        y = d1s[rows, :]
        a3 = dhs[rows, :]
        wlf = wl[...]
        wsel = wsel_ref[...]
        ct = ct_ref[i]
        zl = nt(a3, wlf)
        cdf, pdf = gauss(zl)
        t = (zl * cdf).astype(bf16)
        slope = cdf + zl * pdf
        col_bias = col[rows, 0:1]
        logits = nt(t, wsel) + col_bias
        e = jnp.exp(logits - jnp.max(logits, axis=0, keepdims=True))
        maps = e * (1.0 / jnp.sum(e, axis=0, keepdims=True))
        mb = maps.astype(bf16)
        learned_ref[i] = tn(mb, y).astype(bf16)
        dmaps = nt(y, ct)
        dlog = (maps * (dmaps - jnp.sum(maps * dmaps, axis=0, keepdims=True))).astype(bf16)
        gsel_sum[...] += tn(dlog, t)
        dzl = (nn(dlog, wsel) * slope).astype(bf16)
        gl_sum[...] += tn(dzl, a3)
        part_a[...] = nn(dzl, wlf)
        part_b[...] = nn(mb, ct)
        for r in chunks():
            da3 = part_a[r : r + CH, :]
            dy = part_b[r : r + CH, :]
            s = scale[r : r + CH, :]
            u = (d1s[chunk_of(i, r), :].astype(f32) - centre[r : r + CH, :]) * s
            dg[2] += fold(da3 * u)
            dhs[chunk_of(i, r), :] = (dy + back(da3 * g3, u, s)).astype(bf16)

    def mlp_back(i):
        rows = rows_of(i)
        dhb = dhs[rows, :]
        for c in range(4):
            cols = slice(c * TILE, (c + 1) * TILE)
            dr = nt(dhb, wdn[cols, :])
            gs[rows, cols] = (dr * gs[rows, cols].astype(f32)).astype(bf16)
        dz = gs[rows, :]
        for c in range(4):
            store_p(i, c, nt(dz, wup[c * TILE : (c + 1) * TILE, :]))

    early = images // 2

    def learner_mlp(i):
        learner(i)

        @pl.when(i < early)
        def _():
            mlp_back(i)
            copy_core(i).start()

        @pl.when((i > 0) & (i <= early))
        def _():
            hop_two(i - 1, 0)

    hop_three(0, 1)
    each(learner_mlp, 0, images, from_far(1))

    def grad(left, right, first, after):
        def step(j, carry):
            lhs = left[:, pl.ds(pl.multiple_of(j * TILE, TILE), TILE)]
            rows = g_tile(first + j)
            for c in range(0, width, TILE):
                big[rows, c : c + TILE] = tn(lhs, right[:, c : c + TILE]).astype(bf16)
            if after is not None:
                after(j)
            return carry

        lax.fori_loop(0, left.shape[1] // TILE, step, 0)

    def ready():
        pl.semaphore_signal(ready_y, inc=1, device_id=mate_y, device_id_type=MESH)

        @pl.when(middle)
        def _():
            pl.semaphore_signal(ready_z, inc=1, device_id=mate_e, device_id_type=MESH)
            pl.semaphore_signal(ready_z, inc=1, device_id=mate_m, device_id_type=MESH)

    def both_ready():
        pl.semaphore_wait(ready_y, 1)
        pl.semaphore_wait(ready_z, 1)

    grad(rs, dhs, 0, tick_mlp)

    def mlp_back_tick(i):
        mlp_back(i)
        tick_mlp(4 + i - early)

    stage(mlp_back_tick, early, images, far(0))
    def after_up(j):
        @pl.when(lax.rem(j, 2) == 1)
        def _():
            tick_mlp(8 + j // 2)

    ready()
    both_ready()
    grad(a2s, gs, 4, after_up)
    ready()
    for i in range(images):
        y_out(i).wait()

    def attention_back(i):
        rows = rows_of(i)
        for r in chunks():
            where = chunk_of(i, r)
            da2 = summed(i, r)
            s = col[where, 4:5]
            u = (get_wide(where) - col[where, 3:4]) * s
            dg[1] += fold(da2 * u)
            d1s[where, :] = (dhs[where, :].astype(f32) + back(da2 * g2, u, s)).astype(bf16)
            ux = (xs[where, :].astype(f32) - col[where, 1:2]) * col[where, 2:3]
            a2s[where, :] = (ux * g1).astype(bf16)
        d1 = d1s[rows, :]
        do = nt(d1, wo[...]).astype(bf16)
        q = qkv[rows, 0:256]
        k = qkv[rows, 256:512]
        v = qkv[rows, 512:768]
        col_bias = col[rows, 0:1]
        dq = jnp.zeros((PAD, 256), f32)
        dk = jnp.zeros((PAD, 256), f32)
        dv = jnp.zeros((PAD, 256), f32)
        for h in range(4):
            kh = only(k, h)
            scores = nt(kh, q) + col_bias
            e = jnp.exp(scores - jnp.max(scores, axis=0, keepdims=True))
            p = e * (1.0 / jnp.sum(e, axis=0, keepdims=True))
            dv = dv + nn(p.astype(bf16), only(do, h))
            dpr = nt(only(v, h), do)
            ds = (p * (dpr - jnp.sum(p * dpr, axis=0, keepdims=True))).astype(bf16)
            dk = dk + nn(ds, only(q, h))
            dq = dq + tn(ds, kh)
        qkv[rows, 0:256] = (dq * 0.125).astype(bf16)
        qkv[rows, 256:512] = dk.astype(bf16)
        qkv[rows, 512:768] = dv.astype(bf16)
        dall = qkv[rows, :]
        for c in range(4):
            store_p(i, c, nt(dall, wqkv[c * TILE : (c + 1) * TILE, :]))
        tick_mlp(10 + i)

    hop_three(0, 0)
    stage(attention_back, 0, images, far(1), from_far(0))
    both_ready()
    grad(os, d1s, 8, lambda j: tick_mlp(18))
    tick_attention(0)
    tick_attention(1)

    def grad_qkv(j, carry):
        lhs = a2s[:, pl.ds(pl.multiple_of(j * TILE, TILE), TILE)]
        for n in range(3):
            value = tn(lhs, qkv[:, n * TILE : (n + 1) * TILE]).astype(bf16)
            rows = pl.ds(pl.multiple_of(1280 + j * 192 + n * 64, 16), 64)
            for c in range(4):
                big[rows, c * TILE : (c + 1) * TILE] = value[c * 64 : (c + 1) * 64]
        tick_mlp(19 + j)
        tick_attention(2 + j)
        return carry

    lax.fori_loop(0, 4, grad_qkv, 0)

    def gp_out(i):
        return pltpu.make_async_copy(dhs.at[rows_of(i)], gp_hbm.at[rows_of(i)], sy.at[i])

    def finish(i, carry):
        @pl.when(i + 1 < images)
        def _():
            hop_three(i + 1, 1)
        arrived(i)
        for r in chunks():
            where = chunk_of(i, r)
            da1 = summed(i, r)
            s = col[where, 2:3]
            u = (xs[where, :].astype(f32) - col[where, 1:2]) * s
            dg[0] += fold(da1 * u)
            dhs[where, :] = (d1s[where, :].astype(f32) + back(da1 * g1, u, s)).astype(bf16)
        gp_out(i).start()
        tick_mlp(23 + i)
        tick_attention(6 + i)
        return carry

    hop_three(0, 1)
    lax.fori_loop(0, images, finish, 0)

    small_mine[0:8, :] = jnp.concatenate(
        [jnp.sum(dg[n], axis=0, keepdims=True) for n in range(3)] + [jnp.zeros((5, width), f32)], axis=0
    ).astype(bf16)
    small_mine[8:16, 0:64] = gsel_sum[...].astype(bf16)
    small_mine[8:16, 64:width] = jnp.zeros((8, width - 64), bf16)
    gl_mine[...] = gl_sum[...].astype(bf16)
    part = wl_hbm.shape[1]

    def gl_part(d):
        return pl.ds(pl.multiple_of(d * part, 128), part)

    def small_copy(k):
        peer = lax.rem(dp + k, dps)
        return (
            pltpu.make_async_remote_copy(
                src_ref=small_mine, dst_ref=small_in.at[k - 1], send_sem=s_small.at[0, k - 1],
                recv_sem=r_small.at[0, k - 1], device_id=(peer, mp), device_id_type=MESH,
            ),
            pltpu.make_async_remote_copy(
                src_ref=gl_mine.at[:, gl_part(peer)], dst_ref=gl_in.at[k - 1], send_sem=s_small.at[1, k - 1],
                recv_sem=r_small.at[1, k - 1], device_id=(peer, mp), device_id_type=MESH,
            ),
        )

    for k in range(1, dps):
        for copy in small_copy(k):
            copy.start()
    ticks(tick_mlp, 31, 16 + 5 * LAG)
    ticks(tick_attention, 14, 16)
    for k in range(1, dps):
        for copy in small_copy(k):
            copy.wait()
    small_ref[...] = small_mine[...].astype(f32)
    gl_ref[...] = gl_mine[:, gl_part(dp)].astype(f32)
    for k in range(dps - 1):
        small_ref[...] += small_in[k].astype(f32)
        gl_ref[...] += gl_in[k].astype(f32)
    ticks(tick_attention, 16, 256 // QB + 5 * LAG_END)
    for i in range(images):
        gp_out(i).wait()


def finish_up(
    gall, y, gp, learned, small, gl,
    learned_ref, y_ref, gp_ref, gq_ref, gk_ref, gv_ref, gout_ref, gup_ref, gdn_ref, d1_ref, d2_ref, d3_ref,
    gl_ref, gsel_ref,
    tiles, y_in, gp_in, wide, square, y_turned, gp_turned, strip, s_tile, s_in, s_wide, s_square, s_turned,
):
    count = y_ref.shape[0]

    def tile_in(j):
        rows = pl.ds(j * TILE, TILE)
        return pltpu.make_async_copy(gall.at[rows], tiles.at[rows], s_tile.at[j])

    ins = [pltpu.make_async_copy(y, y_in, s_in.at[0]), pltpu.make_async_copy(gp, gp_in, s_in.at[1])]
    queue = [tile_in(j) for j in range(5)] + ins[:1] + [tile_in(j) for j in range(5, 9)] + ins[1:]
    queue += [tile_in(j) for j in range(9, 12)]
    outs = []

    def begin(n):
        for _ in range(n):
            if queue:
                queue.pop(0).start()

    def tile_out(j):
        tile_in(j).wait()
        begin(1)
        rows = slice(j * TILE, (j + 1) * TILE)
        wide[rows, :] = tiles[rows, :].astype(f32)
        ref, first = ((gdn_ref, 0), (gup_ref, 4), (gout_ref, 8))[j // 4]
        copy = pltpu.make_async_copy(
            wide.at[pl.ds(j * TILE, TILE)], ref.at[pl.ds((j - first) * TILE, TILE)], s_wide.at[j]
        )
        copy.start()
        outs.append(copy)

    def turn(n, src, dst, ref):
        ins[n].wait()
        begin(2)
        for block in range(0, count, CH):
            rows = min(CH, count - block)
            for c in range(src.shape[2] // 128):
                cols = slice(c * 128, (c + 1) * 128)
                slot = strip.at[c]
                slot[...] = src[:, block : block + CH, cols].astype(f32).reshape(slot.shape)
                for r in range(rows):
                    dst[block + r, :, cols] = slot[pl.ds(r, dst.shape[1], stride=CH), :].astype(bf16)
            copy = pltpu.make_async_copy(
                dst.at[pl.ds(block, rows)], ref.at[pl.ds(block, rows)], s_turned.at[n, block // CH]
            )
            copy.start()
            outs.append(copy)

    begin(AHEAD)
    for j in range(6):
        tile_out(j)
    turn(0, y_in, y_turned, y_ref)
    for j in range(6, 9):
        tile_out(j)
    turn(1, gp_in, gp_turned, gp_ref)
    begin(len(queue))
    for j in range(9, 12):
        tile_in(j).wait()
    for n, ref in enumerate((gq_ref, gk_ref, gv_ref)):
        for j in range(4):
            for c in range(4):
                square[n, j * TILE + c * 64 : j * TILE + (c + 1) * 64, :] = tiles[
                    9 * TILE + j * 192 + n * 64 : 9 * TILE + j * 192 + (n + 1) * 64, c * TILE : (c + 1) * TILE
                ].astype(f32)
        copy = pltpu.make_async_copy(square.at[n], ref, s_square.at[n])
        copy.start()
        outs.append(copy)
    learned_ref[...] = learned[...]
    for n, ref in enumerate((d1_ref, d2_ref, d3_ref)):
        ref[...] = small[n : n + 1, :]
    gl_ref[...] = gl[...]
    gsel_ref[...] = small[8:16, 0 : gsel_ref.shape[1]]
    for copy in outs:
        copy.wait()


def local_fused(
    patches, keep_mask, w_query, w_key, w_value, w_out, w_up, w_down,
    gain_attn, gain_mlp, gain_learn, w_learn, w_select, cotangent,
):
    images, count, width = patches.shape
    total = images * PAD
    hidden = w_up.shape[1]
    learn_rows, learn_cols = w_learn.shape
    dps = lax.axis_size("dp")
    anywhere = pl.BlockSpec(memory_space=pl.ANY)
    vmem = pl.BlockSpec(memory_space=pltpu.VMEM)
    sds = jax.ShapeDtypeStruct
    dma = pltpu.SemaphoreType.DMA
    outs = pl.pallas_call(
        fused,
        name="block",
        out_shape=(
            sds((images, 8, width), bf16),
            sds((total, width), bf16),
            sds((total, width), bf16),
            sds((3072, width), bf16),
            sds((16, width), f32),
            sds((learn_cols, learn_rows), f32),
        ),
        in_specs=[anywhere, vmem] + [anywhere] * 6 + [vmem] * 3 + [anywhere] + [vmem] * 2,
        out_specs=(vmem,) + (anywhere,) * 3 + (vmem,) * 2,
        scratch_shapes=[
            pltpu.VMEM((images, 1, PAD), f32),
            pltpu.VMEM((width, 768), bf16),
            pltpu.VMEM((256, width), bf16),
            pltpu.VMEM((learn_cols, width), bf16),
            pltpu.VMEM((total, width), bf16),
            pltpu.VMEM((total, 768), bf16),
            pltpu.VMEM((total, 256), bf16),
            pltpu.VMEM((width // 128, total, 128), f32),
            pltpu.VMEM((total, width), bf16),
            pltpu.VMEM((total, width), bf16),
            pltpu.VMEM((total, width), bf16),
            pltpu.VMEM((3072, width), bf16),
            pltpu.VMEM((8 * PAIR_IN + total + 2 * width, width), bf16),
            pltpu.VMEM((2, total, width // 2), bf16),
            pltpu.VMEM((total, width // 2), bf16),
            pltpu.VMEM((2, total, width // 2), bf16),
            pltpu.VMEM((2, total, width // 2), bf16),
            pltpu.VMEM((3, 8, width), f32),
            pltpu.VMEM((learn_cols, width), f32),
            pltpu.VMEM((8, learn_cols), f32),
            pltpu.VMEM((learn_cols, width), bf16),
            pltpu.VMEM((dps - 1, learn_cols, learn_rows), bf16),
            pltpu.VMEM((16, width), bf16),
            pltpu.VMEM((dps - 1, 16, width), bf16),
            pltpu.VMEM((total, 8), f32),
            pltpu.VMEM((PAD, 1), f32),
            pltpu.VMEM((PAD, 1), f32),
            pltpu.VMEM((PAD, width), f32),
            pltpu.VMEM((PAD, width), f32),
            dma((4,)), dma((7,)), dma((images,)), dma((dps - 1,)), dma((dps - 1,)),
            dma((images,)), dma((images,)), dma((images,)), dma((2, images)), dma((images,)), dma((images,)),
            dma((11, 16 + 256 // QB)), dma((11, 16 + 256 // QB)), dma((2, 16 + 256 // QB)),
            pltpu.SemaphoreType.REGULAR, pltpu.SemaphoreType.REGULAR, dma((2, dps - 1)), dma((2, dps - 1)),
        ],
        compiler_params=pltpu.CompilerParams(
            collective_id=0, has_side_effects=True, vmem_limit_bytes=60 * 2**20
        ),
    )(
        patches.transpose(1, 0, 2).reshape(count * images, width), keep_mask, w_query, w_key, w_value, w_out, w_up, w_down,
        gain_attn[None], gain_mlp[None], gain_learn[None], w_learn.T, w_select.T, cotangent,
    )
    learned, y, gpat, gall, small, gl = outs

    square = (width, TILE)
    row = (1, width)
    blocks = -(-count // CH)
    outs = pl.pallas_call(
        finish_up,
        name="finish",
        out_shape=(
            sds((images, 8, width), bf16), sds((count, images, width), bf16), sds((count, images, width), bf16),
            sds(square, f32), sds(square, f32), sds(square, f32),
            sds((TILE, width), f32), sds((width, hidden), f32), sds((hidden, width), f32),
            sds(row, f32), sds(row, f32), sds(row, f32),
            sds((learn_cols, learn_rows), f32), sds((8, learn_cols), f32),
        ),
        in_specs=[anywhere] * 3 + [vmem] * 3,
        out_specs=(vmem,) + (anywhere,) * 8 + (vmem,) * 5,
        scratch_shapes=[
            pltpu.VMEM((3072, width), bf16),
            pltpu.VMEM((images, PAD, width), bf16),
            pltpu.VMEM((images, PAD, width), bf16),
            pltpu.VMEM((9 * TILE, width), f32),
            pltpu.VMEM((3,) + square, f32),
            pltpu.VMEM((count, images, width), bf16),
            pltpu.VMEM((count, images, width), bf16),
            pltpu.VMEM((width // 128, images * CH, 128), f32),
            dma((12,)), dma((2,)), dma((9,)), dma((3,)), dma((2, blocks)),
        ],
        compiler_params=pltpu.CompilerParams(vmem_limit_bytes=60 * 2**20),
    )(gall, y.reshape(images, PAD, width), gpat.reshape(images, PAD, width), learned, small, gl)
    learned, y, gpat, gq, gk, gv, gout, gup, gdn, d1, d2, d3, gl, gsel = outs
    return (
        learned, y.transpose(1, 0, 2), gpat.transpose(1, 0, 2), gq, gk, gv, gout, gup, gdn,
        d1[0], d2[0], d3[0], gl.T, gsel.T,
    )


def solution(mesh):
    small = mesh.shape["dp"] == 8 and mesh.shape["mp"] == 4
    return jax.shard_map(
        local_fused if small else local,
        mesh=mesh,
        in_specs=(
            P("dp", None, None),
            P("dp", None),
            P(None, "mp"),
            P(None, "mp"),
            P(None, "mp"),
            P("mp", None),
            P(None, "mp"),
            P("mp", None),
            P(),
            P(),
            P(),
            P("dp", None),
            P(),
            P("dp", None, None),
        ),
        out_specs=(
            P("dp", None, None),
            P("dp", None, None),
            P("dp", None, None),
            P(None, "mp"),
            P(None, "mp"),
            P(None, "mp"),
            P("mp", None),
            P(None, "mp"),
            P("mp", None),
            P(),
            P(),
            P(),
            P("dp", None),
            P(),
        ),
        check_vma=False,
    )
```

```python
import math

import jax
import jax.numpy as jnp
from jax import lax
from jax.experimental import pallas as pl
from jax.experimental.pallas import tpu as pltpu
from jax.sharding import PartitionSpec as P

D = 1024
HEADS = 16


def product(left, right):
    return jnp.dot(left, right, preferred_element_type=jnp.float32)


def contract_rows(left, right):
    return lax.dot_general(
        left, right, (((0,), (0,)), ((), ())), preferred_element_type=jnp.float32
    )


def contract_cols(left, right):
    return lax.dot_general(
        left, right, (((1,), (1,)), ((), ())), preferred_element_type=jnp.float32
    )


def normalize(inputs):
    row_mean = jnp.mean(inputs, axis=-1, keepdims=True)
    centered = inputs - row_mean
    inverse = lax.rsqrt(jnp.mean(centered * centered, axis=-1, keepdims=True) + 1e-06)
    return (centered * inverse, inverse)


def norm_back(grad_norm, normed, inverse, gain):
    scaled_grad = grad_norm * gain
    grad_input = inverse * (
        scaled_grad
        - jnp.mean(scaled_grad, axis=-1, keepdims=True)
        - normed * jnp.mean(scaled_grad * normed, axis=-1, keepdims=True)
    )
    return (grad_input, jnp.sum(grad_norm * normed, axis=0))


def gelu_exact(inputs):
    return jax.nn.gelu(inputs, approximate=False)


def gelu_back(hidden_pre, grad_act):
    _, pullback = jax.vjp(gelu_exact, hidden_pre)
    return pullback(grad_act)[0]


def local(
    patches,
    keep_mask,
    w_query,
    w_key,
    w_value,
    w_out,
    w_up,
    w_down,
    gain_attn,
    gain_mlp,
    gain_learn,
    w_learn,
    w_select,
    cotangent,
):
    images, patch_count, feature_count = patches.shape
    row_count = images * patch_count
    head_size = D // HEADS
    heads_here = w_query.shape[1] // head_size
    score_scale = 1.0 / math.sqrt(head_size)
    visible = keep_mask > 0
    head_shape = (images, patch_count, heads_here, head_size)
    residual_rows = patches.reshape(row_count, feature_count).astype(jnp.float32)
    normed_one, inverse_one = normalize(residual_rows)
    attn_input = (normed_one * gain_attn).astype(jnp.bfloat16)
    query_flat = product(attn_input, w_query).astype(jnp.bfloat16)
    key_flat = product(attn_input, w_key).astype(jnp.bfloat16)
    value_flat = product(attn_input, w_value).astype(jnp.bfloat16)
    query_heads = query_flat.reshape(head_shape)
    key_heads = key_flat.reshape(head_shape)
    value_heads = value_flat.reshape(head_shape)

    def masked_scores():
        raw_scores = (
            jnp.einsum(
                "bqhe,bkhe->bhqk", query_heads, key_heads, preferred_element_type=jnp.float32
            )
            * score_scale
        )
        return jnp.where(visible[:, None, None, :], raw_scores, -1e30)

    scores = masked_scores()
    top_score = jnp.max(scores, axis=-1, keepdims=True)
    exponent = jnp.exp(scores - top_score)
    denominator = jnp.sum(exponent, axis=-1, keepdims=True)
    logsum = top_score + jnp.log(denominator)
    probs_low = (exponent / denominator).astype(jnp.bfloat16)
    mixed_heads = jnp.einsum(
        "bhqk,bkhe->bqhe", probs_low, value_heads, preferred_element_type=jnp.float32
    )
    mixed_heads = mixed_heads.astype(jnp.bfloat16).reshape(row_count, heads_here * head_size)
    attn_term = product(mixed_heads, w_out)
    hidden_one = residual_rows + lax.psum(attn_term.astype(jnp.bfloat16), "mp").astype(jnp.float32)
    normed_two, inverse_two = normalize(hidden_one)
    mlp_input = (normed_two * gain_mlp).astype(jnp.bfloat16)
    hidden_pre = product(mlp_input, w_up)
    activated = gelu_exact(hidden_pre).astype(jnp.bfloat16)
    mlp_out = lax.psum(product(activated, w_down).astype(jnp.bfloat16), "mp").astype(jnp.float32)
    block_rows = (hidden_one + mlp_out).astype(jnp.bfloat16)
    normed_learn, inverse_learn = normalize(block_rows.astype(jnp.float32))
    learn_input = (normed_learn * gain_learn).astype(jnp.bfloat16)
    learn_full = lax.all_gather(w_learn, "dp", axis=0, tiled=True)
    learn_pre = product(learn_input, learn_full)
    learn_act = gelu_exact(learn_pre).astype(jnp.bfloat16)
    logits = product(learn_act, w_select).reshape(images, patch_count, -1)
    logits = jnp.where(visible[:, :, None], logits, -1e30)
    top_logit = jnp.max(logits, axis=1, keepdims=True)
    exp_logit = jnp.exp(logits - top_logit)
    token_maps = exp_logit / jnp.sum(exp_logit, axis=1, keepdims=True)
    maps_low = token_maps.astype(jnp.bfloat16)
    block_three = block_rows.reshape(images, patch_count, feature_count)
    learned = jnp.einsum(
        "bpn,bpd->bnd", maps_low, block_three, preferred_element_type=jnp.float32
    ).astype(jnp.bfloat16)
    grad_maps = jnp.einsum(
        "bnd,bpd->bpn", cotangent, block_three, preferred_element_type=jnp.float32
    )
    grad_block = jnp.einsum(
        "bpn,bnd->bpd", maps_low, cotangent, preferred_element_type=jnp.float32
    ).reshape(row_count, feature_count)
    grad_logits = token_maps * (grad_maps - jnp.sum(token_maps * grad_maps, axis=1, keepdims=True))
    grad_logits = grad_logits.reshape(row_count, -1).astype(jnp.bfloat16)
    grad_select = contract_rows(learn_act, grad_logits)
    grad_learn_act = contract_cols(grad_logits, w_select)
    grad_learn_pre = gelu_back(learn_pre, grad_learn_act).astype(jnp.bfloat16)
    grad_learn = contract_rows(learn_input, grad_learn_pre)
    grad_learn_input = contract_cols(grad_learn_pre, learn_full)
    grad_from_learn, grad_gain_learn = norm_back(
        grad_learn_input, normed_learn, inverse_learn, gain_learn
    )
    grad_hidden = grad_block + grad_from_learn
    grad_hidden_low = grad_hidden.astype(jnp.bfloat16)
    grad_down = contract_rows(activated, grad_hidden_low)
    grad_act = contract_cols(grad_hidden_low, w_down)
    grad_pre = gelu_back(hidden_pre, grad_act).astype(jnp.bfloat16)
    grad_up = contract_rows(mlp_input, grad_pre)
    mlp_back_term = contract_cols(grad_pre, w_up)
    grad_mlp_input = lax.psum(mlp_back_term.astype(jnp.bfloat16), "mp").astype(jnp.float32)
    grad_from_two, grad_gain_mlp = norm_back(grad_mlp_input, normed_two, inverse_two, gain_mlp)
    grad_hidden = grad_hidden + grad_from_two
    grad_attn_low = grad_hidden.astype(jnp.bfloat16)
    grad_out = contract_rows(mixed_heads, grad_attn_low)
    grad_mixed = contract_cols(grad_attn_low, w_out).astype(jnp.bfloat16).reshape(head_shape)
    probs_again = jnp.exp(masked_scores() - logsum)
    probs_again_low = probs_again.astype(jnp.bfloat16)
    grad_probs = jnp.einsum(
        "bqhe,bkhe->bhqk", grad_mixed, value_heads, preferred_element_type=jnp.float32
    )
    grad_value_heads = jnp.einsum(
        "bhqk,bqhe->bkhe", probs_again_low, grad_mixed, preferred_element_type=jnp.float32
    ).astype(jnp.bfloat16)
    grad_scores = probs_again * (
        grad_probs - jnp.sum(probs_again * grad_probs, axis=-1, keepdims=True)
    )
    grad_scores = grad_scores.astype(jnp.bfloat16)
    grad_query_heads = (
        jnp.einsum("bhqk,bkhe->bqhe", grad_scores, key_heads, preferred_element_type=jnp.float32)
        * score_scale
    ).astype(jnp.bfloat16)
    grad_key_heads = (
        jnp.einsum("bhqk,bqhe->bkhe", grad_scores, query_heads, preferred_element_type=jnp.float32)
        * score_scale
    ).astype(jnp.bfloat16)
    grad_query_flat = grad_query_heads.reshape(row_count, -1)
    grad_key_flat = grad_key_heads.reshape(row_count, -1)
    grad_value_flat = grad_value_heads.reshape(row_count, -1)
    grad_query = contract_rows(attn_input, grad_query_flat)
    grad_key = contract_rows(attn_input, grad_key_flat)
    grad_value = contract_rows(attn_input, grad_value_flat)
    attn_terms = (
        contract_cols(grad_query_flat, w_query)
        + contract_cols(grad_key_flat, w_key)
        + contract_cols(grad_value_flat, w_value)
    )
    grad_attn_input = lax.psum(attn_terms.astype(jnp.bfloat16), "mp").astype(jnp.float32)
    grad_from_one, grad_gain_attn = norm_back(grad_attn_input, normed_one, inverse_one, gain_attn)
    grad_patches = (
        (grad_hidden + grad_from_one)
        .astype(jnp.bfloat16)
        .reshape(images, patch_count, feature_count)
    )
    (
        grad_query,
        grad_key,
        grad_value,
        grad_out,
        grad_gain_attn,
        grad_up,
        grad_down,
        grad_gain_mlp,
        grad_gain_learn,
        grad_select,
        grad_learn,
    ) = (
        lax.psum(grad_query.astype(jnp.bfloat16), "dp").astype(jnp.float32),
        lax.psum(grad_key.astype(jnp.bfloat16), "dp").astype(jnp.float32),
        lax.psum(grad_value.astype(jnp.bfloat16), "dp").astype(jnp.float32),
        lax.psum(grad_out.astype(jnp.bfloat16), "dp").astype(jnp.float32),
        lax.psum(grad_gain_attn.astype(jnp.bfloat16), "dp").astype(jnp.float32),
        lax.psum(grad_up.astype(jnp.bfloat16), "dp").astype(jnp.float32),
        lax.psum(grad_down.astype(jnp.bfloat16), "dp").astype(jnp.float32),
        lax.psum(grad_gain_mlp.astype(jnp.bfloat16), "dp").astype(jnp.float32),
        lax.psum(grad_gain_learn.astype(jnp.bfloat16), "dp").astype(jnp.float32),
        lax.psum(grad_select.astype(jnp.bfloat16), "dp").astype(jnp.float32),
        lax.psum(grad_learn.astype(jnp.bfloat16), "dp").astype(jnp.float32),
    )
    learn_rows = w_learn.shape[0]
    grad_learn = lax.dynamic_slice_in_dim(
        grad_learn, lax.axis_index("dp") * learn_rows, learn_rows, 0
    )
    return (
        learned,
        block_three,
        grad_patches,
        grad_query,
        grad_key,
        grad_value,
        grad_out,
        grad_up,
        grad_down,
        grad_gain_attn,
        grad_gain_mlp,
        grad_gain_learn,
        grad_learn,
        grad_select,
    )


MESH = pl.DeviceIdType.MESH
PAD = 208
CH = 16
TILE = 256
PAIR_IN = 224
LAG = 2
LAG_END = 2
QB = 32
AHEAD = 7
f32 = jnp.float32
bf16 = jnp.bfloat16


def nn(a, b):
    return jnp.dot(a, b, preferred_element_type=f32)


def nt(a, b):
    return lax.dot_general(a, b, (((1,), (1,)), ((), ())), preferred_element_type=f32)


def tn(a, b):
    return lax.dot_general(a, b, (((0,), (0,)), ((), ())), preferred_element_type=f32)


def gauss(z):
    bell = jnp.exp(-0.5 * (z * z))
    t = 1.0 / (1.0 + 0.23164189 * jnp.abs(z))
    poly = t * (
        0.127414796 + t * (-0.142248368 + t * (0.7107068705 + t * (-0.7265760135 + t * 0.5307027145)))
    )
    tail = poly * bell
    return jnp.where(z >= 0, 1.0 - tail, tail), 0.3989422804014327 * bell


def stats(v):
    mean = jnp.sum(v, axis=-1, keepdims=True) * (1.0 / v.shape[-1])
    c = v - mean
    s = lax.rsqrt(jnp.sum(c * c, axis=-1, keepdims=True) * (1.0 / v.shape[-1]) + 1e-06)
    return c * s, mean, s


def back(e, u, s):
    width = 1.0 / e.shape[-1]
    return s * (
        e
        - jnp.sum(e, axis=-1, keepdims=True) * width
        - u * (jnp.sum(e * u, axis=-1, keepdims=True) * width)
    )


def fold(v):
    total = v[0:8]
    for r in range(8, v.shape[0], 8):
        total = total + v[r : r + 8]
    return total


def chunks():
    return range(0, PAD, CH)


def fused(
    patches, keep_ref, wq_hbm, wk_hbm, wv_hbm, wo_hbm, wup_hbm, wdn_hbm, g1_ref, g2_ref, g3_ref,
    wl_hbm, wsel_ref, ct_ref,
    learned_ref, y_hbm, gp_hbm, gall_hbm, small_ref, gl_ref,
    bias, wqkv, wo, wl,
    xs, qkv, os, h1s, a2s, dhs, d1s, big, recv,
    pbuf, rcore, rx, sumb, dg, gl_sum, gsel_sum, gl_mine, gl_in, small_mine, small_in, col, centre, scale, part_a, part_b,
    sx, sw, sy, slearn_s, slearn_r, s_core, r_core, s_x, r_x, s_ag, r_ag,
    s_pair, r_pair, s_out, ready_y, ready_z, s_small, r_small,
):
    images, count = keep_ref.shape
    width = patches.shape[1]
    half = width // 2
    dp = lax.axis_index("dp")
    mp = lax.axis_index("mp")
    core = lax.rem(mp, 2)
    mate = (dp, mp + 1 - 2 * core)
    across = (dp, lax.rem(mp + 2, 4))
    dps = lax.axis_size("dp")
    yy = lax.rem(dp, 2)
    zz = dp // 2
    middle = (zz == 1) | (zz == 2)
    zm = jnp.where(zz >= 2, 1, 0)
    mate_y = (dp + 1 - 2 * yy, mp)
    mate_e = ((zz + 1 - 2 * lax.rem(zz, 2)) * 2 + yy, mp)
    mate_m = ((3 - zz) * 2 + yy, mp)
    total = images * PAD
    kept = 8 * PAIR_IN
    rs = big.at[pl.ds(0, total)]
    wup = recv.at[pl.ds(kept, width)]
    wdn = recv.at[pl.ds(kept + width, width)]
    gs = recv.at[pl.ds(kept + 2 * width, total)]

    barrier = pltpu.get_barrier_semaphore()
    for device in (mate, across):
        pl.semaphore_signal(barrier, inc=1, device_id=device, device_id_type=MESH)
    for k in range(1, dps):
        pl.semaphore_signal(barrier, inc=1, device_id=(lax.rem(dp + k, dps), mp), device_id_type=MESH)

    def wl_part(d):
        return wl.at[:, pl.ds(pl.multiple_of(d * wl_hbm.shape[1], 128), wl_hbm.shape[1])]

    loads = [
        pltpu.make_async_copy(wq_hbm, wqkv.at[:, pl.ds(0, 256)], sw.at[0]),
        pltpu.make_async_copy(wk_hbm, wqkv.at[:, pl.ds(256, 256)], sw.at[1]),
        pltpu.make_async_copy(wv_hbm, wqkv.at[:, pl.ds(512, 256)], sw.at[2]),
        pltpu.make_async_copy(wo_hbm, wo, sw.at[3]),
        pltpu.make_async_copy(wup_hbm, wup, sw.at[4]),
        pltpu.make_async_copy(wdn_hbm, wdn, sw.at[5]),
        pltpu.make_async_copy(wl_hbm, wl_part(dp), sw.at[6]),
    ]

    load_x = [
        pltpu.make_async_copy(
            patches.at[:, pl.ds(c * TILE, TILE)], dhs.at[pl.ds(0, images * count), pl.ds(c * TILE, TILE)], sx.at[c]
        )
        for c in range(4)
    ]
    for copy in load_x:
        copy.start()
    for k in (0, 1, 2, 3, 6):
        loads[k].start()

    for i in range(images):
        xs[i * PAD + PAD - 16 : (i + 1) * PAD, :] = jnp.zeros((16, width), bf16)
    bias[...] = jnp.full(bias.shape, -1e30, f32)
    for i in range(images):
        bias[i, :, 0:count] = jnp.where(keep_ref[i : i + 1, :] > 0, 0.0, -1e30)
    turned = jnp.transpose(bias[...].reshape(images, PAD))
    for i in range(images):
        col[i * PAD : (i + 1) * PAD, 0:1] = turned[:, i : i + 1]
    for c in range(4):
        load_x[c].wait()
        for r in range(0, images * count, 8 * CH):
            top = min(r + 8 * CH, images * count)
            for n in (2 * c, 2 * c + 1):
                h1s[n, r:top, :] = dhs[r:top, n * 128 : (n + 1) * 128].astype(f32)

    g1 = g1_ref[...]
    g2 = g2_ref[...]
    g3 = g3_ref[...]
    lane_head = lax.broadcasted_iota(jnp.int32, (1, 256), 1) // 64

    def only(v, h):
        return jnp.where(lane_head == h, v, jnp.zeros_like(v))

    def put_wide(where, value):
        for c in range(width // 128):
            h1s[c, where, :] = value[:, c * 128 : (c + 1) * 128]

    def get_wide(where):
        return jnp.concatenate([h1s[c, where, :] for c in range(width // 128)], axis=1)

    def rows_of(i):
        return pl.ds(pl.multiple_of(i * PAD, 16), PAD)

    def chunk_of(i, r):
        return pl.ds(pl.multiple_of(i * PAD + r, 16), CH)

    def copy_core(i):
        return pltpu.make_async_remote_copy(
            src_ref=pbuf.at[1 - core, rows_of(i)], dst_ref=rcore.at[rows_of(i)],
            send_sem=s_core.at[i], recv_sem=r_core.at[i], device_id=mate, device_id_type=MESH,
        )

    def copy_x(i, par):
        return pltpu.make_async_remote_copy(
            src_ref=pbuf.at[core, rows_of(i)], dst_ref=rx.at[par, rows_of(i)],
            send_sem=s_x.at[i], recv_sem=r_x.at[par, i], device_id=across, device_id_type=MESH,
        )

    def copy_ag(i):
        return pltpu.make_async_remote_copy(
            src_ref=sumb.at[core, rows_of(i)], dst_ref=sumb.at[core, rows_of(i)],
            send_sem=s_ag.at[i], recv_sem=r_ag.at[i], device_id=mate, device_id_type=MESH,
        )

    def hop_two(i, par):
        copy_core(i).wait()
        rows = rows_of(i)
        pbuf[core, rows] = (pbuf[core, rows].astype(f32) + rcore[rows].astype(f32)).astype(bf16)
        copy_x(i, par).start()

    def hop_three(i, par):
        copy_x(i, par).wait()
        rows = rows_of(i)
        sumb[core, rows] = (pbuf[core, rows].astype(f32) + rx[par, rows].astype(f32)).astype(bf16)
        copy_ag(i).start()

    def arrived(i):
        copy_ag(i).wait()

    def summed(i, r):
        where = chunk_of(i, r)
        return jnp.concatenate([sumb[0, where].astype(f32), sumb[1, where].astype(f32)], axis=1)

    def store_p(i, t, value):
        pbuf[t // 2, rows_of(i), (t % 2) * TILE : (t % 2 + 1) * TILE] = value.astype(bf16)

    def stage(body, lo, hi, second, before=None, begun=False):
        def step(i, carry):
            if before is not None:
                before(i, hi)
            body(i)
            copy_core(i).start()

            @pl.when((i > lo) | begun)
            def _():
                second(i - 1)
            return carry

        lax.fori_loop(lo, hi, step, 0)
        second(hi - 1)

    def far(par):
        return lambda i: hop_two(i, par)

    def from_far(par):
        def before(i, hi):
            @pl.when(i + 1 < hi)
            def _():
                hop_three(i + 1, par)
            arrived(i)
        return before

    def each(body, lo, hi, before=None):
        def step(i, carry):
            if before is not None:
                before(i, hi)
            body(i)
            return carry

        lax.fori_loop(lo, hi, step, 0)

    def g_tile(j):
        return pl.ds(pl.multiple_of(lax.rem(j * TILE + 2048, 3072), 16), TILE)

    def pieces(q, count_of, first, number, lag):
        def g_rows(k, lo, n):
            return pl.ds(pl.multiple_of(lax.rem(k * (4 * q) + first + 2048, 3072) + lo, 16), n)

        def in_rows(k, lo, n):
            return pl.ds(pl.multiple_of(k * (7 * q) + first // 128 * PAIR_IN + lo, 16), n)

        def send(k, slot, src, dst, device):
            return pltpu.make_async_remote_copy(
                src_ref=src, dst_ref=dst, send_sem=s_pair.at[slot, k + number], recv_sem=r_pair.at[slot, k + number],
                device_id=device, device_id_type=MESH,
            )

        def y_swap(k):
            return send(k, 0, big.at[g_rows(k, q - q * yy, q)], recv.at[in_rows(k, 0, q)], mate_y)

        def y_end(k):
            return send(k, 1, big.at[g_rows(k, q * yy, q)], recv.at[in_rows(k, q, q)], mate_e)

        def y_mid(k):
            return send(k, 2, big.at[g_rows(k, q * yy, q)], recv.at[in_rows(k, 2 * q, q)], mate_m)

        def o_rows(k, lo, n):
            return gall_hbm.at[pl.ds(pl.multiple_of(k * (4 * q) + first + lo, 16), n)]

        def y_back(k):
            return send(k, 3, big.at[g_rows(k, q * yy, q)], o_rows(k, q * yy, q), mate_e)

        def y_share_mid(k):
            return send(k, 4, big.at[g_rows(k, q * yy, q)], o_rows(k, q * yy, q), mate_y)

        def y_share_end(k):
            return send(k, 4, o_rows(k, q * yy, q), o_rows(k, q * yy, q), mate_y)

        def z_end(k):
            return send(k, 5, big.at[g_rows(k, 2 * q, 2 * q)], recv.at[in_rows(k, 5 * q, 2 * q)], mate_e)

        def z_mid(k):
            return send(k, 6, big.at[g_rows(k, 3 * q - q * zm, q)], recv.at[in_rows(k, 3 * q, q)], mate_m)

        def z_swap(k):
            return send(k, 7, big.at[g_rows(k, 2 * q + q * zm, q)], recv.at[in_rows(k, 4 * q, q)], mate_y)

        def z_share(k):
            return send(k, 8, big.at[g_rows(k, 2 * q + q * zm, q)], o_rows(k, 2 * q + q * zm, q), mate_m)

        def z_back(k):
            return send(k, 9, big.at[g_rows(k, 2 * q + q * zm, q)], o_rows(k, 2 * q + q * zm, q), mate_e)

        def z_pass(k):
            return send(k, 10, o_rows(k, 3 * q - q * zm, q), o_rows(k, 3 * q - q * zm, q), mate_e)

        def accumulate(k, lo, n, at):
            rows = g_rows(k, lo, n)
            big[rows, :] = (big[rows, :].astype(f32) + recv[in_rows(k, at, n), :].astype(f32)).astype(bf16)

        def keep_y(k):
            return pltpu.make_async_copy(big.at[g_rows(k, q * yy, q)], o_rows(k, q * yy, q), s_out.at[0, k + number])

        def keep_z(k):
            return pltpu.make_async_copy(
                big.at[g_rows(k, 2 * q + q * zm, q)], o_rows(k, 2 * q + q * zm, q), s_out.at[1, k + number]
            )

        def hop0(k):
            y_swap(k).start()

            @pl.when(jnp.logical_not(middle))
            def _():
                z_end(k).start()

        def hop1(k):
            y_swap(k).wait()
            accumulate(k, q * yy, q, 0)

            @pl.when(middle)
            def _():
                z_end(k).wait_recv()
                accumulate(k, 2 * q, 2 * q, 5 * q)
                z_mid(k).start()

            @pl.when(jnp.logical_not(middle))
            def _():
                y_end(k).start()

        def hop2(k):
            @pl.when(middle)
            def _():
                y_end(k).wait_recv()
                accumulate(k, q * yy, q, q)
                y_mid(k).start()
                z_mid(k).wait()
                accumulate(k, 2 * q + q * zm, q, 3 * q)
                z_swap(k).start()

        def hop3(k):
            @pl.when(middle)
            def _():
                y_mid(k).wait()
                accumulate(k, q * yy, q, 2 * q)
                y_back(k).start()
                y_share_mid(k).start()
                keep_y(k).start()
                z_swap(k).wait()
                accumulate(k, 2 * q + q * zm, q, 4 * q)
                z_share(k).start()
                z_back(k).start()
                keep_z(k).start()

        def hop4(k):
            @pl.when(middle)
            def _():
                z_share(k).wait()
                z_pass(k).start()

            @pl.when(jnp.logical_not(middle))
            def _():
                y_end(k).wait_send()
                y_back(k).wait_recv()
                y_share_end(k).start()

        def hop5(k):
            @pl.when(middle)
            def _():
                y_share_mid(k).wait()
                y_back(k).wait_send()
                z_back(k).wait_send()
                z_pass(k).wait_send()
                keep_y(k).wait()
                keep_z(k).wait()

            @pl.when(jnp.logical_not(middle))
            def _():
                y_share_end(k).wait()
                z_end(k).wait_send()
                z_back(k).wait_recv()
                z_pass(k).wait_recv()

        hops = ((5, hop5), (4, hop4), (3, hop3), (2, hop2), (1, hop1), (0, hop0))

        def tick(t):
            for h, hop in hops:
                k = t - lag * h

                @pl.when((k >= 0) & (k < count_of))
                def _(hop=hop, k=k):
                    hop(k)

        return tick

    tick_mlp = pieces(32, 16, 0, 0, LAG)
    tick_attention = pieces(QB, 256 // QB, 2048, 16, LAG_END)

    def ticks(run, lo, hi):
        def step(t, carry):
            run(t)
            return carry

        lax.fori_loop(lo, hi, step, 0)

    for k in (0, 1, 2, 3):
        loads[k].wait()
    loads[4].start()
    loads[5].start()


    def attend(q, k, v, row_bias):
        o = jnp.zeros((PAD, 256), f32)
        for h in range(4):
            scores = nt(only(q, h), k) + row_bias
            e = jnp.exp(scores - jnp.max(scores, axis=1, keepdims=True))
            p = (e * (1.0 / jnp.sum(e, axis=1, keepdims=True))).astype(bf16)
            o = o + nn(p, only(v, h))
        return o.astype(bf16)

    def attention(i):
        start = pl.multiple_of(i * PAD, 16)
        for c in range(width // 128):
            xs[pl.ds(start, count), c * 128 : (c + 1) * 128] = h1s[c, pl.ds(i, count, stride=images), :].astype(bf16)
        for r in chunks():
            u, mean, s = stats(xs[chunk_of(i, r), :].astype(f32))
            col[chunk_of(i, r), 1:2] = mean
            col[chunk_of(i, r), 2:3] = s
            a2s[chunk_of(i, r), :] = (u * g1).astype(bf16)
        rows = rows_of(i)
        a1 = a2s[rows, :]
        qkv[rows, 0:256] = (nn(a1, wqkv[:, 0:256]) * 0.125).astype(bf16)
        qkv[rows, 256:512] = nn(a1, wqkv[:, 256:512]).astype(bf16)
        qkv[rows, 512:768] = nn(a1, wqkv[:, 512:768]).astype(bf16)
        os[rows, :] = attend(qkv[rows, 0:256], qkv[rows, 256:512], qkv[rows, 512:768], bias[i])

    def attention_sent(i):
        attention(i)
        ob = os[rows_of(i), :]
        for t in range(4):
            store_p(i, t, nn(ob, wo[:, t * TILE : (t + 1) * TILE]))

    attention_sent(0)

    pl.semaphore_wait(barrier, dps + 1)

    def learn_copy(k):
        return pltpu.make_async_remote_copy(
            src_ref=wl_part(dp), dst_ref=wl_part(dp),
            send_sem=slearn_s.at[k - 1], recv_sem=slearn_r.at[k - 1],
            device_id=(lax.rem(dp + k, dps), mp), device_id_type=MESH,
        )

    loads[6].wait()
    for k in range(1, dps):
        learn_copy(k).start()

    copy_core(0).start()
    hop_two(0, 0)
    stage(attention_sent, 1, images, far(0))

    loads[4].wait()
    loads[5].wait()

    def mlp(i):
        for r in chunks():
            h1 = xs[chunk_of(i, r), :].astype(f32) + summed(i, r)
            put_wide(chunk_of(i, r), h1)
            u, mean, s = stats(h1)
            col[chunk_of(i, r), 3:4] = mean
            col[chunk_of(i, r), 4:5] = s
            a2s[chunk_of(i, r), :] = (u * g2).astype(bf16)
        rows = rows_of(i)
        a2 = a2s[rows, :]
        for t in range(4):
            cols = slice(t * TILE, (t + 1) * TILE)
            z = nn(a2, wup[:, cols])
            cdf, pdf = gauss(z)
            rs[rows, cols] = (z * cdf).astype(bf16)
            gs[rows, cols] = (cdf + z * pdf).astype(bf16)
        act = rs[rows, :]
        for t in range(4):
            store_p(i, t, nn(act, wdn[:, t * TILE : (t + 1) * TILE]))

    hop_three(0, 0)
    stage(mlp, 0, images, far(1), from_far(0))

    for k in range(1, dps):
        learn_copy(k).wait()
    dg[...] = jnp.zeros_like(dg)
    gl_sum[...] = jnp.zeros_like(gl_sum)
    gsel_sum[...] = jnp.zeros_like(gsel_sum)

    def y_out(i):
        return pltpu.make_async_copy(d1s.at[rows_of(i)], y_hbm.at[rows_of(i)], sy.at[i])

    def learner(i):
        rows = rows_of(i)
        for r in chunks():
            yb = (get_wide(chunk_of(i, r)) + summed(i, r)).astype(bf16)
            d1s[chunk_of(i, r), :] = yb
            v = yb.astype(f32)
            mean = jnp.sum(v, axis=-1, keepdims=True) * (1.0 / width)
            v = v - mean
            s = lax.rsqrt(jnp.sum(v * v, axis=-1, keepdims=True) * (1.0 / width) + 1e-06)
            centre[r : r + CH, :] = mean
            scale[r : r + CH, :] = s
            dhs[chunk_of(i, r), :] = (v * s * g3).astype(bf16)
        y_out(i).start()
        y = d1s[rows, :]
        a3 = dhs[rows, :]
        wlf = wl[...]
        wsel = wsel_ref[...]
        ct = ct_ref[i]
        zl = nt(a3, wlf)
        cdf, pdf = gauss(zl)
        t = (zl * cdf).astype(bf16)
        slope = cdf + zl * pdf
        col_bias = col[rows, 0:1]
        logits = nt(t, wsel) + col_bias
        e = jnp.exp(logits - jnp.max(logits, axis=0, keepdims=True))
        maps = e * (1.0 / jnp.sum(e, axis=0, keepdims=True))
        mb = maps.astype(bf16)
        learned_ref[i] = tn(mb, y).astype(bf16)
        dmaps = nt(y, ct)
        dlog = (maps * (dmaps - jnp.sum(maps * dmaps, axis=0, keepdims=True))).astype(bf16)
        gsel_sum[...] += tn(dlog, t)
        dzl = (nn(dlog, wsel) * slope).astype(bf16)
        gl_sum[...] += tn(dzl, a3)
        part_a[...] = nn(dzl, wlf)
        part_b[...] = nn(mb, ct)
        for r in chunks():
            da3 = part_a[r : r + CH, :]
            dy = part_b[r : r + CH, :]
            s = scale[r : r + CH, :]
            u = (d1s[chunk_of(i, r), :].astype(f32) - centre[r : r + CH, :]) * s
            dg[2] += fold(da3 * u)
            dhs[chunk_of(i, r), :] = (dy + back(da3 * g3, u, s)).astype(bf16)

    def mlp_back(i):
        rows = rows_of(i)
        dhb = dhs[rows, :]
        for c in range(4):
            cols = slice(c * TILE, (c + 1) * TILE)
            dr = nt(dhb, wdn[cols, :])
            gs[rows, cols] = (dr * gs[rows, cols].astype(f32)).astype(bf16)
        dz = gs[rows, :]
        for c in range(4):
            store_p(i, c, nt(dz, wup[c * TILE : (c + 1) * TILE, :]))

    early = images // 2

    def learner_mlp(i):
        learner(i)

        @pl.when(i < early)
        def _():
            mlp_back(i)
            copy_core(i).start()

        @pl.when((i > 0) & (i <= early))
        def _():
            hop_two(i - 1, 0)

        @pl.when(i == images - 2)
        def _():
            hop_three(i + 1, 1)

    hop_three(0, 1)
    def before_learner(i, hi):
        @pl.when(i + 2 < hi)
        def _():
            hop_three(i + 1, 1)
        arrived(i)

    each(learner_mlp, 0, images, before_learner)

    def grad(left, right, first, after):
        def step(j, carry):
            lhs = left[:, pl.ds(pl.multiple_of(j * TILE, TILE), TILE)]
            rows = g_tile(first + j)
            for c in range(0, width, TILE):
                big[rows, c : c + TILE] = tn(lhs, right[:, c : c + TILE]).astype(bf16)
            if after is not None:
                after(j)
            return carry

        lax.fori_loop(0, left.shape[1] // TILE, step, 0)

    def ready():
        pl.semaphore_signal(ready_y, inc=1, device_id=mate_y, device_id_type=MESH)

        @pl.when(middle)
        def _():
            pl.semaphore_signal(ready_z, inc=1, device_id=mate_e, device_id_type=MESH)
            pl.semaphore_signal(ready_z, inc=1, device_id=mate_m, device_id_type=MESH)

    def both_ready():
        pl.semaphore_wait(ready_y, 1)
        pl.semaphore_wait(ready_z, 1)

    grad(rs, dhs, 0, tick_mlp)

    def mlp_back_tick(i):
        mlp_back(i)
        tick_mlp(4 + i - early)

    stage(mlp_back_tick, early, images, far(0))
    def after_up(j):
        @pl.when(lax.rem(j, 2) == 1)
        def _():
            tick_mlp(8 + j // 2)

    ready()
    both_ready()
    grad(a2s, gs, 4, after_up)
    ready()
    for i in range(images):
        y_out(i).wait()

    def attention_back(i):
        rows = rows_of(i)
        for r in chunks():
            where = chunk_of(i, r)
            da2 = summed(i, r)
            s = col[where, 4:5]
            u = (get_wide(where) - col[where, 3:4]) * s
            dg[1] += fold(da2 * u)
            d1s[where, :] = (dhs[where, :].astype(f32) + back(da2 * g2, u, s)).astype(bf16)
            ux = (xs[where, :].astype(f32) - col[where, 1:2]) * col[where, 2:3]
            a2s[where, :] = (ux * g1).astype(bf16)
        d1 = d1s[rows, :]
        do = nt(d1, wo[...]).astype(bf16)
        q = qkv[rows, 0:256]
        k = qkv[rows, 256:512]
        v = qkv[rows, 512:768]
        col_bias = col[rows, 0:1]
        dq = jnp.zeros((PAD, 256), f32)
        dk = jnp.zeros((PAD, 256), f32)
        dv = jnp.zeros((PAD, 256), f32)
        for h in range(4):
            kh = only(k, h)
            scores = nt(kh, q) + col_bias
            e = jnp.exp(scores - jnp.max(scores, axis=0, keepdims=True))
            p = e * (1.0 / jnp.sum(e, axis=0, keepdims=True))
            dv = dv + nn(p.astype(bf16), only(do, h))
            dpr = nt(only(v, h), do)
            ds = (p * (dpr - jnp.sum(p * dpr, axis=0, keepdims=True))).astype(bf16)
            dk = dk + nn(ds, only(q, h))
            dq = dq + tn(ds, kh)
        qkv[rows, 0:256] = (dq * 0.125).astype(bf16)
        qkv[rows, 256:512] = dk.astype(bf16)
        qkv[rows, 512:768] = dv.astype(bf16)
        dall = qkv[rows, :]
        for c in range(4):
            store_p(i, c, nt(dall, wqkv[c * TILE : (c + 1) * TILE, :]))
        tick_mlp(10 + i)

    hop_three(0, 0)
    stage(attention_back, 0, images, far(1), from_far(0))
    both_ready()
    grad(os, d1s, 8, lambda j: tick_mlp(18))
    tick_attention(0)
    tick_attention(1)

    def grad_qkv(j, carry):
        lhs = a2s[:, pl.ds(pl.multiple_of(j * TILE, TILE), TILE)]
        for n in range(3):
            value = tn(lhs, qkv[:, n * TILE : (n + 1) * TILE]).astype(bf16)
            rows = pl.ds(pl.multiple_of(1280 + j * 192 + n * 64, 16), 64)
            for c in range(4):
                big[rows, c * TILE : (c + 1) * TILE] = value[c * 64 : (c + 1) * 64]
        tick_mlp(19 + j)
        tick_attention(2 + j)
        return carry

    lax.fori_loop(0, 4, grad_qkv, 0)

    def gp_out(i):
        return pltpu.make_async_copy(dhs.at[rows_of(i)], gp_hbm.at[rows_of(i)], sy.at[i])

    def finish(i, carry):
        @pl.when(i + 1 < images)
        def _():
            hop_three(i + 1, 1)
        arrived(i)
        for r in chunks():
            where = chunk_of(i, r)
            da1 = summed(i, r)
            s = col[where, 2:3]
            u = (xs[where, :].astype(f32) - col[where, 1:2]) * s
            dg[0] += fold(da1 * u)
            dhs[where, :] = (d1s[where, :].astype(f32) + back(da1 * g1, u, s)).astype(bf16)
        gp_out(i).start()
        tick_mlp(23 + i)
        tick_attention(6 + i)
        return carry

    hop_three(0, 1)
    lax.fori_loop(0, images, finish, 0)

    small_mine[0:8, :] = jnp.concatenate(
        [jnp.sum(dg[n], axis=0, keepdims=True) for n in range(3)] + [jnp.zeros((5, width), f32)], axis=0
    ).astype(bf16)
    small_mine[8:16, 0:64] = gsel_sum[...].astype(bf16)
    small_mine[8:16, 64:width] = jnp.zeros((8, width - 64), bf16)
    gl_mine[...] = gl_sum[...].astype(bf16)
    part = wl_hbm.shape[1]

    def gl_part(d):
        return pl.ds(pl.multiple_of(d * part, 128), part)

    def small_copy(k):
        peer = lax.rem(dp + k, dps)
        return (
            pltpu.make_async_remote_copy(
                src_ref=small_mine, dst_ref=small_in.at[k - 1], send_sem=s_small.at[0, k - 1],
                recv_sem=r_small.at[0, k - 1], device_id=(peer, mp), device_id_type=MESH,
            ),
            pltpu.make_async_remote_copy(
                src_ref=gl_mine.at[:, gl_part(peer)], dst_ref=gl_in.at[k - 1], send_sem=s_small.at[1, k - 1],
                recv_sem=r_small.at[1, k - 1], device_id=(peer, mp), device_id_type=MESH,
            ),
        )

    for k in range(1, dps):
        for copy in small_copy(k):
            copy.start()
    ticks(tick_mlp, 31, 16 + 5 * LAG)
    ticks(tick_attention, 14, 16)
    for k in range(1, dps):
        for copy in small_copy(k):
            copy.wait()
    small_ref[...] = small_mine[...].astype(f32)
    gl_ref[...] = gl_mine[:, gl_part(dp)].astype(f32)
    for k in range(dps - 1):
        small_ref[...] += small_in[k].astype(f32)
        gl_ref[...] += gl_in[k].astype(f32)
    ticks(tick_attention, 16, 256 // QB + 5 * LAG_END)
    for i in range(images):
        gp_out(i).wait()


def finish_up(
    gall, y, gp, learned, small, gl,
    learned_ref, y_ref, gp_ref, gq_ref, gk_ref, gv_ref, gout_ref, gup_ref, gdn_ref, d1_ref, d2_ref, d3_ref,
    gl_ref, gsel_ref,
    tiles, y_in, gp_in, wide, square, y_turned, gp_turned, strip, s_tile, s_in, s_wide, s_square, s_turned,
):
    count = y_ref.shape[0]

    def tile_in(j):
        rows = pl.ds(j * TILE, TILE)
        return pltpu.make_async_copy(gall.at[rows], tiles.at[rows], s_tile.at[j])

    ins = [pltpu.make_async_copy(y, y_in, s_in.at[0]), pltpu.make_async_copy(gp, gp_in, s_in.at[1])]
    queue = [tile_in(j) for j in range(5)] + ins[:1] + [tile_in(j) for j in range(5, 9)] + ins[1:]
    queue += [tile_in(j) for j in range(9, 12)]
    outs = []

    def begin(n):
        for _ in range(n):
            if queue:
                queue.pop(0).start()

    def tile_out(j):
        tile_in(j).wait()
        begin(1)
        rows = slice(j * TILE, (j + 1) * TILE)
        wide[rows, :] = tiles[rows, :].astype(f32)
        ref, first = ((gdn_ref, 0), (gup_ref, 4), (gout_ref, 8))[j // 4]
        copy = pltpu.make_async_copy(
            wide.at[pl.ds(j * TILE, TILE)], ref.at[pl.ds((j - first) * TILE, TILE)], s_wide.at[j]
        )
        copy.start()
        outs.append(copy)

    def turn(n, src, dst, ref):
        ins[n].wait()
        begin(2)
        for block in range(0, count, CH):
            rows = min(CH, count - block)
            for c in range(src.shape[2] // 128):
                cols = slice(c * 128, (c + 1) * 128)
                slot = strip.at[c]
                slot[...] = src[:, block : block + CH, cols].astype(f32).reshape(slot.shape)
                for r in range(rows):
                    dst[block + r, :, cols] = slot[pl.ds(r, dst.shape[1], stride=CH), :].astype(bf16)
            copy = pltpu.make_async_copy(
                dst.at[pl.ds(block, rows)], ref.at[pl.ds(block, rows)], s_turned.at[n, block // CH]
            )
            copy.start()
            outs.append(copy)

    begin(AHEAD)
    for j in range(6):
        tile_out(j)
    turn(0, y_in, y_turned, y_ref)
    for j in range(6, 9):
        tile_out(j)
    turn(1, gp_in, gp_turned, gp_ref)
    begin(len(queue))
    for j in range(9, 12):
        tile_in(j).wait()
    for n, ref in enumerate((gq_ref, gk_ref, gv_ref)):
        for j in range(4):
            for c in range(4):
                square[n, j * TILE + c * 64 : j * TILE + (c + 1) * 64, :] = tiles[
                    9 * TILE + j * 192 + n * 64 : 9 * TILE + j * 192 + (n + 1) * 64, c * TILE : (c + 1) * TILE
                ].astype(f32)
        copy = pltpu.make_async_copy(square.at[n], ref, s_square.at[n])
        copy.start()
        outs.append(copy)
    learned_ref[...] = learned[...]
    for n, ref in enumerate((d1_ref, d2_ref, d3_ref)):
        ref[...] = small[n : n + 1, :]
    gl_ref[...] = gl[...]
    gsel_ref[...] = small[8:16, 0 : gsel_ref.shape[1]]
    for copy in outs:
        copy.wait()


def local_fused(
    patches, keep_mask, w_query, w_key, w_value, w_out, w_up, w_down,
    gain_attn, gain_mlp, gain_learn, w_learn, w_select, cotangent,
):
    images, count, width = patches.shape
    total = images * PAD
    hidden = w_up.shape[1]
    learn_rows, learn_cols = w_learn.shape
    dps = lax.axis_size("dp")
    anywhere = pl.BlockSpec(memory_space=pl.ANY)
    vmem = pl.BlockSpec(memory_space=pltpu.VMEM)
    sds = jax.ShapeDtypeStruct
    dma = pltpu.SemaphoreType.DMA
    outs = pl.pallas_call(
        fused,
        name="block",
        out_shape=(
            sds((images, 8, width), bf16),
            sds((total, width), bf16),
            sds((total, width), bf16),
            sds((3072, width), bf16),
            sds((16, width), f32),
            sds((learn_cols, learn_rows), f32),
        ),
        in_specs=[anywhere, vmem] + [anywhere] * 6 + [vmem] * 3 + [anywhere] + [vmem] * 2,
        out_specs=(vmem,) + (anywhere,) * 3 + (vmem,) * 2,
        scratch_shapes=[
            pltpu.VMEM((images, 1, PAD), f32),
            pltpu.VMEM((width, 768), bf16),
            pltpu.VMEM((256, width), bf16),
            pltpu.VMEM((learn_cols, width), bf16),
            pltpu.VMEM((total, width), bf16),
            pltpu.VMEM((total, 768), bf16),
            pltpu.VMEM((total, 256), bf16),
            pltpu.VMEM((width // 128, total, 128), f32),
            pltpu.VMEM((total, width), bf16),
            pltpu.VMEM((total, width), bf16),
            pltpu.VMEM((total, width), bf16),
            pltpu.VMEM((3072, width), bf16),
            pltpu.VMEM((8 * PAIR_IN + total + 2 * width, width), bf16),
            pltpu.VMEM((2, total, width // 2), bf16),
            pltpu.VMEM((total, width // 2), bf16),
            pltpu.VMEM((2, total, width // 2), bf16),
            pltpu.VMEM((2, total, width // 2), bf16),
            pltpu.VMEM((3, 8, width), f32),
            pltpu.VMEM((learn_cols, width), f32),
            pltpu.VMEM((8, learn_cols), f32),
            pltpu.VMEM((learn_cols, width), bf16),
            pltpu.VMEM((dps - 1, learn_cols, learn_rows), bf16),
            pltpu.VMEM((16, width), bf16),
            pltpu.VMEM((dps - 1, 16, width), bf16),
            pltpu.VMEM((total, 8), f32),
            pltpu.VMEM((PAD, 1), f32),
            pltpu.VMEM((PAD, 1), f32),
            pltpu.VMEM((PAD, width), f32),
            pltpu.VMEM((PAD, width), f32),
            dma((4,)), dma((7,)), dma((images,)), dma((dps - 1,)), dma((dps - 1,)),
            dma((images,)), dma((images,)), dma((images,)), dma((2, images)), dma((images,)), dma((images,)),
            dma((11, 16 + 256 // QB)), dma((11, 16 + 256 // QB)), dma((2, 16 + 256 // QB)),
            pltpu.SemaphoreType.REGULAR, pltpu.SemaphoreType.REGULAR, dma((2, dps - 1)), dma((2, dps - 1)),
        ],
        compiler_params=pltpu.CompilerParams(
            collective_id=0, has_side_effects=True, vmem_limit_bytes=60 * 2**20
        ),
    )(
        patches.transpose(1, 0, 2).reshape(count * images, width), keep_mask, w_query, w_key, w_value, w_out, w_up, w_down,
        gain_attn[None], gain_mlp[None], gain_learn[None], w_learn.T, w_select.T, cotangent,
    )
    learned, y, gpat, gall, small, gl = outs

    square = (width, TILE)
    row = (1, width)
    blocks = -(-count // CH)
    outs = pl.pallas_call(
        finish_up,
        name="finish",
        out_shape=(
            sds((images, 8, width), bf16), sds((count, images, width), bf16), sds((count, images, width), bf16),
            sds(square, f32), sds(square, f32), sds(square, f32),
            sds((TILE, width), f32), sds((width, hidden), f32), sds((hidden, width), f32),
            sds(row, f32), sds(row, f32), sds(row, f32),
            sds((learn_cols, learn_rows), f32), sds((8, learn_cols), f32),
        ),
        in_specs=[anywhere] * 3 + [vmem] * 3,
        out_specs=(vmem,) + (anywhere,) * 8 + (vmem,) * 5,
        scratch_shapes=[
            pltpu.VMEM((3072, width), bf16),
            pltpu.VMEM((images, PAD, width), bf16),
            pltpu.VMEM((images, PAD, width), bf16),
            pltpu.VMEM((9 * TILE, width), f32),
            pltpu.VMEM((3,) + square, f32),
            pltpu.VMEM((count, images, width), bf16),
            pltpu.VMEM((count, images, width), bf16),
            pltpu.VMEM((width // 128, images * CH, 128), f32),
            dma((12,)), dma((2,)), dma((9,)), dma((3,)), dma((2, blocks)),
        ],
        compiler_params=pltpu.CompilerParams(vmem_limit_bytes=60 * 2**20),
    )(gall, y.reshape(images, PAD, width), gpat.reshape(images, PAD, width), learned, small, gl)
    learned, y, gpat, gq, gk, gv, gout, gup, gdn, d1, d2, d3, gl, gsel = outs
    return (
        learned, y.transpose(1, 0, 2), gpat.transpose(1, 0, 2), gq, gk, gv, gout, gup, gdn,
        d1[0], d2[0], d3[0], gl.T, gsel.T,
    )


def solution(mesh):
    small = mesh.shape["dp"] == 8 and mesh.shape["mp"] == 4
    return jax.shard_map(
        local_fused if small else local,
        mesh=mesh,
        in_specs=(
            P("dp", None, None),
            P("dp", None),
            P(None, "mp"),
            P(None, "mp"),
            P(None, "mp"),
            P("mp", None),
            P(None, "mp"),
            P("mp", None),
            P(),
            P(),
            P(),
            P("dp", None),
            P(),
            P("dp", None, None),
        ),
        out_specs=(
            P("dp", None, None),
            P("dp", None, None),
            P("dp", None, None),
            P(None, "mp"),
            P(None, "mp"),
            P(None, "mp"),
            P("mp", None),
            P(None, "mp"),
            P("mp", None),
            P(),
            P(),
            P(),
            P("dp", None),
            P(),
        ),
        check_vma=False,
    )
```

```python
import math

import jax
import jax.numpy as jnp
from jax import lax
from jax.experimental import pallas as pl
from jax.experimental.pallas import tpu as pltpu
from jax.sharding import PartitionSpec as P

D = 1024
HEADS = 16


def product(left, right):
    return jnp.dot(left, right, preferred_element_type=jnp.float32)


def contract_rows(left, right):
    return lax.dot_general(
        left, right, (((0,), (0,)), ((), ())), preferred_element_type=jnp.float32
    )


def contract_cols(left, right):
    return lax.dot_general(
        left, right, (((1,), (1,)), ((), ())), preferred_element_type=jnp.float32
    )


def normalize(inputs):
    row_mean = jnp.mean(inputs, axis=-1, keepdims=True)
    centered = inputs - row_mean
    inverse = lax.rsqrt(jnp.mean(centered * centered, axis=-1, keepdims=True) + 1e-06)
    return (centered * inverse, inverse)


def norm_back(grad_norm, normed, inverse, gain):
    scaled_grad = grad_norm * gain
    grad_input = inverse * (
        scaled_grad
        - jnp.mean(scaled_grad, axis=-1, keepdims=True)
        - normed * jnp.mean(scaled_grad * normed, axis=-1, keepdims=True)
    )
    return (grad_input, jnp.sum(grad_norm * normed, axis=0))


def gelu_exact(inputs):
    return jax.nn.gelu(inputs, approximate=False)


def gelu_back(hidden_pre, grad_act):
    _, pullback = jax.vjp(gelu_exact, hidden_pre)
    return pullback(grad_act)[0]


def local(
    patches,
    keep_mask,
    w_query,
    w_key,
    w_value,
    w_out,
    w_up,
    w_down,
    gain_attn,
    gain_mlp,
    gain_learn,
    w_learn,
    w_select,
    cotangent,
):
    images, patch_count, feature_count = patches.shape
    row_count = images * patch_count
    head_size = D // HEADS
    heads_here = w_query.shape[1] // head_size
    score_scale = 1.0 / math.sqrt(head_size)
    visible = keep_mask > 0
    head_shape = (images, patch_count, heads_here, head_size)
    residual_rows = patches.reshape(row_count, feature_count).astype(jnp.float32)
    normed_one, inverse_one = normalize(residual_rows)
    attn_input = (normed_one * gain_attn).astype(jnp.bfloat16)
    query_flat = product(attn_input, w_query).astype(jnp.bfloat16)
    key_flat = product(attn_input, w_key).astype(jnp.bfloat16)
    value_flat = product(attn_input, w_value).astype(jnp.bfloat16)
    query_heads = query_flat.reshape(head_shape)
    key_heads = key_flat.reshape(head_shape)
    value_heads = value_flat.reshape(head_shape)

    def masked_scores():
        raw_scores = (
            jnp.einsum(
                "bqhe,bkhe->bhqk", query_heads, key_heads, preferred_element_type=jnp.float32
            )
            * score_scale
        )
        return jnp.where(visible[:, None, None, :], raw_scores, -1e30)

    scores = masked_scores()
    top_score = jnp.max(scores, axis=-1, keepdims=True)
    exponent = jnp.exp(scores - top_score)
    denominator = jnp.sum(exponent, axis=-1, keepdims=True)
    logsum = top_score + jnp.log(denominator)
    probs_low = (exponent / denominator).astype(jnp.bfloat16)
    mixed_heads = jnp.einsum(
        "bhqk,bkhe->bqhe", probs_low, value_heads, preferred_element_type=jnp.float32
    )
    mixed_heads = mixed_heads.astype(jnp.bfloat16).reshape(row_count, heads_here * head_size)
    attn_term = product(mixed_heads, w_out)
    hidden_one = residual_rows + lax.psum(attn_term.astype(jnp.bfloat16), "mp").astype(jnp.float32)
    normed_two, inverse_two = normalize(hidden_one)
    mlp_input = (normed_two * gain_mlp).astype(jnp.bfloat16)
    hidden_pre = product(mlp_input, w_up)
    activated = gelu_exact(hidden_pre).astype(jnp.bfloat16)
    mlp_out = lax.psum(product(activated, w_down).astype(jnp.bfloat16), "mp").astype(jnp.float32)
    block_rows = (hidden_one + mlp_out).astype(jnp.bfloat16)
    normed_learn, inverse_learn = normalize(block_rows.astype(jnp.float32))
    learn_input = (normed_learn * gain_learn).astype(jnp.bfloat16)
    learn_full = lax.all_gather(w_learn, "dp", axis=0, tiled=True)
    learn_pre = product(learn_input, learn_full)
    learn_act = gelu_exact(learn_pre).astype(jnp.bfloat16)
    logits = product(learn_act, w_select).reshape(images, patch_count, -1)
    logits = jnp.where(visible[:, :, None], logits, -1e30)
    top_logit = jnp.max(logits, axis=1, keepdims=True)
    exp_logit = jnp.exp(logits - top_logit)
    token_maps = exp_logit / jnp.sum(exp_logit, axis=1, keepdims=True)
    maps_low = token_maps.astype(jnp.bfloat16)
    block_three = block_rows.reshape(images, patch_count, feature_count)
    learned = jnp.einsum(
        "bpn,bpd->bnd", maps_low, block_three, preferred_element_type=jnp.float32
    ).astype(jnp.bfloat16)
    grad_maps = jnp.einsum(
        "bnd,bpd->bpn", cotangent, block_three, preferred_element_type=jnp.float32
    )
    grad_block = jnp.einsum(
        "bpn,bnd->bpd", maps_low, cotangent, preferred_element_type=jnp.float32
    ).reshape(row_count, feature_count)
    grad_logits = token_maps * (grad_maps - jnp.sum(token_maps * grad_maps, axis=1, keepdims=True))
    grad_logits = grad_logits.reshape(row_count, -1).astype(jnp.bfloat16)
    grad_select = contract_rows(learn_act, grad_logits)
    grad_learn_act = contract_cols(grad_logits, w_select)
    grad_learn_pre = gelu_back(learn_pre, grad_learn_act).astype(jnp.bfloat16)
    grad_learn = contract_rows(learn_input, grad_learn_pre)
    grad_learn_input = contract_cols(grad_learn_pre, learn_full)
    grad_from_learn, grad_gain_learn = norm_back(
        grad_learn_input, normed_learn, inverse_learn, gain_learn
    )
    grad_hidden = grad_block + grad_from_learn
    grad_hidden_low = grad_hidden.astype(jnp.bfloat16)
    grad_down = contract_rows(activated, grad_hidden_low)
    grad_act = contract_cols(grad_hidden_low, w_down)
    grad_pre = gelu_back(hidden_pre, grad_act).astype(jnp.bfloat16)
    grad_up = contract_rows(mlp_input, grad_pre)
    mlp_back_term = contract_cols(grad_pre, w_up)
    grad_mlp_input = lax.psum(mlp_back_term.astype(jnp.bfloat16), "mp").astype(jnp.float32)
    grad_from_two, grad_gain_mlp = norm_back(grad_mlp_input, normed_two, inverse_two, gain_mlp)
    grad_hidden = grad_hidden + grad_from_two
    grad_attn_low = grad_hidden.astype(jnp.bfloat16)
    grad_out = contract_rows(mixed_heads, grad_attn_low)
    grad_mixed = contract_cols(grad_attn_low, w_out).astype(jnp.bfloat16).reshape(head_shape)
    probs_again = jnp.exp(masked_scores() - logsum)
    probs_again_low = probs_again.astype(jnp.bfloat16)
    grad_probs = jnp.einsum(
        "bqhe,bkhe->bhqk", grad_mixed, value_heads, preferred_element_type=jnp.float32
    )
    grad_value_heads = jnp.einsum(
        "bhqk,bqhe->bkhe", probs_again_low, grad_mixed, preferred_element_type=jnp.float32
    ).astype(jnp.bfloat16)
    grad_scores = probs_again * (
        grad_probs - jnp.sum(probs_again * grad_probs, axis=-1, keepdims=True)
    )
    grad_scores = grad_scores.astype(jnp.bfloat16)
    grad_query_heads = (
        jnp.einsum("bhqk,bkhe->bqhe", grad_scores, key_heads, preferred_element_type=jnp.float32)
        * score_scale
    ).astype(jnp.bfloat16)
    grad_key_heads = (
        jnp.einsum("bhqk,bqhe->bkhe", grad_scores, query_heads, preferred_element_type=jnp.float32)
        * score_scale
    ).astype(jnp.bfloat16)
    grad_query_flat = grad_query_heads.reshape(row_count, -1)
    grad_key_flat = grad_key_heads.reshape(row_count, -1)
    grad_value_flat = grad_value_heads.reshape(row_count, -1)
    grad_query = contract_rows(attn_input, grad_query_flat)
    grad_key = contract_rows(attn_input, grad_key_flat)
    grad_value = contract_rows(attn_input, grad_value_flat)
    attn_terms = (
        contract_cols(grad_query_flat, w_query)
        + contract_cols(grad_key_flat, w_key)
        + contract_cols(grad_value_flat, w_value)
    )
    grad_attn_input = lax.psum(attn_terms.astype(jnp.bfloat16), "mp").astype(jnp.float32)
    grad_from_one, grad_gain_attn = norm_back(grad_attn_input, normed_one, inverse_one, gain_attn)
    grad_patches = (
        (grad_hidden + grad_from_one)
        .astype(jnp.bfloat16)
        .reshape(images, patch_count, feature_count)
    )
    (
        grad_query,
        grad_key,
        grad_value,
        grad_out,
        grad_gain_attn,
        grad_up,
        grad_down,
        grad_gain_mlp,
        grad_gain_learn,
        grad_select,
        grad_learn,
    ) = (
        lax.psum(grad_query.astype(jnp.bfloat16), "dp").astype(jnp.float32),
        lax.psum(grad_key.astype(jnp.bfloat16), "dp").astype(jnp.float32),
        lax.psum(grad_value.astype(jnp.bfloat16), "dp").astype(jnp.float32),
        lax.psum(grad_out.astype(jnp.bfloat16), "dp").astype(jnp.float32),
        lax.psum(grad_gain_attn.astype(jnp.bfloat16), "dp").astype(jnp.float32),
        lax.psum(grad_up.astype(jnp.bfloat16), "dp").astype(jnp.float32),
        lax.psum(grad_down.astype(jnp.bfloat16), "dp").astype(jnp.float32),
        lax.psum(grad_gain_mlp.astype(jnp.bfloat16), "dp").astype(jnp.float32),
        lax.psum(grad_gain_learn.astype(jnp.bfloat16), "dp").astype(jnp.float32),
        lax.psum(grad_select.astype(jnp.bfloat16), "dp").astype(jnp.float32),
        lax.psum(grad_learn.astype(jnp.bfloat16), "dp").astype(jnp.float32),
    )
    learn_rows = w_learn.shape[0]
    grad_learn = lax.dynamic_slice_in_dim(
        grad_learn, lax.axis_index("dp") * learn_rows, learn_rows, 0
    )
    return (
        learned,
        block_three,
        grad_patches,
        grad_query,
        grad_key,
        grad_value,
        grad_out,
        grad_up,
        grad_down,
        grad_gain_attn,
        grad_gain_mlp,
        grad_gain_learn,
        grad_learn,
        grad_select,
    )


MESH = pl.DeviceIdType.MESH
PAD = 208
CH = 16
TILE = 256
PAIR_IN = 224
LAG = 2
LAG_END = 2
QB = 32
AHEAD = 7
f32 = jnp.float32
bf16 = jnp.bfloat16


def nn(a, b):
    return jnp.dot(a, b, preferred_element_type=f32)


def nt(a, b):
    return lax.dot_general(a, b, (((1,), (1,)), ((), ())), preferred_element_type=f32)


def tn(a, b):
    return lax.dot_general(a, b, (((0,), (0,)), ((), ())), preferred_element_type=f32)


def gauss(z):
    bell = jnp.exp(-0.5 * (z * z))
    t = 1.0 / (1.0 + 0.23164189 * jnp.abs(z))
    poly = t * (
        0.127414796 + t * (-0.142248368 + t * (0.7107068705 + t * (-0.7265760135 + t * 0.5307027145)))
    )
    tail = poly * bell
    return jnp.where(z >= 0, 1.0 - tail, tail), 0.3989422804014327 * bell


def stats(v):
    mean = jnp.sum(v, axis=-1, keepdims=True) * (1.0 / v.shape[-1])
    c = v - mean
    s = lax.rsqrt(jnp.sum(c * c, axis=-1, keepdims=True) * (1.0 / v.shape[-1]) + 1e-06)
    return c * s, mean, s


def back(e, u, s):
    width = 1.0 / e.shape[-1]
    return s * (
        e
        - jnp.sum(e, axis=-1, keepdims=True) * width
        - u * (jnp.sum(e * u, axis=-1, keepdims=True) * width)
    )


def fold(v):
    total = v[0:8]
    for r in range(8, v.shape[0], 8):
        total = total + v[r : r + 8]
    return total


def chunks():
    return range(0, PAD, CH)


def fused(
    patches, keep_ref, wq_hbm, wk_hbm, wv_hbm, wo_hbm, wup_hbm, wdn_hbm, g1_ref, g2_ref, g3_ref,
    wl_hbm, wsel_ref, ct_ref,
    learned_ref, y_hbm, gp_hbm, gall_hbm, small_ref, gl_ref,
    bias, wqkv, wo, wl,
    xs, qkv, os, h1s, a2s, dhs, d1s, big, recv,
    pbuf, rcore, rx, sumb, dg, gl_sum, gsel_sum, gl_mine, gl_in, small_mine, small_in, col, centre, scale, part_a, part_b,
    sx, sw, sy, slearn_s, slearn_r, s_core, r_core, s_x, r_x, s_ag, r_ag,
    s_pair, r_pair, s_out, ready_y, ready_z, s_small, r_small,
):
    images, count = keep_ref.shape
    width = patches.shape[1]
    half = width // 2
    dp = lax.axis_index("dp")
    mp = lax.axis_index("mp")
    core = lax.rem(mp, 2)
    mate = (dp, mp + 1 - 2 * core)
    across = (dp, lax.rem(mp + 2, 4))
    dps = lax.axis_size("dp")
    yy = lax.rem(dp, 2)
    zz = dp // 2
    middle = (zz == 1) | (zz == 2)
    zm = jnp.where(zz >= 2, 1, 0)
    mate_y = (dp + 1 - 2 * yy, mp)
    mate_e = ((zz + 1 - 2 * lax.rem(zz, 2)) * 2 + yy, mp)
    mate_m = ((3 - zz) * 2 + yy, mp)
    total = images * PAD
    kept = 8 * PAIR_IN
    rs = big.at[pl.ds(0, total)]
    wup = recv.at[pl.ds(kept, width)]
    wdn = recv.at[pl.ds(kept + width, width)]
    gs = recv.at[pl.ds(kept + 2 * width, total)]

    barrier = pltpu.get_barrier_semaphore()
    for device in (mate, across):
        pl.semaphore_signal(barrier, inc=1, device_id=device, device_id_type=MESH)
    for k in range(1, dps):
        pl.semaphore_signal(barrier, inc=1, device_id=(lax.rem(dp + k, dps), mp), device_id_type=MESH)

    def wl_part(d):
        return wl.at[:, pl.ds(pl.multiple_of(d * wl_hbm.shape[1], 128), wl_hbm.shape[1])]

    loads = [
        pltpu.make_async_copy(wq_hbm, wqkv.at[:, pl.ds(0, 256)], sw.at[0]),
        pltpu.make_async_copy(wk_hbm, wqkv.at[:, pl.ds(256, 256)], sw.at[1]),
        pltpu.make_async_copy(wv_hbm, wqkv.at[:, pl.ds(512, 256)], sw.at[2]),
        pltpu.make_async_copy(wo_hbm, wo, sw.at[3]),
        pltpu.make_async_copy(wup_hbm, wup, sw.at[4]),
        pltpu.make_async_copy(wdn_hbm, wdn, sw.at[5]),
        pltpu.make_async_copy(wl_hbm, wl_part(dp), sw.at[6]),
    ]

    load_x = [
        pltpu.make_async_copy(
            patches.at[:, pl.ds(c * TILE, TILE)], dhs.at[pl.ds(0, images * count), pl.ds(c * TILE, TILE)], sx.at[c]
        )
        for c in range(4)
    ]
    for copy in load_x:
        copy.start()
    for k in (0, 1, 2, 3, 6):
        loads[k].start()

    for i in range(images):
        xs[i * PAD + PAD - 16 : (i + 1) * PAD, :] = jnp.zeros((16, width), bf16)
    bias[...] = jnp.full(bias.shape, -1e30, f32)
    for i in range(images):
        bias[i, :, 0:count] = jnp.where(keep_ref[i : i + 1, :] > 0, 0.0, -1e30)
    turned = jnp.transpose(bias[...].reshape(images, PAD))
    for i in range(images):
        col[i * PAD : (i + 1) * PAD, 0:1] = turned[:, i : i + 1]
    for c in range(4):
        load_x[c].wait()
        for r in range(0, images * count, 8 * CH):
            top = min(r + 8 * CH, images * count)
            for n in (2 * c, 2 * c + 1):
                h1s[n, r:top, :] = dhs[r:top, n * 128 : (n + 1) * 128].astype(f32)

    g1 = g1_ref[...]
    g2 = g2_ref[...]
    g3 = g3_ref[...]
    lane_head = lax.broadcasted_iota(jnp.int32, (1, 256), 1) // 64

    def only(v, h):
        return jnp.where(lane_head == h, v, jnp.zeros_like(v))

    def put_wide(where, value):
        for c in range(width // 128):
            h1s[c, where, :] = value[:, c * 128 : (c + 1) * 128]

    def get_wide(where):
        return jnp.concatenate([h1s[c, where, :] for c in range(width // 128)], axis=1)

    def rows_of(i):
        return pl.ds(pl.multiple_of(i * PAD, 16), PAD)

    def chunk_of(i, r):
        return pl.ds(pl.multiple_of(i * PAD + r, 16), CH)

    def copy_core(i):
        return pltpu.make_async_remote_copy(
            src_ref=pbuf.at[1 - core, rows_of(i)], dst_ref=rcore.at[rows_of(i)],
            send_sem=s_core.at[i], recv_sem=r_core.at[i], device_id=mate, device_id_type=MESH,
        )

    def copy_x(i, par):
        return pltpu.make_async_remote_copy(
            src_ref=pbuf.at[core, rows_of(i)], dst_ref=rx.at[par, rows_of(i)],
            send_sem=s_x.at[i], recv_sem=r_x.at[par, i], device_id=across, device_id_type=MESH,
        )

    def copy_ag(i):
        return pltpu.make_async_remote_copy(
            src_ref=sumb.at[core, rows_of(i)], dst_ref=sumb.at[core, rows_of(i)],
            send_sem=s_ag.at[i], recv_sem=r_ag.at[i], device_id=mate, device_id_type=MESH,
        )

    def hop_two(i, par):
        copy_core(i).wait()
        rows = rows_of(i)
        pbuf[core, rows] = (pbuf[core, rows].astype(f32) + rcore[rows].astype(f32)).astype(bf16)
        copy_x(i, par).start()

    def hop_three(i, par):
        copy_x(i, par).wait()
        rows = rows_of(i)
        sumb[core, rows] = (pbuf[core, rows].astype(f32) + rx[par, rows].astype(f32)).astype(bf16)
        copy_ag(i).start()

    def arrived(i):
        copy_ag(i).wait()

    def summed(i, r):
        where = chunk_of(i, r)
        return jnp.concatenate([sumb[0, where].astype(f32), sumb[1, where].astype(f32)], axis=1)

    def store_p(i, t, value):
        pbuf[t // 2, rows_of(i), (t % 2) * TILE : (t % 2 + 1) * TILE] = value.astype(bf16)

    def stage(body, lo, hi, second, before=None, begun=False):
        def step(i, carry):
            if before is not None:
                before(i, hi)
            body(i)
            copy_core(i).start()

            @pl.when((i > lo) | begun)
            def _():
                second(i - 1)
            return carry

        lax.fori_loop(lo, hi, step, 0)
        second(hi - 1)

    def far(par):
        return lambda i: hop_two(i, par)

    def from_far(par):
        def before(i, hi):
            @pl.when(i + 1 < hi)
            def _():
                hop_three(i + 1, par)
            arrived(i)
        return before

    def each(body, lo, hi, before=None):
        def step(i, carry):
            if before is not None:
                before(i, hi)
            body(i)
            return carry

        lax.fori_loop(lo, hi, step, 0)

    def g_tile(j):
        return pl.ds(pl.multiple_of(lax.rem(j * TILE + 2048, 3072), 16), TILE)

    def pieces(q, count_of, first, number, lag):
        def g_rows(k, lo, n):
            return pl.ds(pl.multiple_of(lax.rem(k * (4 * q) + first + 2048, 3072) + lo, 16), n)

        def in_rows(k, lo, n):
            return pl.ds(pl.multiple_of(k * (7 * q) + first // 128 * PAIR_IN + lo, 16), n)

        def send(k, slot, src, dst, device):
            return pltpu.make_async_remote_copy(
                src_ref=src, dst_ref=dst, send_sem=s_pair.at[slot, k + number], recv_sem=r_pair.at[slot, k + number],
                device_id=device, device_id_type=MESH,
            )

        def y_swap(k):
            return send(k, 0, big.at[g_rows(k, q - q * yy, q)], recv.at[in_rows(k, 0, q)], mate_y)

        def y_end(k):
            return send(k, 1, big.at[g_rows(k, q * yy, q)], recv.at[in_rows(k, q, q)], mate_e)

        def y_mid(k):
            return send(k, 2, big.at[g_rows(k, q * yy, q)], recv.at[in_rows(k, 2 * q, q)], mate_m)

        def o_rows(k, lo, n):
            return gall_hbm.at[pl.ds(pl.multiple_of(k * (4 * q) + first + lo, 16), n)]

        def y_back(k):
            return send(k, 3, big.at[g_rows(k, q * yy, q)], o_rows(k, q * yy, q), mate_e)

        def y_share_mid(k):
            return send(k, 4, big.at[g_rows(k, q * yy, q)], o_rows(k, q * yy, q), mate_y)

        def y_share_end(k):
            return send(k, 4, o_rows(k, q * yy, q), o_rows(k, q * yy, q), mate_y)

        def z_end(k):
            return send(k, 5, big.at[g_rows(k, 2 * q, 2 * q)], recv.at[in_rows(k, 5 * q, 2 * q)], mate_e)

        def z_mid(k):
            return send(k, 6, big.at[g_rows(k, 3 * q - q * zm, q)], recv.at[in_rows(k, 3 * q, q)], mate_m)

        def z_swap(k):
            return send(k, 7, big.at[g_rows(k, 2 * q + q * zm, q)], recv.at[in_rows(k, 4 * q, q)], mate_y)

        def z_share(k):
            return send(k, 8, big.at[g_rows(k, 2 * q + q * zm, q)], o_rows(k, 2 * q + q * zm, q), mate_m)

        def z_back(k):
            return send(k, 9, big.at[g_rows(k, 2 * q + q * zm, q)], o_rows(k, 2 * q + q * zm, q), mate_e)

        def z_pass(k):
            return send(k, 10, o_rows(k, 3 * q - q * zm, q), o_rows(k, 3 * q - q * zm, q), mate_e)

        def accumulate(k, lo, n, at):
            rows = g_rows(k, lo, n)
            big[rows, :] = (big[rows, :].astype(f32) + recv[in_rows(k, at, n), :].astype(f32)).astype(bf16)

        def keep_y(k):
            return pltpu.make_async_copy(big.at[g_rows(k, q * yy, q)], o_rows(k, q * yy, q), s_out.at[0, k + number])

        def keep_z(k):
            return pltpu.make_async_copy(
                big.at[g_rows(k, 2 * q + q * zm, q)], o_rows(k, 2 * q + q * zm, q), s_out.at[1, k + number]
            )

        def hop0(k):
            y_swap(k).start()

            @pl.when(jnp.logical_not(middle))
            def _():
                z_end(k).start()

        def hop1(k):
            y_swap(k).wait()
            accumulate(k, q * yy, q, 0)

            @pl.when(middle)
            def _():
                z_end(k).wait_recv()
                accumulate(k, 2 * q, 2 * q, 5 * q)
                z_mid(k).start()

            @pl.when(jnp.logical_not(middle))
            def _():
                y_end(k).start()

        def hop2(k):
            @pl.when(middle)
            def _():
                y_end(k).wait_recv()
                accumulate(k, q * yy, q, q)
                y_mid(k).start()
                z_mid(k).wait()
                accumulate(k, 2 * q + q * zm, q, 3 * q)
                z_swap(k).start()

        def hop3(k):
            @pl.when(middle)
            def _():
                y_mid(k).wait()
                accumulate(k, q * yy, q, 2 * q)
                y_back(k).start()
                y_share_mid(k).start()
                keep_y(k).start()
                z_swap(k).wait()
                accumulate(k, 2 * q + q * zm, q, 4 * q)
                z_share(k).start()
                z_back(k).start()
                keep_z(k).start()

        def hop4(k):
            @pl.when(middle)
            def _():
                z_share(k).wait()
                z_pass(k).start()

            @pl.when(jnp.logical_not(middle))
            def _():
                y_end(k).wait_send()
                y_back(k).wait_recv()
                y_share_end(k).start()

        def hop5(k):
            @pl.when(middle)
            def _():
                y_share_mid(k).wait()
                y_back(k).wait_send()
                z_back(k).wait_send()
                z_pass(k).wait_send()
                keep_y(k).wait()
                keep_z(k).wait()

            @pl.when(jnp.logical_not(middle))
            def _():
                y_share_end(k).wait()
                z_end(k).wait_send()
                z_back(k).wait_recv()
                z_pass(k).wait_recv()

        hops = ((5, hop5), (4, hop4), (3, hop3), (2, hop2), (1, hop1), (0, hop0))

        def tick(t):
            for h, hop in hops:
                k = t - lag * h

                @pl.when((k >= 0) & (k < count_of))
                def _(hop=hop, k=k):
                    hop(k)

        return tick

    tick_mlp = pieces(32, 16, 0, 0, LAG)
    tick_attention = pieces(QB, 256 // QB, 2048, 16, LAG_END)

    def ticks(run, lo, hi):
        def step(t, carry):
            run(t)
            return carry

        lax.fori_loop(lo, hi, step, 0)

    for k in (0, 1, 2, 3):
        loads[k].wait()
    loads[4].start()
    loads[5].start()


    def attend(q, k, v, row_bias):
        o = jnp.zeros((PAD, 256), f32)
        for h in range(4):
            scores = nt(only(q, h), k) + row_bias
            e = jnp.exp(scores - jnp.max(scores, axis=1, keepdims=True))
            p = (e * (1.0 / jnp.sum(e, axis=1, keepdims=True))).astype(bf16)
            o = o + nn(p, only(v, h))
        return o.astype(bf16)

    def attention(i):
        start = pl.multiple_of(i * PAD, 16)
        for c in range(width // 128):
            xs[pl.ds(start, count), c * 128 : (c + 1) * 128] = h1s[c, pl.ds(i, count, stride=images), :].astype(bf16)
        for r in chunks():
            u, mean, s = stats(xs[chunk_of(i, r), :].astype(f32))
            col[chunk_of(i, r), 1:2] = mean
            col[chunk_of(i, r), 2:3] = s
            a2s[chunk_of(i, r), :] = (u * g1).astype(bf16)
        rows = rows_of(i)
        a1 = a2s[rows, :]
        qkv[rows, 0:256] = (nn(a1, wqkv[:, 0:256]) * 0.125).astype(bf16)
        qkv[rows, 256:512] = nn(a1, wqkv[:, 256:512]).astype(bf16)
        qkv[rows, 512:768] = nn(a1, wqkv[:, 512:768]).astype(bf16)
        os[rows, :] = attend(qkv[rows, 0:256], qkv[rows, 256:512], qkv[rows, 512:768], bias[i])

    def attention_sent(i):
        attention(i)
        ob = os[rows_of(i), :]
        for t in range(4):
            store_p(i, t, nn(ob, wo[:, t * TILE : (t + 1) * TILE]))

    attention_sent(0)

    pl.semaphore_wait(barrier, dps + 1)

    def learn_copy(k):
        return pltpu.make_async_remote_copy(
            src_ref=wl_part(dp), dst_ref=wl_part(dp),
            send_sem=slearn_s.at[k - 1], recv_sem=slearn_r.at[k - 1],
            device_id=(lax.rem(dp + k, dps), mp), device_id_type=MESH,
        )

    loads[6].wait()
    for k in range(1, dps):
        learn_copy(k).start()

    copy_core(0).start()
    hop_two(0, 0)
    stage(attention_sent, 1, images, far(0))

    loads[4].wait()
    loads[5].wait()

    def mlp(i):
        for r in chunks():
            h1 = xs[chunk_of(i, r), :].astype(f32) + summed(i, r)
            put_wide(chunk_of(i, r), h1)
            u, mean, s = stats(h1)
            col[chunk_of(i, r), 3:4] = mean
            col[chunk_of(i, r), 4:5] = s
            a2s[chunk_of(i, r), :] = (u * g2).astype(bf16)
        rows = rows_of(i)
        a2 = a2s[rows, :]
        for t in range(4):
            cols = slice(t * TILE, (t + 1) * TILE)
            z = nn(a2, wup[:, cols])
            cdf, pdf = gauss(z)
            rs[rows, cols] = (z * cdf).astype(bf16)
            gs[rows, cols] = (cdf + z * pdf).astype(bf16)
        act = rs[rows, :]
        for t in range(4):
            store_p(i, t, nn(act, wdn[:, t * TILE : (t + 1) * TILE]))

    hop_three(0, 0)
    stage(mlp, 0, images, far(1), from_far(0))

    for k in range(1, dps):
        learn_copy(k).wait()
    dg[...] = jnp.zeros_like(dg)
    gl_sum[...] = jnp.zeros_like(gl_sum)
    gsel_sum[...] = jnp.zeros_like(gsel_sum)

    def y_out(i):
        return pltpu.make_async_copy(d1s.at[rows_of(i)], y_hbm.at[rows_of(i)], sy.at[i])

    def learner(i):
        rows = rows_of(i)
        for r in chunks():
            yb = (get_wide(chunk_of(i, r)) + summed(i, r)).astype(bf16)
            d1s[chunk_of(i, r), :] = yb
            v = yb.astype(f32)
            mean = jnp.sum(v, axis=-1, keepdims=True) * (1.0 / width)
            v = v - mean
            s = lax.rsqrt(jnp.sum(v * v, axis=-1, keepdims=True) * (1.0 / width) + 1e-06)
            centre[r : r + CH, :] = mean
            scale[r : r + CH, :] = s
            dhs[chunk_of(i, r), :] = (v * s * g3).astype(bf16)
        y_out(i).start()
        y = d1s[rows, :]
        a3 = dhs[rows, :]
        wlf = wl[...]
        wsel = wsel_ref[...]
        ct = ct_ref[i]
        zl = nt(a3, wlf)
        cdf, pdf = gauss(zl)
        t = (zl * cdf).astype(bf16)
        slope = cdf + zl * pdf
        col_bias = col[rows, 0:1]
        logits = nt(t, wsel) + col_bias
        e = jnp.exp(logits - jnp.max(logits, axis=0, keepdims=True))
        maps = e * (1.0 / jnp.sum(e, axis=0, keepdims=True))
        mb = maps.astype(bf16)
        learned_ref[i] = tn(mb, y).astype(bf16)
        dmaps = nt(y, ct)
        dlog = (maps * (dmaps - jnp.sum(maps * dmaps, axis=0, keepdims=True))).astype(bf16)
        gsel_sum[...] += tn(dlog, t)
        dzl = (nn(dlog, wsel) * slope).astype(bf16)
        gl_sum[...] += tn(dzl, a3)
        part_a[...] = nn(dzl, wlf)
        part_b[...] = nn(mb, ct)
        for r in chunks():
            da3 = part_a[r : r + CH, :]
            dy = part_b[r : r + CH, :]
            s = scale[r : r + CH, :]
            u = (d1s[chunk_of(i, r), :].astype(f32) - centre[r : r + CH, :]) * s
            dg[2] += fold(da3 * u)
            dhs[chunk_of(i, r), :] = (dy + back(da3 * g3, u, s)).astype(bf16)

    def mlp_back(i):
        rows = rows_of(i)
        dhb = dhs[rows, :]
        for c in range(4):
            cols = slice(c * TILE, (c + 1) * TILE)
            dr = nt(dhb, wdn[cols, :])
            gs[rows, cols] = (dr * gs[rows, cols].astype(f32)).astype(bf16)
        dz = gs[rows, :]
        for c in range(4):
            store_p(i, c, nt(dz, wup[c * TILE : (c + 1) * TILE, :]))

    early = images // 2

    def learner_mlp(i):
        learner(i)

        @pl.when(i < early)
        def _():
            mlp_back(i)
            copy_core(i).start()

        @pl.when((i > 0) & (i <= early))
        def _():
            hop_two(i - 1, 0)

        @pl.when(i == images - 2)
        def _():
            hop_three(i + 1, 1)

    hop_three(0, 1)
    def before_learner(i, hi):
        @pl.when(i + 2 < hi)
        def _():
            hop_three(i + 1, 1)
        arrived(i)

    each(learner_mlp, 0, images, before_learner)

    def grad(left, right, first, after):
        def step(j, carry):
            lhs = left[:, pl.ds(pl.multiple_of(j * TILE, TILE), TILE)]
            rows = g_tile(first + j)
            for c in range(0, width, TILE):
                big[rows, c : c + TILE] = tn(lhs, right[:, c : c + TILE]).astype(bf16)
            if after is not None:
                after(j)
            return carry

        lax.fori_loop(0, left.shape[1] // TILE, step, 0)

    def ready():
        pl.semaphore_signal(ready_y, inc=1, device_id=mate_y, device_id_type=MESH)

        @pl.when(middle)
        def _():
            pl.semaphore_signal(ready_z, inc=1, device_id=mate_e, device_id_type=MESH)
            pl.semaphore_signal(ready_z, inc=1, device_id=mate_m, device_id_type=MESH)

    def both_ready():
        pl.semaphore_wait(ready_y, 1)
        pl.semaphore_wait(ready_z, 1)

    grad(rs, dhs, 0, tick_mlp)

    def mlp_back_tick(i):
        mlp_back(i)
        tick_mlp(4 + i - early)

    stage(mlp_back_tick, early, images, far(0))
    def after_up(j):
        @pl.when(lax.rem(j, 2) == 1)
        def _():
            tick_mlp(8 + j // 2)

    ready()
    both_ready()
    grad(a2s, gs, 4, after_up)
    ready()
    for i in range(images):
        y_out(i).wait()

    def attention_back(i):
        rows = rows_of(i)
        for r in chunks():
            where = chunk_of(i, r)
            da2 = summed(i, r)
            s = col[where, 4:5]
            u = (get_wide(where) - col[where, 3:4]) * s
            dg[1] += fold(da2 * u)
            d1s[where, :] = (dhs[where, :].astype(f32) + back(da2 * g2, u, s)).astype(bf16)
            ux = (xs[where, :].astype(f32) - col[where, 1:2]) * col[where, 2:3]
            a2s[where, :] = (ux * g1).astype(bf16)
        d1 = d1s[rows, :]
        do = nt(d1, wo[...]).astype(bf16)
        q = qkv[rows, 0:256]
        k = qkv[rows, 256:512]
        v = qkv[rows, 512:768]
        col_bias = col[rows, 0:1]
        dq = jnp.zeros((PAD, 256), f32)
        dk = jnp.zeros((PAD, 256), f32)
        dv = jnp.zeros((PAD, 256), f32)
        for h in range(4):
            kh = only(k, h)
            scores = nt(kh, q) + col_bias
            e = jnp.exp(scores - jnp.max(scores, axis=0, keepdims=True))
            p = e * (1.0 / jnp.sum(e, axis=0, keepdims=True))
            dv = dv + nn(p.astype(bf16), only(do, h))
            dpr = nt(only(v, h), do)
            ds = (p * (dpr - jnp.sum(p * dpr, axis=0, keepdims=True))).astype(bf16)
            dk = dk + nn(ds, only(q, h))
            dq = dq + tn(ds, kh)
        qkv[rows, 0:256] = (dq * 0.125).astype(bf16)
        qkv[rows, 256:512] = dk.astype(bf16)
        qkv[rows, 512:768] = dv.astype(bf16)
        dall = qkv[rows, :]
        for c in range(4):
            store_p(i, c, nt(dall, wqkv[c * TILE : (c + 1) * TILE, :]))
        tick_mlp(10 + i)

        @pl.when(i == images - 2)
        def _():
            hop_three(i + 1, 0)

    hop_three(0, 0)
    def before_back(i, hi):
        @pl.when(i + 2 < hi)
        def _():
            hop_three(i + 1, 0)
        arrived(i)

    stage(attention_back, 0, images, far(1), before_back)
    both_ready()
    grad(os, d1s, 8, lambda j: tick_mlp(18))
    tick_attention(0)
    tick_attention(1)

    def grad_qkv(j, carry):
        lhs = a2s[:, pl.ds(pl.multiple_of(j * TILE, TILE), TILE)]
        for n in range(3):
            value = tn(lhs, qkv[:, n * TILE : (n + 1) * TILE]).astype(bf16)
            rows = pl.ds(pl.multiple_of(1280 + j * 192 + n * 64, 16), 64)
            for c in range(4):
                big[rows, c * TILE : (c + 1) * TILE] = value[c * 64 : (c + 1) * 64]
        tick_mlp(19 + j)
        tick_attention(2 + j)
        return carry

    lax.fori_loop(0, 4, grad_qkv, 0)

    def gp_out(i):
        return pltpu.make_async_copy(dhs.at[rows_of(i)], gp_hbm.at[rows_of(i)], sy.at[i])

    def finish(i, carry):
        @pl.when(i + 1 < images)
        def _():
            hop_three(i + 1, 1)
        arrived(i)
        for r in chunks():
            where = chunk_of(i, r)
            da1 = summed(i, r)
            s = col[where, 2:3]
            u = (xs[where, :].astype(f32) - col[where, 1:2]) * s
            dg[0] += fold(da1 * u)
            dhs[where, :] = (d1s[where, :].astype(f32) + back(da1 * g1, u, s)).astype(bf16)
        gp_out(i).start()
        tick_mlp(23 + i)
        tick_attention(6 + i)
        return carry

    hop_three(0, 1)
    lax.fori_loop(0, images, finish, 0)

    small_mine[0:8, :] = jnp.concatenate(
        [jnp.sum(dg[n], axis=0, keepdims=True) for n in range(3)] + [jnp.zeros((5, width), f32)], axis=0
    ).astype(bf16)
    small_mine[8:16, 0:64] = gsel_sum[...].astype(bf16)
    small_mine[8:16, 64:width] = jnp.zeros((8, width - 64), bf16)
    gl_mine[...] = gl_sum[...].astype(bf16)
    part = wl_hbm.shape[1]

    def gl_part(d):
        return pl.ds(pl.multiple_of(d * part, 128), part)

    def small_copy(k):
        peer = lax.rem(dp + k, dps)
        return (
            pltpu.make_async_remote_copy(
                src_ref=small_mine, dst_ref=small_in.at[k - 1], send_sem=s_small.at[0, k - 1],
                recv_sem=r_small.at[0, k - 1], device_id=(peer, mp), device_id_type=MESH,
            ),
            pltpu.make_async_remote_copy(
                src_ref=gl_mine.at[:, gl_part(peer)], dst_ref=gl_in.at[k - 1], send_sem=s_small.at[1, k - 1],
                recv_sem=r_small.at[1, k - 1], device_id=(peer, mp), device_id_type=MESH,
            ),
        )

    for k in range(1, dps):
        for copy in small_copy(k):
            copy.start()
    ticks(tick_mlp, 31, 16 + 5 * LAG)
    ticks(tick_attention, 14, 16)
    for k in range(1, dps):
        for copy in small_copy(k):
            copy.wait()
    small_ref[...] = small_mine[...].astype(f32)
    gl_ref[...] = gl_mine[:, gl_part(dp)].astype(f32)
    for k in range(dps - 1):
        small_ref[...] += small_in[k].astype(f32)
        gl_ref[...] += gl_in[k].astype(f32)
    ticks(tick_attention, 16, 256 // QB + 5 * LAG_END)
    for i in range(images):
        gp_out(i).wait()


def finish_up(
    gall, y, gp, learned, small, gl,
    learned_ref, y_ref, gp_ref, gq_ref, gk_ref, gv_ref, gout_ref, gup_ref, gdn_ref, d1_ref, d2_ref, d3_ref,
    gl_ref, gsel_ref,
    tiles, y_in, gp_in, wide, square, y_turned, gp_turned, strip, s_tile, s_in, s_wide, s_square, s_turned,
):
    count = y_ref.shape[0]

    def tile_in(j):
        rows = pl.ds(j * TILE, TILE)
        return pltpu.make_async_copy(gall.at[rows], tiles.at[rows], s_tile.at[j])

    ins = [pltpu.make_async_copy(y, y_in, s_in.at[0]), pltpu.make_async_copy(gp, gp_in, s_in.at[1])]
    queue = [tile_in(j) for j in range(5)] + ins[:1] + [tile_in(j) for j in range(5, 9)] + ins[1:]
    queue += [tile_in(j) for j in range(9, 12)]
    outs = []

    def begin(n):
        for _ in range(n):
            if queue:
                queue.pop(0).start()

    def tile_out(j):
        tile_in(j).wait()
        begin(1)
        rows = slice(j * TILE, (j + 1) * TILE)
        wide[rows, :] = tiles[rows, :].astype(f32)
        ref, first = ((gdn_ref, 0), (gup_ref, 4), (gout_ref, 8))[j // 4]
        copy = pltpu.make_async_copy(
            wide.at[pl.ds(j * TILE, TILE)], ref.at[pl.ds((j - first) * TILE, TILE)], s_wide.at[j]
        )
        copy.start()
        outs.append(copy)

    def turn(n, src, dst, ref):
        ins[n].wait()
        begin(2)
        for block in range(0, count, CH):
            rows = min(CH, count - block)
            for c in range(src.shape[2] // 128):
                cols = slice(c * 128, (c + 1) * 128)
                slot = strip.at[c]
                slot[...] = src[:, block : block + CH, cols].astype(f32).reshape(slot.shape)
                for r in range(rows):
                    dst[block + r, :, cols] = slot[pl.ds(r, dst.shape[1], stride=CH), :].astype(bf16)
            copy = pltpu.make_async_copy(
                dst.at[pl.ds(block, rows)], ref.at[pl.ds(block, rows)], s_turned.at[n, block // CH]
            )
            copy.start()
            outs.append(copy)

    begin(AHEAD)
    for j in range(6):
        tile_out(j)
    turn(0, y_in, y_turned, y_ref)
    for j in range(6, 9):
        tile_out(j)
    turn(1, gp_in, gp_turned, gp_ref)
    begin(len(queue))
    for j in range(9, 12):
        tile_in(j).wait()
    for n, ref in enumerate((gq_ref, gk_ref, gv_ref)):
        for j in range(4):
            for c in range(4):
                square[n, j * TILE + c * 64 : j * TILE + (c + 1) * 64, :] = tiles[
                    9 * TILE + j * 192 + n * 64 : 9 * TILE + j * 192 + (n + 1) * 64, c * TILE : (c + 1) * TILE
                ].astype(f32)
        copy = pltpu.make_async_copy(square.at[n], ref, s_square.at[n])
        copy.start()
        outs.append(copy)
    learned_ref[...] = learned[...]
    for n, ref in enumerate((d1_ref, d2_ref, d3_ref)):
        ref[...] = small[n : n + 1, :]
    gl_ref[...] = gl[...]
    gsel_ref[...] = small[8:16, 0 : gsel_ref.shape[1]]
    for copy in outs:
        copy.wait()


def local_fused(
    patches, keep_mask, w_query, w_key, w_value, w_out, w_up, w_down,
    gain_attn, gain_mlp, gain_learn, w_learn, w_select, cotangent,
):
    images, count, width = patches.shape
    total = images * PAD
    hidden = w_up.shape[1]
    learn_rows, learn_cols = w_learn.shape
    dps = lax.axis_size("dp")
    anywhere = pl.BlockSpec(memory_space=pl.ANY)
    vmem = pl.BlockSpec(memory_space=pltpu.VMEM)
    sds = jax.ShapeDtypeStruct
    dma = pltpu.SemaphoreType.DMA
    outs = pl.pallas_call(
        fused,
        name="block",
        out_shape=(
            sds((images, 8, width), bf16),
            sds((total, width), bf16),
            sds((total, width), bf16),
            sds((3072, width), bf16),
            sds((16, width), f32),
            sds((learn_cols, learn_rows), f32),
        ),
        in_specs=[anywhere, vmem] + [anywhere] * 6 + [vmem] * 3 + [anywhere] + [vmem] * 2,
        out_specs=(vmem,) + (anywhere,) * 3 + (vmem,) * 2,
        scratch_shapes=[
            pltpu.VMEM((images, 1, PAD), f32),
            pltpu.VMEM((width, 768), bf16),
            pltpu.VMEM((256, width), bf16),
            pltpu.VMEM((learn_cols, width), bf16),
            pltpu.VMEM((total, width), bf16),
            pltpu.VMEM((total, 768), bf16),
            pltpu.VMEM((total, 256), bf16),
            pltpu.VMEM((width // 128, total, 128), f32),
            pltpu.VMEM((total, width), bf16),
            pltpu.VMEM((total, width), bf16),
            pltpu.VMEM((total, width), bf16),
            pltpu.VMEM((3072, width), bf16),
            pltpu.VMEM((8 * PAIR_IN + total + 2 * width, width), bf16),
            pltpu.VMEM((2, total, width // 2), bf16),
            pltpu.VMEM((total, width // 2), bf16),
            pltpu.VMEM((2, total, width // 2), bf16),
            pltpu.VMEM((2, total, width // 2), bf16),
            pltpu.VMEM((3, 8, width), f32),
            pltpu.VMEM((learn_cols, width), f32),
            pltpu.VMEM((8, learn_cols), f32),
            pltpu.VMEM((learn_cols, width), bf16),
            pltpu.VMEM((dps - 1, learn_cols, learn_rows), bf16),
            pltpu.VMEM((16, width), bf16),
            pltpu.VMEM((dps - 1, 16, width), bf16),
            pltpu.VMEM((total, 8), f32),
            pltpu.VMEM((PAD, 1), f32),
            pltpu.VMEM((PAD, 1), f32),
            pltpu.VMEM((PAD, width), f32),
            pltpu.VMEM((PAD, width), f32),
            dma((4,)), dma((7,)), dma((images,)), dma((dps - 1,)), dma((dps - 1,)),
            dma((images,)), dma((images,)), dma((images,)), dma((2, images)), dma((images,)), dma((images,)),
            dma((11, 16 + 256 // QB)), dma((11, 16 + 256 // QB)), dma((2, 16 + 256 // QB)),
            pltpu.SemaphoreType.REGULAR, pltpu.SemaphoreType.REGULAR, dma((2, dps - 1)), dma((2, dps - 1)),
        ],
        compiler_params=pltpu.CompilerParams(
            collective_id=0, has_side_effects=True, vmem_limit_bytes=60 * 2**20
        ),
    )(
        patches.transpose(1, 0, 2).reshape(count * images, width), keep_mask, w_query, w_key, w_value, w_out, w_up, w_down,
        gain_attn[None], gain_mlp[None], gain_learn[None], w_learn.T, w_select.T, cotangent,
    )
    learned, y, gpat, gall, small, gl = outs

    square = (width, TILE)
    row = (1, width)
    blocks = -(-count // CH)
    outs = pl.pallas_call(
        finish_up,
        name="finish",
        out_shape=(
            sds((images, 8, width), bf16), sds((count, images, width), bf16), sds((count, images, width), bf16),
            sds(square, f32), sds(square, f32), sds(square, f32),
            sds((TILE, width), f32), sds((width, hidden), f32), sds((hidden, width), f32),
            sds(row, f32), sds(row, f32), sds(row, f32),
            sds((learn_cols, learn_rows), f32), sds((8, learn_cols), f32),
        ),
        in_specs=[anywhere] * 3 + [vmem] * 3,
        out_specs=(vmem,) + (anywhere,) * 8 + (vmem,) * 5,
        scratch_shapes=[
            pltpu.VMEM((3072, width), bf16),
            pltpu.VMEM((images, PAD, width), bf16),
            pltpu.VMEM((images, PAD, width), bf16),
            pltpu.VMEM((9 * TILE, width), f32),
            pltpu.VMEM((3,) + square, f32),
            pltpu.VMEM((count, images, width), bf16),
            pltpu.VMEM((count, images, width), bf16),
            pltpu.VMEM((width // 128, images * CH, 128), f32),
            dma((12,)), dma((2,)), dma((9,)), dma((3,)), dma((2, blocks)),
        ],
        compiler_params=pltpu.CompilerParams(vmem_limit_bytes=60 * 2**20),
    )(gall, y.reshape(images, PAD, width), gpat.reshape(images, PAD, width), learned, small, gl)
    learned, y, gpat, gq, gk, gv, gout, gup, gdn, d1, d2, d3, gl, gsel = outs
    return (
        learned, y.transpose(1, 0, 2), gpat.transpose(1, 0, 2), gq, gk, gv, gout, gup, gdn,
        d1[0], d2[0], d3[0], gl.T, gsel.T,
    )


def solution(mesh):
    small = mesh.shape["dp"] == 8 and mesh.shape["mp"] == 4
    return jax.shard_map(
        local_fused if small else local,
        mesh=mesh,
        in_specs=(
            P("dp", None, None),
            P("dp", None),
            P(None, "mp"),
            P(None, "mp"),
            P(None, "mp"),
            P("mp", None),
            P(None, "mp"),
            P("mp", None),
            P(),
            P(),
            P(),
            P("dp", None),
            P(),
            P("dp", None, None),
        ),
        out_specs=(
            P("dp", None, None),
            P("dp", None, None),
            P("dp", None, None),
            P(None, "mp"),
            P(None, "mp"),
            P(None, "mp"),
            P("mp", None),
            P(None, "mp"),
            P("mp", None),
            P(),
            P(),
            P(),
            P("dp", None),
            P(),
        ),
        check_vma=False,
    )
```
